32 devices in a mesh: row: 8 (over y, x, core), col: 4 (over z).
Axes of the slice: x: 2, y: 2, z: 4, core: 2. Of those that a mesh axis runs over, the one named last changes fastest.
Arguments:
- x_blocks: bfloat16 [64, 8, 256, 256], P('row', 'col'), may hold values from -0.75 to 0.75, as said below
- x_cols: int32 [64, 8], P('row', 'col'), may hold values from -1 to 63, as said below
- out_cols: int32 [64, 16], P('row', 'col'), may hold values from 0 to 63, as said below
- branch_flag: int32 [64], P('row'), may hold values from 0 to 1
Outputs:
- purified: bfloat16 [64, 16, 256, 256], P('row', 'col')
- trace: float32 [1], replicated
The draws below stay inside these ranges and needn't reach their ends.
Inputs may be any that keep to these rules, and one draw needn't show every extreme that they name: `x_cols`: slot c * 2 + s of block row i holds -1 or a block column in c * 16 to (c + 1) * 16 - 1; the filled columns of one block row are distinct. The pattern is symmetric: block row i names column j exactly when block row j names column i. The rows of one device hold at most 13 filled slots together, and the rows of some device hold exactly 13. `x_blocks`: the stored block of position (j, i) is the transpose of the stored block of position (i, j); stored diagonal blocks are symmetric. `out_cols`: slot c * 4 + o of block row i holds a block column in c * 16 to (c + 1) * 16 - 1, distinct within one block row; column i is always among the slots of block row i. `branch_flag`: entry i is 0 where block row i takes X times X, 1 where it takes 2 X minus X times X.
All inputs are finite; a program needn't handle non-finite values.
Results may differ from the reference program's by a relative error of at most 0.001.
Values may be sent and summed in bfloat16 or wider, within the bound.
No kernel may reach another device: no remote copies, remote signals or barrier semaphores. Data moves between devices by JAX's collectives and lax.ppermute only.
A program may use at most 192 MiB of HBM per device.

```python
import jax
import jax.numpy as jnp
from jax import lax

BLOCK = 256
ROW_BLOCKS = 8
SLOTS = 2
OUT_SLOTS = 4
BLOCKS = 64
COL_BLOCKS = 16
PACKED = 13


def device_perms(key, devs, length):
    return jax.vmap(lambda sub: jax.random.permutation(sub, length))(jax.random.split(key, devs))


def fill_pattern(key):
    n_col = BLOCKS // COL_BLOCKS
    n_row = BLOCKS // ROW_BLOCKS
    ratio = n_row // n_col
    key = jax.random.fold_in(key, 11)
    keys = jax.random.split(key, 6)
    heavy_cap = (PACKED + 1) // 2
    light_cap = PACKED // 2
    devices = jnp.arange(n_row, dtype=jnp.int32)
    dev_first = devices[:, None]
    dev_second = devices[None, :]
    square_caps = jnp.where((dev_first + dev_second) % 2 == 0, heavy_cap, light_cap).astype(jnp.int32)
    low_counts = (square_caps + 1) // 2
    raw_counts = jax.random.randint(keys[0], (n_row, n_row), low_counts, square_caps + 1)
    counts = jnp.where(dev_first <= dev_second, raw_counts, raw_counts.T)
    forced_row = jax.random.randint(keys[1], (), 0, n_row)
    forced_col = jax.random.randint(keys[2], (), 0, n_col)
    forced_hit = (dev_first == forced_row) & (dev_second // ratio == forced_col) | (dev_second == forced_row) & (dev_first // ratio == forced_col)
    counts = jnp.where(forced_hit, square_caps, counts)
    local = jnp.arange(ROW_BLOCKS, dtype=jnp.int32)
    squares = n_row * n_row
    column_perm = device_perms(keys[3], squares, ROW_BLOCKS).reshape(n_row, n_row, ROW_BLOCKS)
    keep_rank = device_perms(keys[4], squares, ROW_BLOCKS).reshape(n_row, n_row, ROW_BLOCKS)
    keep = keep_rank < counts[:, :, None]
    loose = ((column_perm[..., None] == local) & keep[..., None]).astype(jnp.int32)
    match_perm = device_perms(keys[5], n_row, ROW_BLOCKS)
    diag_counts = jnp.diagonal(counts)
    paired_limit = 2 * (diag_counts // 2)
    partner_spot = jnp.where(local[None, :] < paired_limit[:, None], jnp.bitwise_xor(local, 1)[None, :], local[None, :])
    active = (local[None, :] < diag_counts[:, None]).astype(jnp.int32)
    row_of = match_perm
    col_of = jnp.take_along_axis(match_perm, partner_spot, axis=1)
    row_hot = (row_of[..., None] == local).astype(jnp.int32) * active[..., None]
    col_hot = (col_of[..., None] == local).astype(jnp.int32)
    sym = jnp.sum(row_hot[:, :, :, None] * col_hot[:, :, None, :], axis=1)
    mirrored = jnp.swapaxes(jnp.swapaxes(loose, 0, 1), 2, 3)
    diag_part = jnp.broadcast_to(sym[:, None], (n_row, n_row, ROW_BLOCKS, ROW_BLOCKS))
    upper = (dev_first < dev_second)[..., None, None]
    lower = (dev_first > dev_second)[..., None, None]
    adj = jnp.where(upper, loose, jnp.where(lower, mirrored, diag_part))
    full = adj.transpose(0, 2, 1, 3).reshape(BLOCKS, BLOCKS)
    grouped = full.reshape(BLOCKS, n_col, COL_BLOCKS)
    rank = jnp.cumsum(grouped, axis=2) - 1
    totals = jnp.sum(grouped, axis=2)
    group_spots = jnp.arange(COL_BLOCKS, dtype=jnp.int32)
    group_base = (jnp.arange(n_col, dtype=jnp.int32) * COL_BLOCKS)[None, :]
    slot_list = []
    for slot in range(SLOTS):
        chosen = (grouped > 0) & (rank == slot)
        where_col = jnp.sum(jnp.where(chosen, group_spots[None, None, :], 0), axis=2)
        slot_list.append(jnp.where(totals > slot, group_base + where_col, -1))
    columns = jnp.stack(slot_list, axis=2)
    return columns.reshape(BLOCKS, n_col * SLOTS).astype(jnp.int32)


def draw_x_cols(key, part):
    return fill_pattern(key)


def draw_x_blocks(key, part):
    columns = fill_pattern(key)
    width = columns.shape[1]
    live = columns >= 0
    safe = jnp.where(live, columns, 0)
    rows_there = columns[safe]
    own_rows = jnp.arange(BLOCKS, dtype=jnp.int32)[:, None, None]
    back = jnp.sum(jnp.where(rows_there == own_rows, jnp.arange(width, dtype=jnp.int32)[None, None, :], 0), axis=2)
    flat_self = jnp.arange(BLOCKS, dtype=jnp.int32)[:, None] * width + jnp.arange(width, dtype=jnp.int32)[None, :]
    mirror = jnp.where(live, safe * width + back, flat_self).reshape(-1)
    key_vals = jax.random.fold_in(key, 31)
    shape = (BLOCKS * width, BLOCK, BLOCK)
    raw = jax.random.truncated_normal(key_vals, -4.0, 4.0, shape, jnp.float32) * 0.125
    values = (raw + jnp.swapaxes(raw[mirror], 1, 2)) * 0.7071067811865476
    return values.reshape(BLOCKS, width, BLOCK, BLOCK).astype(jnp.bfloat16)


def draw_out_cols(key, part):
    n_col = BLOCKS // COL_BLOCKS
    columns = fill_pattern(key)
    every = jnp.arange(BLOCKS)
    present = jnp.sum((columns[:, :, None] == every[None, None, :]).astype(jnp.int32), axis=1)
    present = jnp.minimum(present, 1)
    second = jnp.dot(present, present)
    eye = (every[:, None] == every[None, :]).astype(jnp.int32)
    reach = jnp.minimum(second + present + eye, 1).reshape(BLOCKS, n_col, COL_BLOCKS)
    diag = eye.reshape(BLOCKS, n_col, COL_BLOCKS)
    key_rank = jax.random.fold_in(key, 23)
    ranks = jax.vmap(lambda k: jax.random.permutation(k, COL_BLOCKS))(jax.random.split(key_rank, BLOCKS * n_col))
    ranks = ranks.reshape(BLOCKS, n_col, COL_BLOCKS)
    scores = diag * 4 * (COL_BLOCKS + 1) + reach * (COL_BLOCKS + 1) + ranks
    best = jax.lax.top_k(scores, OUT_SLOTS)[1]
    best = best + (jnp.arange(n_col) * COL_BLOCKS)[None, :, None]
    return best.reshape(BLOCKS, n_col * OUT_SLOTS).astype(jnp.int32)


def touch_ends(values, own_key, low, high):
    place = [jax.random.randint(jax.random.fold_in(own_key, axis), (), 0, length) for axis, length in enumerate(values.shape)]
    widest = values.shape.index(max(values.shape))
    next_to = place[:widest] + [(place[widest] + 1) % values.shape[widest]] + place[widest + 1:]
    return values.at[tuple(place)].set(low).at[tuple(next_to)].set(high)


def setup_inputs(seed: int = 0) -> dict:
    splits = jax.random.split(jax.random.key(seed), 5)
    x_blocks = draw_x_blocks(jax.random.fold_in(splits[4], 71), 0)
    x_cols = draw_x_cols(jax.random.fold_in(splits[4], 71), 0)
    out_cols = draw_out_cols(jax.random.fold_in(splits[4], 71), 0)
    branch_flag = touch_ends(jax.random.randint(splits[3], (BLOCKS,), 0, 2), jax.random.fold_in(splits[3], 1), 0, 1).astype(jnp.int32)
    return {"x_blocks": x_blocks, "x_cols": x_cols, "out_cols": out_cols, "branch_flag": branch_flag}


def reference(x_blocks, x_cols, out_cols, branch_flag):
    n_col = x_cols.shape[1] // SLOTS
    filled = x_cols >= 0
    cleared = jnp.where(filled[:, :, None, None], x_blocks, jnp.zeros_like(x_blocks))

    def one_row(index):
        flag_on = branch_flag[index] == 1
        cols = x_cols[index]
        live = cols >= 0
        source = jnp.where(live, cols, 0).astype(jnp.int32)
        lhs = cleared[index].astype(jnp.float32)
        fetched_all = cleared[source]
        fetched_cols_all = jnp.where(live[:, None], x_cols[source], -1)
        targets = out_cols[index]

        def by_device(device):
            start = (device * SLOTS).astype(jnp.int32)
            ostart = (device * OUT_SLOTS).astype(jnp.int32)
            fetched = lax.dynamic_slice_in_dim(fetched_all, start, SLOTS, 1).astype(jnp.float32)
            fetched_cols = lax.dynamic_slice_in_dim(fetched_cols_all, start, SLOTS, 1)
            chosen = lax.dynamic_slice_in_dim(targets, ostart, OUT_SLOTS, 0)
            products = jnp.einsum("exy,esyz->esxz", lhs, fetched, precision=lax.Precision.HIGHEST)
            match = (fetched_cols[None, :, :] == chosen[:, None, None]).astype(jnp.float32)
            square = jnp.einsum("oes,esxz->oxz", match, products, precision=lax.Precision.HIGHEST)
            own_cols = lax.dynamic_slice_in_dim(cols, start, SLOTS, 0)
            own_match = (own_cols[None, :] == chosen[:, None]).astype(jnp.float32)
            own_blocks = lax.dynamic_slice_in_dim(cleared[index], start, SLOTS, 0).astype(jnp.float32)
            own = jnp.einsum("os,sxz->oxz", own_match, own_blocks, precision=lax.Precision.HIGHEST)
            return square, own

        square, own = lax.map(by_device, jnp.arange(n_col, dtype=jnp.int32))
        square = square.reshape(n_col * OUT_SLOTS, BLOCK, BLOCK)
        own = own.reshape(n_col * OUT_SLOTS, BLOCK, BLOCK)
        result = jnp.where(flag_on, 2.0 * own - square, square)
        diag_here = (targets == index).astype(jnp.float32)
        part = jnp.sum(diag_here * jnp.trace(result, axis1=1, axis2=2))
        return result.astype(jnp.bfloat16), part

    purified, parts = lax.map(one_row, jnp.arange(BLOCKS, dtype=jnp.int32))
    trace = jnp.sum(parts).reshape(1)
    return purified, trace
```

```python
import functools

import jax
import jax.numpy as jnp
from jax import lax
from jax.experimental import pallas as pl
from jax.experimental.pallas import tpu as pltpu
from jax.sharding import PartitionSpec as P

PACKED = 13


def multiply_kernel(
    n_pieces, spans, kept, count_ref, left_ref, right_ref, own_ref, flag_ref, *refs
):
    pieces = refs[:n_pieces]
    out_ref = refs[n_pieces]
    left, right, total, done, in_sem, out_sem = refs[n_pieces + 1 :]
    copies = []
    for index, (piece, span) in enumerate(zip(pieces, spans)):
        side, first, size = span
        target = left if side == "left" else right
        copies.append(
            pltpu.make_async_copy(piece, target.at[pl.ds(first, size)], in_sem.at[index])
        )
    for copy in copies:
        copy.start()
    for copy in copies:
        copy.wait()
    outputs = out_ref.shape[0]
    depth = done.shape[0]

    def write(output, slot):
        return pltpu.make_async_copy(done.at[slot], out_ref.at[output], out_sem.at[slot])

    def one_output(output, carry):
        slot = lax.rem(output, depth)

        @pl.when(output >= depth)
        def _():
            write(output - depth, slot).wait()

        n_terms = count_ref[output]
        flag = flag_ref[output // kept]
        own = own_ref[output]
        total[...] = jnp.zeros_like(total)

        def one_term(term, carry):
            total[...] += jnp.dot(
                left[left_ref[output, term]],
                right[right_ref[output, term]],
                preferred_element_type=jnp.float32,
            )
            return carry

        lax.fori_loop(0, n_terms, one_term, 0)

        @pl.when(flag == 0)
        def _():
            done[slot] = total[...].astype(done.dtype)

        @pl.when(jnp.logical_and(flag != 0, own < 0))
        def _():
            done[slot] = (-total[...]).astype(done.dtype)

        @pl.when(jnp.logical_and(flag != 0, own >= 0))
        def _():
            mine = left[jnp.maximum(own, 0)].astype(jnp.float32)
            done[slot] = (2.0 * mine - total[...]).astype(done.dtype)

        write(output, slot).start()
        return carry

    lax.fori_loop(0, outputs, one_output, 0)
    for output in range(outputs - depth, outputs):
        write(output, output % depth).wait()


def multiply(left_pieces, right_pieces, tables, kept):
    counts, left_index, right_index, own_index, flags = tables
    outputs = counts.shape[0]
    block = left_pieces[0][1].shape[-1]
    dtype = left_pieces[0][1].dtype
    pieces = [("left", first, p) for first, p in left_pieces]
    pieces += [("right", first, p) for first, p in right_pieces]
    spans = tuple((side, first, p.shape[0]) for side, first, p in pieces)
    n_left = max(first + size for side, first, size in spans if side == "left")
    n_right = max(first + size for side, first, size in spans if side == "right")
    depth = min(4, outputs)
    smem = pl.BlockSpec(memory_space=pltpu.SMEM)
    hbm = pl.BlockSpec(memory_space=pl.ANY)
    vmem_bytes = (n_left + n_right + depth + 2) * block * block * 2 + (8 << 20)
    return pl.pallas_call(
        functools.partial(multiply_kernel, len(pieces), spans, kept),
        out_shape=jax.ShapeDtypeStruct((outputs, block, block), dtype),
        in_specs=[smem] * 5 + [hbm] * len(pieces),
        out_specs=hbm,
        scratch_shapes=[
            pltpu.VMEM((n_left, block, block), dtype),
            pltpu.VMEM((n_right, block, block), dtype),
            pltpu.VMEM((block, block), jnp.float32),
            pltpu.VMEM((depth, block, block), dtype),
            pltpu.SemaphoreType.DMA((len(pieces),)),
            pltpu.SemaphoreType.DMA((depth,)),
        ],
        compiler_params=pltpu.CompilerParams(vmem_limit_bytes=vmem_bytes),
    )(counts, left_index, right_index, own_index, flags, *[p for _, _, p in pieces])


def exchange(array, mask):
    size = lax.axis_size("row")
    return lax.ppermute(array, "row", [(i, i ^ mask) for i in range(size)])


def gather_rows(packed):
    size = lax.axis_size("row")
    half = (PACKED + 1) // 2
    whole = {0: packed}
    halves = {}
    masks = []
    mask = 2
    while mask < size:
        masks.append(mask)
        mask *= 2
    for mask in masks:
        whole[mask] = exchange(packed, mask)

    def part(delta, side):
        if delta in whole:
            return whole[delta][:half] if side == 0 else whole[delta][half:]
        return halves[delta, side]

    for delta in range(2, size, 2):
        bits = [mask for mask in masks if delta & mask]
        if len(bits) > 1:
            halves[delta, 0] = exchange(part(delta ^ bits[-1], 0), bits[-1])
            halves[delta, 1] = exchange(part(delta ^ bits[0], 1), bits[0])
    pieces = []
    for delta, array in whole.items():
        pieces.append((delta * PACKED, array))
        pieces.append(((delta ^ 1) * PACKED, exchange(array, 1)))
    for (delta, side), array in halves.items():
        first = side * half
        pieces.append((delta * PACKED + first, array))
        pieces.append(((delta ^ 1) * PACKED + first, exchange(array, 1)))
    return pieces


def running_count(fill):
    count = fill.shape[-1]
    before = jnp.arange(count)[:, None] < jnp.arange(count)[None, :]
    return jnp.sum(jnp.where(before, fill[..., :, None], 0), axis=-2)


def local_trace(x_blocks, x_cols, branch_flag, first_row):
    rows, slots, block, _ = x_blocks.shape
    own_row = first_row + jnp.arange(rows, dtype=jnp.int32)
    flag = branch_flag.astype(jnp.float32)[:, None]
    norm_weight = jnp.where(x_cols >= 0, 1.0 - 2.0 * flag, 0.0)
    diag_weight = jnp.where(x_cols == own_row[:, None], 2.0 * flag, 0.0)
    values = x_blocks.astype(jnp.float32)
    eye = jnp.eye(block, dtype=jnp.float32)
    weight = norm_weight[:, :, None, None] * values + diag_weight[:, :, None, None] * eye
    return jnp.sum(weight * values)


def per_device(x_blocks, x_cols, out_cols, branch_flag):
    rows, slots = x_cols.shape
    kept = out_cols.shape[1]
    block = x_blocks.shape[-1]
    count = rows * slots
    n_row = lax.axis_size("row")
    n_col = lax.axis_size("col")
    row = lax.axis_index("row")
    col = lax.axis_index("col")

    flat_cols = x_cols.reshape(count)
    fill = (flat_cols >= 0).astype(jnp.int32)
    place = jnp.where(fill > 0, running_count(fill), -1)
    slots_of = jnp.arange(PACKED, dtype=jnp.int32)
    source = jnp.sum(
        jnp.where(
            place[None, :] == slots_of[:, None], jnp.arange(count, dtype=jnp.int32)[None, :], 0
        ),
        axis=1,
    )
    packed = x_blocks.reshape(count, block, block)[source]

    left_all = lax.all_gather(packed, "col", axis=0, tiled=True)
    right_pieces = gather_rows(packed)

    part = local_trace(x_blocks, x_cols, branch_flag, row * rows)
    facts = jnp.concatenate([flat_cols.astype(jnp.float32), part.reshape(1)])
    facts = lax.all_gather(facts, ("row", "col"), axis=0).reshape(n_row, n_col, count + 1)
    trace = jnp.sum(facts[:, :, count])
    all_cols = facts[:, :, :count].astype(jnp.int32)
    all_fill = (all_cols >= 0).astype(jnp.int32)
    all_place = running_count(all_fill)

    own_cols = lax.dynamic_index_in_dim(all_cols, row, 0, keepdims=False)
    own_place = lax.dynamic_index_in_dim(all_place, row, 0, keepdims=False)
    own_place = own_place + PACKED * jnp.arange(n_col, dtype=jnp.int32)[:, None]
    width = n_col * slots
    left_cols = own_cols.reshape(n_col, rows, slots).transpose(1, 0, 2).reshape(rows, width)
    left_place = own_place.reshape(n_col, rows, slots).transpose(1, 0, 2).reshape(rows, width)
    right_cols = lax.dynamic_index_in_dim(all_cols, col, 1, keepdims=False)
    right_place = lax.dynamic_index_in_dim(all_place, col, 1, keepdims=False)
    delta = jnp.bitwise_xor(jnp.arange(n_row, dtype=jnp.int32), row)
    right_place = (right_place + PACKED * delta[:, None]).reshape(n_row * rows, slots)
    right_cols = right_cols.reshape(n_row * rows, slots)

    hot = left_cols[:, :, None] == jnp.arange(n_row * rows, dtype=jnp.int32)
    met_cols = jnp.sum(jnp.where(hot[..., None], right_cols + 1, 0), axis=2) - 1
    met_place = jnp.sum(jnp.where(hot[..., None], right_place, 0), axis=2)
    match = met_cols[:, None, :, :] == out_cols[:, :, None, None]
    right_at = jnp.sum(jnp.where(match, met_place[:, None], 0), axis=3)
    live = jnp.any(match, axis=3)
    term = jnp.where(live, running_count(live.astype(jnp.int32)), -1)
    pick = term[:, :, None, :] == jnp.arange(width, dtype=jnp.int32)[:, None]
    right_index = jnp.sum(jnp.where(pick, right_at[:, :, None, :], 0), axis=3)
    left_index = jnp.sum(jnp.where(pick, left_place[:, None, None, :], 0), axis=3)
    counts = jnp.sum(live.astype(jnp.int32), axis=2)
    own_match = left_cols[:, None, :] == out_cols[:, :, None]
    own_index = jnp.sum(jnp.where(own_match, left_place[:, None, :] + 1, 0), axis=2) - 1

    outputs = rows * kept
    tables = (
        counts.reshape(outputs),
        left_index.reshape(outputs, width),
        right_index.reshape(outputs, width),
        own_index.reshape(outputs),
        branch_flag,
    )
    purified = multiply([(0, left_all)], right_pieces, tables, kept)
    return purified.reshape(rows, kept, block, block), trace.reshape(1)


def solution(mesh):
    in_specs = (P("row", "col", None, None), P("row", "col"), P("row", "col"), P("row"))
    out_specs = (P("row", "col", None, None), P())
    return jax.shard_map(
        per_device, mesh=mesh, in_specs=in_specs, out_specs=out_specs, check_vma=False
    )
```

```python
import functools

import jax
import jax.numpy as jnp
from jax import lax
from jax.experimental import pallas as pl
from jax.experimental.pallas import tpu as pltpu
from jax.sharding import PartitionSpec as P

PACKED = 13
SPLIT = (PACKED + 1) // 2
STRIDE = 1 << (PACKED - 1).bit_length()
NOTE_ROWS = 16


def pack_kernel(first, limit, cols_ref, x_ref, note_ref, out_ref, sems):
    count, block, _ = x_ref.shape
    slots = cols_ref.shape[1]
    note = pltpu.make_async_copy(
        note_ref, out_ref.at[pl.ds((limit - first) * block, NOTE_ROWS)], sems.at[count]
    )
    note.start()
    copies = []
    place = jnp.int32(0)
    for index in range(count):
        filled = cols_ref[index // slots, index % slots] >= 0
        wanted = filled & (place >= first) & (place < limit)
        target = pl.multiple_of(jnp.where(wanted, place - first, 0) * block, block)
        copy = pltpu.make_async_copy(
            x_ref.at[index], out_ref.at[pl.ds(target, block)], sems.at[index]
        )
        pl.when(wanted)(copy.start)
        copies.append((wanted, copy))
        place = place + filled.astype(jnp.int32)
    for wanted, copy in copies:
        pl.when(wanted)(copy.wait)
    note.wait()


def pack(x_blocks, x_cols, note, first, limit):
    rows, slots, block, _ = x_blocks.shape
    count = rows * slots
    hbm = pl.BlockSpec(memory_space=pl.ANY)
    return pl.pallas_call(
        functools.partial(pack_kernel, first, limit),
        out_shape=jax.ShapeDtypeStruct(
            ((limit - first) * block + NOTE_ROWS, block), x_blocks.dtype
        ),
        in_specs=[pl.BlockSpec(memory_space=pltpu.SMEM), hbm, hbm],
        out_specs=hbm,
        scratch_shapes=[pltpu.SemaphoreType.DMA((count + 1,))],
    )(x_cols, x_blocks.reshape(count, block, block), note)


def multiply_kernel(loads, kept, counts, lefts, rights, owns, flags, place_ref, *refs):
    n_refs = 1 + max(load[0] for load in loads)
    sources = refs[:n_refs]
    out_ref = refs[n_refs]
    pool, more, done, in_sem, out_sem = refs[n_refs + 1 :]
    block = out_ref.shape[-1]
    copies = []
    for number, (which, index, entry, entries, first, size, ends) in enumerate(loads):
        rows = pl.ds(0, size * block)
        source = sources[which]
        target = pool.at[pl.ds(entry, entries), pl.ds(first * block, size * block)]
        if entries == 1:
            target = pool.at[entry, pl.ds(first * block, size * block)]
            source = source.at[rows] if index is None else source.at[index, rows]
        else:
            source = source.at[:, rows]
        copy = pltpu.make_async_copy(source, target, in_sem.at[number])
        copies.append((None if ends is None else place_ref[0] == ends, copy))
    for here, copy in copies:
        copy.start() if here is None else pl.when(here)(copy.start)
    zero_entry = pool.shape[0] - 1
    pool[zero_entry, pl.ds(0, block)] = jnp.zeros((block, block), pool.dtype)
    for here, copy in copies:
        copy.wait() if here is None else pl.when(here)(copy.wait)

    outputs = out_ref.shape[0]

    def blocks(index):
        entry = lax.shift_right_logical(index, STRIDE.bit_length() - 1)
        first = pl.multiple_of(jnp.bitwise_and(index, STRIDE - 1) * block, block)
        return pool[entry, pl.ds(first, block)]

    def product(output, term):
        return jnp.dot(
            blocks(lefts[output, term]),
            blocks(rights[output, term]),
            preferred_element_type=jnp.float32,
        )

    def write(output, slot):
        return pltpu.make_async_copy(done.at[slot], out_ref.at[output], out_sem.at[slot])

    def one_row(row, carry):
        flag = flags[row].astype(jnp.float32)
        for local in range(kept):
            output = row * kept + local

            @pl.when(counts[output] > 2)
            def _():
                more[local] = product(output, 2)

                def one_term(term, carry):
                    more[local] += product(output, term)
                    return carry

                lax.fori_loop(3, counts[output], one_term, 0)

            @pl.when(counts[output] <= 2)
            def _():
                more[local] = jnp.zeros_like(more[local])

        half = lax.rem(row, 2)

        @pl.when(row >= 2)
        def _():
            for local in range(kept):
                write((row - 2) * kept + local, half * kept + local).wait()

        for local in range(kept):
            output = row * kept + local
            square = product(output, 0) + product(output, 1) + more[local]
            own = blocks(owns[output]).astype(jnp.float32)
            result = (2.0 * flag) * own + (1.0 - 2.0 * flag) * square
            done[half * kept + local] = result.astype(done.dtype)
        for local in range(kept):
            write(row * kept + local, half * kept + local).start()
        return carry

    n_rows = outputs // kept
    lax.fori_loop(0, n_rows, one_row, 0)
    for row in range(max(n_rows - 2, 0), n_rows):
        for local in range(kept):
            write(row * kept + local, (row % 2) * kept + local).wait()


def multiply(arrays, loads, n_entries, tables, place, kept, block, dtype):
    outputs = tables[0].shape[0]
    smem = pl.BlockSpec(memory_space=pltpu.SMEM)
    hbm = pl.BlockSpec(memory_space=pl.ANY)
    pool_bytes = n_entries * PACKED * block * block * 2
    return pl.pallas_call(
        functools.partial(multiply_kernel, loads, kept),
        out_shape=jax.ShapeDtypeStruct((outputs, block, block), dtype),
        in_specs=[smem] * 6 + [hbm] * len(arrays),
        out_specs=hbm,
        scratch_shapes=[
            pltpu.VMEM((n_entries, PACKED * block, block), dtype),
            pltpu.VMEM((kept, block, block), jnp.float32),
            pltpu.VMEM((2 * kept, block, block), dtype),
            pltpu.SemaphoreType.DMA((len(loads),)),
            pltpu.SemaphoreType.DMA((2 * kept,)),
        ],
        compiler_params=pltpu.CompilerParams(vmem_limit_bytes=pool_bytes + (12 << 20)),
    )(*tables, place, *arrays)


def shift(array, pairs):
    return lax.ppermute(array, "col", pairs)


def gather_line(part):
    first = shift(part, [(0, 1), (1, 0), (2, 3), (3, 2)])
    middle = shift(part, [(1, 2), (2, 1)])
    end_two = shift(middle, [(1, 0), (2, 3)])
    middle_two = shift(first, [(1, 2), (2, 1)])
    end_three = shift(middle_two, [(1, 0), (2, 3)])
    return first, (end_two, end_three), (middle, middle_two)


def running_count(fill):
    count = fill.shape[-1]
    before = jnp.arange(count)[:, None] < jnp.arange(count)[None, :]
    return jnp.sum(jnp.where(before, fill[..., :, None], 0), axis=-2)


def places(cols):
    flat = (cols >= 0).astype(jnp.int32).reshape(cols.shape[:-2] + (-1,))
    return running_count(flat).reshape(cols.shape)


def local_trace(x_blocks, x_cols, branch_flag, first_row):
    rows, slots, block, _ = x_blocks.shape
    own_row = first_row + jnp.arange(rows, dtype=jnp.int32)
    flag = branch_flag.astype(jnp.float32)[:, None]
    norm_weight = jnp.where(x_cols >= 0, 1.0 - 2.0 * flag, 0.0)
    diag_weight = jnp.where(x_cols == own_row[:, None], 2.0 * flag, 0.0)
    values = x_blocks.astype(jnp.float32)
    eye = jnp.eye(block, dtype=jnp.float32)
    weight = norm_weight[:, :, None, None] * values + diag_weight[:, :, None, None] * eye
    return jnp.sum(weight * values)


def thirds(value):
    high = lax.reduce_precision(value, 8, 7)
    middle = lax.reduce_precision(value - high, 8, 7)
    return jnp.stack([high, middle, value - high - middle]).astype(jnp.bfloat16)


def per_device(x_blocks, x_cols, out_cols, branch_flag):
    rows, slots = x_cols.shape
    kept = out_cols.shape[1]
    block = x_blocks.shape[-1]
    dtype = x_blocks.dtype
    n_row = lax.axis_size("row")
    n_col = lax.axis_size("col")
    row = lax.axis_index("row")
    col = lax.axis_index("col")
    n_blocks = n_row * rows

    def note(values):
        pad = [(0, NOTE_ROWS - values.shape[0]), (0, block - values.shape[1])]
        return jnp.pad(values.astype(dtype), pad)

    part_a = pack(x_blocks, x_cols, note(x_cols), 0, SPLIT)
    trace_part = local_trace(x_blocks, x_cols, branch_flag, row * rows)
    part_b = pack(x_blocks, x_cols, note(thirds(trace_part)[None, :]), SPLIT, PACKED)
    parts = (part_a, part_b)

    def facts(array):
        return array[..., SPLIT * block : SPLIT * block + rows, :slots].astype(jnp.int32)

    plane = [lax.all_gather(part, "row", axis=0) for part in parts]
    spans = ((0, SPLIT), (SPLIT, PACKED - SPLIT))
    arrays = list(plane)
    loads = [(which, None, 0, n_row) + spans[which] + (None,) for which in range(2)]
    if n_col == 4:
        line = [gather_line(part) for part in parts]
        n_left = 3
        for which, (first, far, near) in enumerate(line):
            for entry, ends, array in (
                (0, None, first),
                (1, 1, far[0]),
                (1, 0, near[0]),
                (2, 1, far[1]),
                (2, 0, near[1]),
            ):
                loads.append((len(arrays), None, n_row + entry, 1) + spans[which] + (ends,))
                arrays.append(array)
        at_end = (col == 0) | (col == n_col - 1)
        first, far, near = line[0]
        left_cols = [facts(first)]
        left_cols += [jnp.where(at_end, facts(far[i]), facts(near[i])) for i in range(2)]
        left_cols = jnp.stack(left_cols + [x_cols])
        left_entries = jnp.stack([n_row + jnp.int32(i) for i in range(n_left)] + [row])
    else:
        line = [lax.all_gather(part, "col", axis=0) for part in parts]
        n_left = n_col
        for which in range(2):
            loads.append((len(arrays), None, n_row, n_col) + spans[which] + (None,))
            arrays.append(line[which])
        at_end = col == 0
        left_cols = facts(line[0])
        left_entries = n_row + jnp.arange(n_col, dtype=jnp.int32)
    n_entries = n_row + n_left + 1
    nothing = (n_entries - 1) * STRIDE

    trace = jnp.sum(plane[1][:, (PACKED - SPLIT) * block, :3].astype(jnp.float32))
    mask = 1
    while mask < n_col:
        trace = trace + shift(trace, [(i, i ^ mask) for i in range(n_col)])
        mask *= 2

    every = jnp.arange(n_blocks, dtype=jnp.int32)
    left_at = places(left_cols) + STRIDE * left_entries[:, None, None]
    hit = left_cols[..., None] == every
    left_of = jnp.sum(jnp.where(hit, left_at[..., None] + 1, 0), axis=(0, 2))
    right_cols = facts(plane[0])
    right_at = places(right_cols) + STRIDE * jnp.arange(n_row, dtype=jnp.int32)[:, None, None]
    right_cols = right_cols.reshape(n_blocks, slots)
    right_at = right_at.reshape(n_blocks, slots)
    targets = out_cols.reshape(rows * kept)
    hit = right_cols[None] == targets[:, None, None]
    right_of = jnp.sum(jnp.where(hit, right_at + 1, 0), axis=2)
    left_of = jnp.repeat(left_of, kept, axis=0)
    live = (left_of > 0) & (right_of > 0)
    width = n_col * slots
    term = jnp.where(live, running_count(live.astype(jnp.int32)), -1)
    pick = term[:, None, :] == jnp.arange(width, dtype=jnp.int32)[:, None]
    lefts = jnp.sum(jnp.where(pick, left_of[:, None, :] - 1 - nothing, 0), axis=2) + nothing
    rights = jnp.sum(jnp.where(pick, right_of[:, None, :] - 1 - nothing, 0), axis=2) + nothing
    counts = jnp.sum(live.astype(jnp.int32), axis=1)
    own_at = places(x_cols) + STRIDE * row
    hit = x_cols[:, None, :] == out_cols[:, :, None]
    owns = jnp.sum(jnp.where(hit, own_at[:, None, :] - nothing, 0), axis=2) + nothing

    tables = (counts, lefts, rights, owns.reshape(rows * kept), branch_flag)
    place = at_end.astype(jnp.int32).reshape(1)
    purified = multiply(arrays, tuple(loads), n_entries, tables, place, kept, block, dtype)
    return purified.reshape(rows, kept, block, block), trace.reshape(1)


def solution(mesh):
    in_specs = (P("row", "col", None, None), P("row", "col"), P("row", "col"), P("row"))
    out_specs = (P("row", "col", None, None), P())
    return jax.shard_map(
        per_device, mesh=mesh, in_specs=in_specs, out_specs=out_specs, check_vma=False
    )
```

```python
import functools

import jax
import jax.numpy as jnp
from jax import lax
from jax.experimental import pallas as pl
from jax.experimental.pallas import tpu as pltpu
from jax.sharding import PartitionSpec as P

PACKED = 13
SPLIT = (PACKED + 1) // 2
STRIDE = 1 << (PACKED - 1).bit_length()
NOTE_ROWS = 16


def pack_kernel(cols_ref, flag_ref, first_ref, x_ref, part_a, part_b, full, note, norm, sems):
    count, block, _ = x_ref.shape
    slots = cols_ref.shape[0]
    rows = count // slots
    sends = []
    place = jnp.int32(0)
    for index in range(count):
        filled = cols_ref[index % slots, index // slots] >= 0
        targets = (
            (full, filled, place),
            (part_a, filled & (place < SPLIT), place),
            (part_b, filled & (place >= SPLIT), place - SPLIT),
        )
        for which, (out, wanted, target) in enumerate(targets):
            target = pl.multiple_of(jnp.where(wanted, target, 0) * block, block)
            copy = pltpu.make_async_copy(
                x_ref.at[index], out.at[pl.ds(target, block)], sems.at[which, index]
            )
            pl.when(wanted)(copy.start)
            sends.append((wanted, copy))
        place = place + filled.astype(jnp.int32)

    norm[...] = jnp.zeros_like(norm)
    eye_rows = lax.broadcasted_iota(jnp.int32, (block, block), 0)
    eye = eye_rows == lax.broadcasted_iota(jnp.int32, (block, block), 1)
    for index in range(count):
        row = index // slots
        col = cols_ref[index % slots, row]
        flag = flag_ref[row]

        @pl.when(col >= 0)
        def _():
            values = x_ref[index].astype(jnp.float32)
            weight = (1 - 2 * flag).astype(jnp.float32)
            norm[...] += weight * jnp.sum(values * values, axis=0, keepdims=True)

        @pl.when((col == first_ref[0] + row) & (flag != 0))
        def _():
            values = x_ref[index].astype(jnp.float32)
            norm[...] += 2.0 * jnp.sum(jnp.where(eye, values, 0.0), axis=0, keepdims=True)

    trace = jnp.full(note.shape, jnp.sum(norm[...]), jnp.float32)
    high = trace.astype(note.dtype).astype(jnp.float32)
    middle = (trace - high).astype(note.dtype).astype(jnp.float32)
    low = trace - high - middle
    down = lax.broadcasted_iota(jnp.int32, note.shape, 0)
    across = lax.broadcasted_iota(jnp.int32, note.shape, 1)
    facts = jnp.where(across == 0, high, jnp.where(across == 1, middle, low))
    facts = jnp.where((down == rows) & (across < 3), facts, 0.0)
    for index in range(count):
        here = (down == index // slots) & (across == index % slots)
        facts = jnp.where(here, cols_ref[index % slots, index // slots].astype(jnp.float32), facts)
    note[...] = facts.astype(note.dtype)
    for which, out in enumerate((full, part_a, part_b)):
        target = out.at[pl.ds(out.shape[0] - NOTE_ROWS, NOTE_ROWS)]
        copy = pltpu.make_async_copy(note, target, sems.at[which, count])
        copy.start()
        sends.append((None, copy))
    for wanted, copy in sends:
        copy.wait() if wanted is None else pl.when(wanted)(copy.wait)


def pack(x_blocks, x_cols, branch_flag, first_row):
    rows, slots, block, _ = x_blocks.shape
    count = rows * slots
    smem = pl.BlockSpec(memory_space=pltpu.SMEM)
    hbm = pl.BlockSpec(memory_space=pltpu.HBM)
    return pl.pallas_call(
        pack_kernel,
        out_shape=[
            jax.ShapeDtypeStruct((size * block + NOTE_ROWS, block), x_blocks.dtype)
            for size in (SPLIT, PACKED - SPLIT, PACKED)
        ],
        in_specs=[smem, smem, smem, pl.BlockSpec(memory_space=pltpu.VMEM)],
        out_specs=[hbm] * 3,
        scratch_shapes=[
            pltpu.VMEM((NOTE_ROWS, block), x_blocks.dtype),
            pltpu.VMEM((1, block), jnp.float32),
            pltpu.SemaphoreType.DMA((3, count + 1)),
        ],
        compiler_params=pltpu.CompilerParams(vmem_limit_bytes=(4 * count * block * block) + (8 << 20)),
    )(x_cols.T, branch_flag, first_row.reshape(1), x_blocks.reshape(count, block, block))


def multiply_kernel(loads, kept, counts, lefts, rights, owns, flags, place_ref, *refs):
    n_refs = 1 + max(load[0] for load in loads)
    sources = refs[:n_refs]
    out_ref = refs[n_refs]
    pool, more, done, in_sem, out_sem = refs[n_refs + 1 :]
    block = out_ref.shape[-1]
    copies = []
    for number, (which, index, entry, entries, first, size, ends) in enumerate(loads):
        rows = pl.ds(0, size * block)
        source = sources[which]
        target = pool.at[pl.ds(entry, entries), pl.ds(first * block, size * block)]
        if entries == 1:
            target = pool.at[entry, pl.ds(first * block, size * block)]
            source = source.at[rows] if index is None else source.at[index, rows]
        else:
            source = source.at[:, rows]
        copy = pltpu.make_async_copy(source, target, in_sem.at[number])
        copies.append((None if ends is None else place_ref[0] == ends, copy))
    for here, copy in copies:
        copy.start() if here is None else pl.when(here)(copy.start)
    zero_entry = pool.shape[0] - 1
    pool[zero_entry, pl.ds(0, block)] = jnp.zeros((block, block), pool.dtype)
    for here, copy in copies:
        copy.wait() if here is None else pl.when(here)(copy.wait)

    outputs = out_ref.shape[0]

    def blocks(index):
        entry = lax.shift_right_logical(index, STRIDE.bit_length() - 1)
        first = pl.multiple_of(jnp.bitwise_and(index, STRIDE - 1) * block, block)
        return pool[entry, pl.ds(first, block)]

    def product(output, term):
        return jnp.dot(
            blocks(lefts[output, term]),
            blocks(rights[output, term]),
            preferred_element_type=jnp.float32,
        )

    def write(output, slot):
        return pltpu.make_async_copy(done.at[slot], out_ref.at[output], out_sem.at[slot])

    def one_row(row, carry):
        flag = flags[row].astype(jnp.float32)
        for local in range(kept):
            output = row * kept + local

            @pl.when(counts[output] > 2)
            def _():
                more[local] = product(output, 2)

                def one_term(term, carry):
                    more[local] += product(output, term)
                    return carry

                lax.fori_loop(3, counts[output], one_term, 0)

            @pl.when(counts[output] <= 2)
            def _():
                more[local] = jnp.zeros_like(more[local])

        half = lax.rem(row, 2)

        @pl.when(row >= 2)
        def _():
            for local in range(kept):
                write((row - 2) * kept + local, half * kept + local).wait()

        for local in range(kept):
            output = row * kept + local
            square = product(output, 0) + product(output, 1) + more[local]
            own = blocks(owns[output]).astype(jnp.float32)
            result = (2.0 * flag) * own + (1.0 - 2.0 * flag) * square
            done[half * kept + local] = result.astype(done.dtype)
        for local in range(kept):
            write(row * kept + local, half * kept + local).start()
        return carry

    n_rows = outputs // kept
    lax.fori_loop(0, n_rows, one_row, 0)
    for row in range(max(n_rows - 2, 0), n_rows):
        for local in range(kept):
            write(row * kept + local, (row % 2) * kept + local).wait()


def multiply(arrays, loads, n_entries, tables, place, kept, block, dtype):
    outputs = tables[0].shape[0]
    smem = pl.BlockSpec(memory_space=pltpu.SMEM)
    hbm = pl.BlockSpec(memory_space=pltpu.HBM)
    pool_bytes = n_entries * PACKED * block * block * 2
    return pl.pallas_call(
        functools.partial(multiply_kernel, loads, kept),
        out_shape=jax.ShapeDtypeStruct((outputs, block, block), dtype),
        in_specs=[smem] * 6 + [hbm] * len(arrays),
        out_specs=hbm,
        scratch_shapes=[
            pltpu.VMEM((n_entries, PACKED * block, block), dtype),
            pltpu.VMEM((kept, block, block), jnp.float32),
            pltpu.VMEM((2 * kept, block, block), dtype),
            pltpu.SemaphoreType.DMA((len(loads),)),
            pltpu.SemaphoreType.DMA((2 * kept,)),
        ],
        compiler_params=pltpu.CompilerParams(vmem_limit_bytes=pool_bytes + (12 << 20)),
    )(*tables, place, *arrays)


def shift(array, pairs):
    return lax.ppermute(array, "col", pairs)


def gather_line(part):
    first = shift(part, [(0, 1), (1, 0), (2, 3), (3, 2)])
    middle = shift(part, [(1, 2), (2, 1)])
    end_two = shift(middle, [(1, 0), (2, 3)])
    middle_two = shift(first, [(1, 2), (2, 1)])
    end_three = shift(middle_two, [(1, 0), (2, 3)])
    return first, (end_two, end_three), (middle, middle_two)


def running_count(fill):
    count = fill.shape[-1]
    before = jnp.arange(count)[:, None] < jnp.arange(count)[None, :]
    return jnp.sum(jnp.where(before, fill[..., :, None], 0), axis=-2)


def places(cols):
    flat = (cols >= 0).astype(jnp.int32).reshape(cols.shape[:-2] + (-1,))
    return running_count(flat).reshape(cols.shape)


def per_device(x_blocks, x_cols, out_cols, branch_flag):
    rows, slots = x_cols.shape
    kept = out_cols.shape[1]
    block = x_blocks.shape[-1]
    dtype = x_blocks.dtype
    n_row = lax.axis_size("row")
    n_col = lax.axis_size("col")
    row = lax.axis_index("row")
    col = lax.axis_index("col")
    n_blocks = n_row * rows

    part_a, part_b, full = pack(x_blocks, x_cols, branch_flag, row * rows)
    parts = (part_a, part_b)

    def facts(array):
        first = array.shape[-2] - NOTE_ROWS
        return array[..., first : first + rows, :slots].astype(jnp.int32)

    plane = lax.all_gather(full, "row", axis=0)
    spans = ((0, SPLIT), (SPLIT, PACKED - SPLIT))
    arrays = [plane]
    loads = [(0, None, 0, n_row, 0, PACKED, None)]
    if n_col == 4:
        line = [gather_line(part) for part in parts]
        n_left = 3
        for which, (first, far, near) in enumerate(line):
            for entry, ends, array in (
                (0, None, first),
                (1, 1, far[0]),
                (1, 0, near[0]),
                (2, 1, far[1]),
                (2, 0, near[1]),
            ):
                loads.append((len(arrays), None, n_row + entry, 1) + spans[which] + (ends,))
                arrays.append(array)
        at_end = (col == 0) | (col == n_col - 1)
        first, far, near = line[0]
        left_cols = [facts(first)]
        left_cols += [jnp.where(at_end, facts(far[i]), facts(near[i])) for i in range(2)]
        left_cols = jnp.stack(left_cols + [x_cols])
        left_entries = jnp.stack([n_row + jnp.int32(i) for i in range(n_left)] + [row])
    else:
        line = [lax.all_gather(part, "col", axis=0) for part in parts]
        n_left = n_col
        for which in range(2):
            loads.append((len(arrays), None, n_row, n_col) + spans[which] + (None,))
            arrays.append(line[which])
        at_end = col == 0
        left_cols = facts(line[0])
        left_entries = n_row + jnp.arange(n_col, dtype=jnp.int32)
    n_entries = n_row + n_left + 1
    nothing = (n_entries - 1) * STRIDE

    own_trace = jnp.sum(plane[:, PACKED * block + rows, :3].astype(jnp.float32))
    heights = jnp.arange(n_col, dtype=jnp.int32)
    traces = jnp.where(heights == col, own_trace, 0.0)
    for step in range(1, n_col):
        other = shift(own_trace, [(i, i ^ step) for i in range(n_col)])
        traces = jnp.where(heights == jnp.bitwise_xor(col, step), other, traces)
    trace = jnp.sum(traces)

    every = jnp.arange(n_blocks, dtype=jnp.int32)
    left_at = places(left_cols) + STRIDE * left_entries[:, None, None]
    hit = left_cols[..., None] == every
    left_of = jnp.sum(jnp.where(hit, left_at[..., None] + 1, 0), axis=(0, 2))
    right_cols = facts(plane)
    right_at = places(right_cols) + STRIDE * jnp.arange(n_row, dtype=jnp.int32)[:, None, None]
    right_cols = right_cols.reshape(n_blocks, slots)
    right_at = right_at.reshape(n_blocks, slots)
    targets = out_cols.reshape(rows * kept)
    hit = right_cols[None] == targets[:, None, None]
    right_of = jnp.sum(jnp.where(hit, right_at + 1, 0), axis=2)
    left_of = jnp.repeat(left_of, kept, axis=0)
    live = (left_of > 0) & (right_of > 0)
    width = n_col * slots
    term = jnp.where(live, running_count(live.astype(jnp.int32)), -1)
    pick = term[:, None, :] == jnp.arange(width, dtype=jnp.int32)[:, None]
    lefts = jnp.sum(jnp.where(pick, left_of[:, None, :] - 1 - nothing, 0), axis=2) + nothing
    rights = jnp.sum(jnp.where(pick, right_of[:, None, :] - 1 - nothing, 0), axis=2) + nothing
    counts = jnp.sum(live.astype(jnp.int32), axis=1)
    own_at = places(x_cols) + STRIDE * row
    hit = x_cols[:, None, :] == out_cols[:, :, None]
    owns = jnp.sum(jnp.where(hit, own_at[:, None, :] - nothing, 0), axis=2) + nothing

    tables = (counts, lefts, rights, owns.reshape(rows * kept), branch_flag)
    place = at_end.astype(jnp.int32).reshape(1)
    purified = multiply(arrays, tuple(loads), n_entries, tables, place, kept, block, dtype)
    return purified.reshape(rows, kept, block, block), trace.reshape(1)


def solution(mesh):
    in_specs = (P("row", "col", None, None), P("row", "col"), P("row", "col"), P("row"))
    out_specs = (P("row", "col", None, None), P())
    return jax.shard_map(
        per_device, mesh=mesh, in_specs=in_specs, out_specs=out_specs, check_vma=False
    )
```

```python
import functools

import jax
import jax.numpy as jnp
from jax import lax
from jax.experimental import pallas as pl
from jax.experimental.pallas import tpu as pltpu
from jax.sharding import PartitionSpec as P

PACKED = 13
SPLIT = (PACKED + 1) // 2
STRIDE = 1 << (PACKED - 1).bit_length()
NOTE_ROWS = 16


def pack_kernel(cols_ref, flag_ref, first_ref, x_ref, part_a, part_b, full, note, norm, sems):
    count, block, _ = x_ref.shape
    slots = cols_ref.shape[0]
    rows = count // slots
    sends = []
    place = jnp.int32(0)
    for index in range(count):
        filled = cols_ref[index % slots, index // slots] >= 0
        targets = (
            (full, filled, place),
            (part_a, filled & (place < SPLIT), place),
            (part_b, filled & (place >= SPLIT), place - SPLIT),
        )
        for which, (out, wanted, target) in enumerate(targets):
            target = pl.multiple_of(jnp.where(wanted, target, 0) * block, block)
            copy = pltpu.make_async_copy(
                x_ref.at[index], out.at[pl.ds(target, block)], sems.at[which, index]
            )
            pl.when(wanted)(copy.start)
            sends.append((wanted, copy))
        place = place + filled.astype(jnp.int32)

    norm[...] = jnp.zeros_like(norm)
    eye_rows = lax.broadcasted_iota(jnp.int32, (block, block), 0)
    eye = eye_rows == lax.broadcasted_iota(jnp.int32, (block, block), 1)
    for index in range(count):
        row = index // slots
        col = cols_ref[index % slots, row]
        flag = flag_ref[row]

        @pl.when(col >= 0)
        def _():
            values = x_ref[index].astype(jnp.float32)
            weight = (1 - 2 * flag).astype(jnp.float32)
            norm[...] += weight * jnp.sum(values * values, axis=0, keepdims=True)

        @pl.when((col == first_ref[0] + row) & (flag != 0))
        def _():
            values = x_ref[index].astype(jnp.float32)
            norm[...] += 2.0 * jnp.sum(jnp.where(eye, values, 0.0), axis=0, keepdims=True)

    trace = jnp.full(note.shape, jnp.sum(norm[...]), jnp.float32)
    high = trace.astype(note.dtype).astype(jnp.float32)
    middle = (trace - high).astype(note.dtype).astype(jnp.float32)
    low = trace - high - middle
    down = lax.broadcasted_iota(jnp.int32, note.shape, 0)
    across = lax.broadcasted_iota(jnp.int32, note.shape, 1)
    facts = jnp.where(across == 0, high, jnp.where(across == 1, middle, low))
    facts = jnp.where((down == rows) & (across < 3), facts, 0.0)
    for index in range(count):
        here = (down == index // slots) & (across == index % slots)
        facts = jnp.where(here, cols_ref[index % slots, index // slots].astype(jnp.float32), facts)
    note[...] = facts.astype(note.dtype)
    for which, out in enumerate((full, part_a, part_b)):
        target = out.at[pl.ds(out.shape[0] - NOTE_ROWS, NOTE_ROWS)]
        copy = pltpu.make_async_copy(note, target, sems.at[which, count])
        copy.start()
        sends.append((None, copy))
    for wanted, copy in sends:
        copy.wait() if wanted is None else pl.when(wanted)(copy.wait)


def pack(x_blocks, x_cols, branch_flag, first_row):
    rows, slots, block, _ = x_blocks.shape
    count = rows * slots
    smem = pl.BlockSpec(memory_space=pltpu.SMEM)
    hbm = pl.BlockSpec(memory_space=pltpu.HBM)
    return pl.pallas_call(
        pack_kernel,
        out_shape=[
            jax.ShapeDtypeStruct((size * block + NOTE_ROWS, block), x_blocks.dtype)
            for size in (SPLIT, PACKED - SPLIT, PACKED)
        ],
        in_specs=[smem, smem, smem, pl.BlockSpec(memory_space=pltpu.VMEM)],
        out_specs=[hbm] * 3,
        scratch_shapes=[
            pltpu.VMEM((NOTE_ROWS, block), x_blocks.dtype),
            pltpu.VMEM((1, block), jnp.float32),
            pltpu.SemaphoreType.DMA((3, count + 1)),
        ],
        compiler_params=pltpu.CompilerParams(vmem_limit_bytes=(4 * count * block * block) + (8 << 20)),
    )(x_cols.T, branch_flag, first_row.reshape(1), x_blocks.reshape(count, block, block))


def multiply_kernel(
    loads, kept, first_turned, control, outs, counts, lefts, rights, owns, flags, *refs
):
    n_arrays = 1 + max(load[0] for load in loads)
    plane = refs[0]
    arrays = refs[:n_arrays]
    out_ref, pool, ring, total, done, in_sem, ring_sem, out_sem = refs[-8:]
    block = out_ref.shape[-1]
    n_out = control[0]
    n_terms = control[1]
    depth = ring.shape[0]
    width = done.shape[0]

    copies = []
    for number, (which, at, entry, first, size, wanted) in enumerate(loads):
        source = arrays[which]
        if at is not None:
            source = source.at[control[at] if at >= 0 else -at - 1]
        copy = pltpu.make_async_copy(
            source.at[pl.ds(0, size * block)],
            pool.at[entry, pl.ds(first * block, size * block)],
            in_sem.at[number],
        )
        copies.append(((control[wanted] != 0) & (n_out > 0), copy))
    for here, copy in copies:
        pl.when(here)(copy.start)

    def decode(index):
        entry = lax.shift_right_logical(index, STRIDE.bit_length() - 1)
        return entry, pl.multiple_of(jnp.bitwise_and(index, STRIDE - 1) * block, block)

    def fetch(term):
        entry, first = decode(rights[term])
        slot = lax.rem(term, depth)
        return pltpu.make_async_copy(
            plane.at[entry, pl.ds(first, block)], ring.at[slot], ring_sem.at[slot]
        )

    def begin(term, carry):
        fetch(term).start()
        return carry

    lax.fori_loop(0, jnp.minimum(depth, n_terms), begin, 0)
    for here, copy in copies:
        pl.when(here)(copy.wait)

    def write(number):
        slot = lax.rem(number, width)
        return pltpu.make_async_copy(done.at[slot], out_ref.at[outs[number]], out_sem.at[slot])

    def one_output(number, term):
        output = outs[number]
        total[...] = jnp.zeros_like(total)

        def one_term(term, carry):
            entry, first = decode(lefts[term])
            fetch(term).wait()
            left = pool[entry, pl.ds(first, block)]
            right = ring[lax.rem(term, depth)]

            def add(dims):
                total[...] += lax.dot_general(
                    left, right, (dims, ((), ())), preferred_element_type=jnp.float32
                )

            if first_turned is None:
                add(((1,), (0,)))
            else:
                pl.when(entry < first_turned)(lambda: add(((1,), (0,))))
                pl.when(entry >= first_turned)(lambda: add(((0,), (0,))))

            @pl.when(term + depth < n_terms)
            def _():
                fetch(term + depth).start()

            return carry

        last = term + counts[number]
        lax.fori_loop(term, last, one_term, 0)

        @pl.when(number >= width)
        def _():
            write(number - width).wait()

        flag = flags[output // kept].astype(jnp.float32)
        own = owns[output]
        _, first = decode(jnp.maximum(own, 0))
        weight = jnp.where(own >= 0, 2.0 * flag, 0.0)
        slot = lax.rem(number, width)

        @pl.when(weight == 0.0)
        def _():
            done[slot] = ((1.0 - 2.0 * flag) * total[...]).astype(done.dtype)

        @pl.when(weight != 0.0)
        def _():
            mine = pool[0, pl.ds(first, block)].astype(jnp.float32)
            done[slot] = (2.0 * mine - total[...]).astype(done.dtype)

        write(number).start()
        return last

    lax.fori_loop(0, n_out, one_output, jnp.int32(0))
    for back in range(width):
        @pl.when(n_out > back)
        def _():
            write(n_out - 1 - back).wait()


def multiply(arrays, loads, n_entries, first_turned, control, tables, shape, before=None):
    rows, kept, block, dtype = shape
    outputs = rows * kept
    smem = pl.BlockSpec(memory_space=pltpu.SMEM)
    hbm = pl.BlockSpec(memory_space=pltpu.HBM)
    depth = 32
    vmem = (n_entries * PACKED + depth + 4 + 2) * block * block * 2 + (8 << 20)
    operands = [control, *tables, *arrays]
    in_specs = [smem] * (1 + len(tables)) + [hbm] * len(arrays)
    aliases = {}
    if before is not None:
        operands += [before[1], before[0]]
        in_specs += [smem, hbm]
        aliases = {len(operands) - 1: 0}
    return pl.pallas_call(
        functools.partial(multiply_kernel, loads, kept, first_turned),
        out_shape=jax.ShapeDtypeStruct((outputs, block, block), dtype),
        in_specs=in_specs,
        out_specs=hbm,
        scratch_shapes=[
            pltpu.VMEM((n_entries, PACKED * block, block), dtype),
            pltpu.VMEM((depth, block, block), dtype),
            pltpu.VMEM((block, block), jnp.float32),
            pltpu.VMEM((4, block, block), dtype),
            pltpu.SemaphoreType.DMA((len(loads),)),
            pltpu.SemaphoreType.DMA((depth,)),
            pltpu.SemaphoreType.DMA((4,)),
        ],
        input_output_aliases=aliases,
        compiler_params=pltpu.CompilerParams(vmem_limit_bytes=vmem),
    )(*operands)


FOUR = range(4)
PLAN = {
    "first": [((q, 3), (q, 2)) for q in FOUR] + [((q, 1), (q, 0)) for q in (0, 1, 2)],
    "middle": [((q, 2), (q, 1)) for q in (0, 2, 3)],
    "middle_two": [((q, 2), (q, 1)) for q in FOUR],
    "end_two": [((q, 1), (q, 0)) for q in (0, 2, 3)],
    "end_three": [((1, 1), (1, 0))],
    "end_last": [((3, 1), (3, 0))],
    "turn_one": [((2, 0), (1, 0))],
    "turn_two": [((3, 0), (2, 0))],
    "turn_three": [((1, 0), (3, 0))],
}
TURNED = {(0, 0): 3, (1, 0): 2, (2, 0): 3, (3, 0): 1, (1, 1): 2}


def both_ends(moves):
    mirrored = [tuple((3 - q, 3 - c) for q, c in move) for move in moves]
    return list(moves) + mirrored


def send(array, name):
    n_col = lax.axis_size("col")
    pairs = []
    for (q, c), (q_to, c_to) in both_ends(PLAN[name]):
        for core in range(2):
            pairs.append(((2 * q + core) * n_col + c, (2 * q_to + core) * n_col + c_to))
    return lax.ppermute(array, ("row", "col"), sorted(pairs))


def gather_line(part):
    got = {"first": send(part, "first"), "middle": send(part, "middle")}
    got["end_two"] = send(got["middle"], "end_two")
    got["middle_two"] = send(got["first"], "middle_two")
    got["end_three"] = send(got["middle_two"], "end_three")
    got["end_last"] = send(got["middle_two"], "end_last")
    turned = send(got["first"], "turn_one") + send(got["end_two"], "turn_two")
    turned = turned + send(got["end_three"], "turn_three")
    got["turned"] = turned
    size = lax.axis_size("row")
    got["other"] = lax.ppermute(turned, "row", [(i, i ^ 1) for i in range(size)])
    return got


def arrives(name):
    table = [[0] * 4 for _ in range(4)]
    for _, (q, c) in both_ends(PLAN[name]):
        table[q][c] = 1
    return table


def look_up(table, pair, col):
    answer = jnp.int32(0)
    for q, line in enumerate(table):
        for c, value in enumerate(line):
            if value:
                answer = jnp.where((pair == q) & (col == c), value, answer)
    return answer


def running_count(fill):
    count = fill.shape[-1]
    before = jnp.arange(count)[:, None] < jnp.arange(count)[None, :]
    return jnp.sum(jnp.where(before, fill[..., :, None], 0), axis=-2)


def places(cols):
    flat = (cols >= 0).astype(jnp.int32).reshape(cols.shape[:-2] + (-1,))
    return running_count(flat).reshape(cols.shape)


def lists(left_of, right_of, chosen, width):
    kept = right_of.shape[0] // left_of.shape[0]
    outputs = right_of.shape[0]
    left_of = jnp.repeat(left_of, kept, axis=0)
    live = (left_of > 0) & (right_of > 0) & chosen[:, None]
    counts = jnp.sum(live.astype(jnp.int32), axis=1)
    term = jnp.where(live, running_count(live.astype(jnp.int32)), -1)
    across = jnp.arange(width, dtype=jnp.int32)
    pick = term[:, None, :] == across[:, None]
    lefts = jnp.sum(jnp.where(pick, left_of[:, None, :] - 1, 0), axis=2)
    rights = jnp.sum(jnp.where(pick, right_of[:, None, :] - 1, 0), axis=2)
    flat = jnp.where(across < counts[:, None], running_count(counts)[:, None] + across, -1)
    pick = flat[None] == jnp.arange(PACKED * width, dtype=jnp.int32)[:, None, None]
    lefts = jnp.sum(jnp.where(pick, lefts, 0), axis=(1, 2))
    rights = jnp.sum(jnp.where(pick, rights, 0), axis=(1, 2))
    every = jnp.arange(outputs, dtype=jnp.int32)
    number = jnp.where(chosen, running_count(chosen.astype(jnp.int32)), -1)
    pick = number[None, :] == every[:, None]
    outs = jnp.sum(jnp.where(pick, every, 0), axis=1)
    ordered = jnp.sum(jnp.where(pick, counts, 0), axis=1)
    sizes = jnp.stack([jnp.sum(chosen.astype(jnp.int32)), jnp.sum(counts)])
    return sizes, (outs, ordered, lefts, rights)


def per_device(x_blocks, x_cols, out_cols, branch_flag):
    rows, slots = x_cols.shape
    kept = out_cols.shape[1]
    block = x_blocks.shape[-1]
    dtype = x_blocks.dtype
    n_row = lax.axis_size("row")
    n_col = lax.axis_size("col")
    row = lax.axis_index("row")
    col = lax.axis_index("col")
    n_blocks = n_row * rows
    width = n_col * slots
    shape = (rows, kept, block, dtype)

    part_a, part_b, full = pack(x_blocks, x_cols, branch_flag, row * rows)

    def facts(array):
        first = array.shape[-2] - NOTE_ROWS
        return array[..., first : first + rows, :slots].astype(jnp.int32)

    plane = lax.all_gather(full, "row", axis=0)
    plane_cols = facts(plane)

    own_trace = jnp.sum(plane[:, PACKED * block + rows, :3].astype(jnp.float32))
    heights = jnp.arange(n_col, dtype=jnp.int32)
    traces = jnp.where(heights == col, own_trace, 0.0)
    for step in range(1, n_col):
        other = lax.ppermute(own_trace, "col", [(i, i ^ step) for i in range(n_col)])
        traces = jnp.where(heights == jnp.bitwise_xor(col, step), other, traces)
    trace = jnp.sum(traces).reshape(1)

    targets = out_cols.reshape(rows * kept)
    right_at = places(plane_cols) + STRIDE * jnp.arange(n_row, dtype=jnp.int32)[:, None, None]
    hit = plane_cols.reshape(n_blocks, slots)[None] == targets[:, None, None]
    right_of = jnp.sum(jnp.where(hit, right_at.reshape(n_blocks, slots) + 1, 0), axis=2)
    hit = x_cols[:, None, :] == out_cols[:, :, None]
    owns = jnp.sum(jnp.where(hit, places(x_cols)[:, None, :] + 1, 0), axis=2) - 1
    owns = owns.reshape(rows * kept)

    every = jnp.arange(n_blocks, dtype=jnp.int32)

    def straight(cols, entries, wanted):
        at = places(cols) + STRIDE * entries[:, None, None]
        hit = (cols[..., None] == every) & (wanted[:, None, None, None] != 0)
        return jnp.sum(jnp.where(hit, at[..., None] + 1, 0), axis=(0, 2))

    def turned(cols, entries, devices, wanted):
        at = places(cols) + STRIDE * entries[:, None, None]
        own = row * rows + jnp.arange(rows, dtype=jnp.int32)
        hit = (cols[..., None] == own) & (wanted != 0)
        found = jnp.sum(jnp.where(hit, at[..., None] + 1, 0), axis=2)
        names = devices[:, None] * rows + jnp.arange(rows, dtype=jnp.int32)
        found = jnp.where(names[:, :, None, None] == every, found[..., None], 0)
        return jnp.sum(found, axis=(0, 1))

    spans = ((0, SPLIT), (SPLIT, PACKED - SPLIT))
    everything = jnp.ones((rows * kept,), bool)
    one = jnp.ones((), jnp.int32)
    if not (n_col == 4 and n_row == 8):
        line = lax.all_gather(full, "col", axis=0)
        entries = 1 + jnp.arange(n_col, dtype=jnp.int32)
        left_of = straight(facts(line), entries, jnp.ones((n_col,), jnp.int32))
        sizes, tables = lists(left_of, right_of, everything, width)
        loads = [(2, None, 0, 0, PACKED, 2)]
        loads += [(1, -1 - c, 1 + c, 0, PACKED, 2) for c in range(n_col)]
        control = jnp.concatenate([sizes, one[None]])
        tables = tables + (owns, branch_flag)
        purified = multiply(
            [plane, line, full], tuple(loads), 1 + n_col, None, control, tables, shape
        )
        return purified.reshape(rows, kept, block, block), trace

    pair = row // 2
    core = row % 2
    line = [gather_line(part) for part in (part_a, part_b)]
    has = {name: look_up(arrives(name), pair, col) for name in PLAN}
    turn_table = [[0] * n_col for _ in FOUR]
    for (q, c), t in TURNED.items():
        turn_table[q][c] = t + 1
        turn_table[3 - q][3 - c] = 4 - t
    turn = look_up(turn_table, pair, col) - 1
    diagonal = (pair == col).astype(jnp.int32)
    moved = ((turn >= 0) & (diagonal == 0)).astype(jnp.int32)
    turn_devices = 2 * jnp.maximum(turn, 0) + jnp.stack([core, 1 - core])
    turn_entries = jnp.array([4, 5], jnp.int32)

    note = {name: facts(array) for name, array in line[0].items()}
    early_cols = jnp.stack(
        [
            x_cols,
            note["first"],
            jnp.where(has["middle"] != 0, note["middle"], note["end_two"]),
            note["middle_two"],
        ]
    )
    early_has = jnp.stack(
        [one, has["first"], has["middle"] + has["end_two"], has["middle_two"]]
    )
    early = straight(early_cols, jnp.arange(4, dtype=jnp.int32), early_has)
    plane_turned = jnp.stack(
        [lax.dynamic_index_in_dim(plane_cols, turn_devices[i], 0, keepdims=False) for i in range(2)]
    )
    early = early + turned(plane_turned, turn_entries, turn_devices, diagonal)

    arrays = [plane, full]
    loads = [(1, None, 0, 0, PACKED, 4)]
    loads += [(0, 2 + i, 4 + i, 0, PACKED, 5) for i in range(2)]
    names = ["first", "middle", "end_two", "middle_two"]
    late_names = ["end_three", "end_last", "turned", "other"]
    entry_of = {"first": 1, "middle": 2, "end_two": 2, "middle_two": 3}
    entry_of.update({"end_three": 3, "end_last": 3, "turned": 4, "other": 5})
    flag_of = {name: 6 + place for place, name in enumerate(names + late_names)}

    def add(some):
        for name in some:
            for which in range(2):
                loads.append((len(arrays), None, entry_of[name]) + spans[which] + (flag_of[name],))
                arrays.append(line[which][name])

    add(names)
    has["turned"] = has["other"] = moved
    flags = [turn_devices, one[None], diagonal[None]]
    flags += [has[name][None] for name in names + late_names]

    sizes, tables = lists(early, right_of, everything, width)
    control = jnp.concatenate([sizes] + flags)
    tables = tables + (owns, branch_flag)
    purified = multiply(list(arrays), tuple(loads), 6, 4, control, tables, shape)

    late_cols = jnp.where(has["end_three"] != 0, note["end_three"], note["end_last"])[None]
    late_has = (has["end_three"] + has["end_last"])[None]
    late = straight(late_cols, jnp.array([3], jnp.int32), late_has)
    late_turned = jnp.stack([note["turned"], note["other"]])
    late = late + turned(late_turned, turn_entries, turn_devices, moved)
    meets = (jnp.repeat(late, kept, axis=0) > 0) & (right_of > 0)
    chosen = jnp.any(meets, axis=1)
    add(late_names)
    sizes, tables = lists(early + late, right_of, chosen, width)
    control = jnp.concatenate([sizes] + flags)
    tables = tables + (owns, branch_flag)
    purified = multiply(
        list(arrays), tuple(loads), 6, 4, control, tables, shape, (purified, trace)
    )
    return purified.reshape(rows, kept, block, block), trace


def solution(mesh):
    in_specs = (P("row", "col", None, None), P("row", "col"), P("row", "col"), P("row"))
    out_specs = (P("row", "col", None, None), P())
    return jax.shard_map(
        per_device, mesh=mesh, in_specs=in_specs, out_specs=out_specs, check_vma=False
    )
```

```python
import functools

import jax
import jax.numpy as jnp
from jax import lax
from jax.experimental import pallas as pl
from jax.experimental.pallas import tpu as pltpu
from jax.sharding import PartitionSpec as P

PACKED = 13
SPLIT = (PACKED + 1) // 2
STRIDE = 1 << (PACKED - 1).bit_length()
NOTE_ROWS = 16


def pack_kernel(cols_ref, flag_ref, first_ref, x_ref, part_a, part_b, full, note, norm, sems):
    count, block, _ = x_ref.shape
    slots = cols_ref.shape[0]
    rows = count // slots
    sends = []
    place = jnp.int32(0)
    for index in range(count):
        filled = cols_ref[index % slots, index // slots] >= 0
        targets = (
            (full, filled, place),
            (part_a, filled & (place < SPLIT), place),
            (part_b, filled & (place >= SPLIT), place - SPLIT),
        )
        for which, (out, wanted, target) in enumerate(targets):
            target = pl.multiple_of(jnp.where(wanted, target, 0) * block, block)
            copy = pltpu.make_async_copy(
                x_ref.at[index], out.at[pl.ds(target, block)], sems.at[which, index]
            )
            pl.when(wanted)(copy.start)
            sends.append((wanted, copy))
        place = place + filled.astype(jnp.int32)

    norm[...] = jnp.zeros_like(norm)
    eye_rows = lax.broadcasted_iota(jnp.int32, (block, block), 0)
    eye = eye_rows == lax.broadcasted_iota(jnp.int32, (block, block), 1)
    for index in range(count):
        row = index // slots
        col = cols_ref[index % slots, row]
        flag = flag_ref[row]

        @pl.when(col >= 0)
        def _():
            values = x_ref[index].astype(jnp.float32)
            weight = (1 - 2 * flag).astype(jnp.float32)
            norm[...] += weight * jnp.sum(values * values, axis=0, keepdims=True)

        @pl.when((col == first_ref[0] + row) & (flag != 0))
        def _():
            values = x_ref[index].astype(jnp.float32)
            norm[...] += 2.0 * jnp.sum(jnp.where(eye, values, 0.0), axis=0, keepdims=True)

    trace = jnp.full(note.shape, jnp.sum(norm[...]), jnp.float32)
    high = trace.astype(note.dtype).astype(jnp.float32)
    middle = (trace - high).astype(note.dtype).astype(jnp.float32)
    low = trace - high - middle
    down = lax.broadcasted_iota(jnp.int32, note.shape, 0)
    across = lax.broadcasted_iota(jnp.int32, note.shape, 1)
    facts = jnp.where(across == 0, high, jnp.where(across == 1, middle, low))
    facts = jnp.where((down == rows) & (across < 3), facts, 0.0)
    for index in range(count):
        here = (down == index // slots) & (across == index % slots)
        facts = jnp.where(here, cols_ref[index % slots, index // slots].astype(jnp.float32), facts)
    note[...] = facts.astype(note.dtype)
    for which, out in enumerate((full, part_a, part_b)):
        target = out.at[pl.ds(out.shape[0] - NOTE_ROWS, NOTE_ROWS)]
        copy = pltpu.make_async_copy(note, target, sems.at[which, count])
        copy.start()
        sends.append((None, copy))
    for wanted, copy in sends:
        copy.wait() if wanted is None else pl.when(wanted)(copy.wait)


def pack(x_blocks, x_cols, branch_flag, first_row):
    rows, slots, block, _ = x_blocks.shape
    count = rows * slots
    smem = pl.BlockSpec(memory_space=pltpu.SMEM)
    hbm = pl.BlockSpec(memory_space=pltpu.HBM)
    return pl.pallas_call(
        pack_kernel,
        out_shape=[
            jax.ShapeDtypeStruct((size * block + NOTE_ROWS, block), x_blocks.dtype)
            for size in (SPLIT, PACKED - SPLIT, PACKED)
        ],
        in_specs=[smem, smem, smem, pl.BlockSpec(memory_space=pltpu.VMEM)],
        out_specs=[hbm] * 3,
        scratch_shapes=[
            pltpu.VMEM((NOTE_ROWS, block), x_blocks.dtype),
            pltpu.VMEM((1, block), jnp.float32),
            pltpu.SemaphoreType.DMA((3, count + 1)),
        ],
        compiler_params=pltpu.CompilerParams(vmem_limit_bytes=(4 * count * block * block) + (8 << 20)),
    )(x_cols.T, branch_flag, first_row.reshape(1), x_blocks.reshape(count, block, block))


BATCH = 4


def multiply_kernel(loads, kept, layout, table, *refs):
    n_arrays = 1 + max(load[0] for load in loads)
    plane = refs[0]
    arrays = refs[:n_arrays]
    out_ref, pool, ring, more, done, in_sem, ring_sem, out_sem = refs[-8:]
    block = out_ref.shape[-1]
    n_out = table[0]
    n_terms = table[1]
    depth = ring.shape[0] - 1
    zero_entry = pool.shape[0] - 1

    copies = []
    for number, (which, at, entry, first, size, wanted) in enumerate(loads):
        source = arrays[which] if at is None else arrays[which].at[at]
        copy = pltpu.make_async_copy(
            source.at[pl.ds(0, size * block)],
            pool.at[entry, pl.ds(first * block, size * block)],
            in_sem.at[number],
        )
        copies.append(((table[wanted] != 0) & (n_out > 0), copy))
    for here, copy in copies:
        pl.when(here)(copy.start)

    def decode(index):
        entry = lax.shift_right_logical(index, STRIDE.bit_length() - 1)
        return entry, pl.multiple_of(jnp.bitwise_and(index, STRIDE - 1) * block, block)

    def fetch(term):
        entry, first = decode(table[layout["rights"] + term])
        slot = lax.rem(term, depth)
        return pltpu.make_async_copy(
            plane.at[entry, pl.ds(first, block)], ring.at[slot], ring_sem.at[slot]
        )

    def begin(term, carry):
        fetch(term).start()
        return carry

    lax.fori_loop(0, jnp.minimum(depth, n_terms), begin, 0)
    pool[zero_entry, pl.ds(0, block)] = jnp.zeros((block, block), pool.dtype)
    ring[depth] = jnp.zeros((block, block), ring.dtype)
    for here, copy in copies:
        pl.when(here)(copy.wait)

    def product(term, live):
        entry, first = decode(
            jnp.where(live, table[layout["lefts"] + term], zero_entry * STRIDE)
        )
        slot = jnp.where(live, lax.rem(term, depth), depth)
        return jnp.dot(
            pool[entry, pl.ds(first, block)], ring[slot], preferred_element_type=jnp.float32
        )

    def write(number, slot):
        output = table[layout["outs"] + number]
        return pltpu.make_async_copy(done.at[slot], out_ref.at[output], out_sem.at[slot])

    def one_batch(batch, term):
        begins, counts = [], []
        last = term
        for local in range(BATCH):
            begins.append(last)
            counts.append(table[layout["counts"] + batch * BATCH + local])
            last = last + counts[local]

        def arrived(number, carry):
            fetch(number).wait()
            return carry

        lax.fori_loop(term, last, arrived, 0)
        half = lax.rem(batch, 2) * BATCH
        for local in range(BATCH):
            @pl.when(batch >= 2)
            def _():
                write((batch - 2) * BATCH + local, half + local).wait()

            @pl.when(counts[local] > 2)
            def _():
                more[local] = product(begins[local] + 2, True)

                def one_term(number, carry):
                    more[local] += product(number, True)
                    return carry

                lax.fori_loop(begins[local] + 3, begins[local] + counts[local], one_term, 0)

            @pl.when(counts[local] <= 2)
            def _():
                more[local] = jnp.zeros_like(more[local])

        for local in range(BATCH):
            output = table[layout["outs"] + batch * BATCH + local]
            square = more[local]
            for place in range(2):
                live = counts[local] > place
                square = square + product(jnp.where(live, begins[local] + place, 0), live)
            flag = table[layout["flags"] + output // kept].astype(jnp.float32)
            own = table[layout["owns"] + output]
            entry, first = decode(jnp.where(own >= 0, own, zero_entry * STRIDE))
            mine = pool[entry, pl.ds(first, block)].astype(jnp.float32)
            result = (2.0 * flag) * mine + (1.0 - 2.0 * flag) * square
            done[half + local] = result.astype(done.dtype)
        for local in range(BATCH):
            @pl.when(batch * BATCH + local < n_out)
            def _():
                write(batch * BATCH + local, half + local).start()

        def refill(number, carry):
            fetch(number + depth).start()
            return carry

        lax.fori_loop(term, jnp.clip(n_terms - depth, term, last), refill, 0)
        return last

    n_batches = (n_out + BATCH - 1) // BATCH
    lax.fori_loop(0, n_batches, one_batch, jnp.int32(0))
    for back in range(2):
        batch = n_batches - 1 - back
        for local in range(BATCH):
            number = jnp.maximum(batch, 0) * BATCH + local

            @pl.when((batch >= 0) & (number < n_out))
            def _():
                write(number, lax.rem(batch, 2) * BATCH + local).wait()


def multiply(arrays, loads, n_entries, layout, table, shape, before=None):
    rows, kept, block, dtype = shape
    outputs = rows * kept
    smem = pl.BlockSpec(memory_space=pltpu.SMEM)
    hbm = pl.BlockSpec(memory_space=pltpu.HBM)
    depth = 48
    vmem = ((n_entries + 1) * PACKED + depth + 5 * BATCH) * block * block * 2 + (8 << 20)
    operands = [table, *arrays]
    in_specs = [smem] + [hbm] * len(arrays)
    aliases = {}
    if before is not None:
        operands += [before[1], before[0]]
        in_specs += [smem, hbm]
        aliases = {len(operands) - 1: 0}
    return pl.pallas_call(
        functools.partial(multiply_kernel, loads, kept, layout),
        out_shape=jax.ShapeDtypeStruct((outputs, block, block), dtype),
        in_specs=in_specs,
        out_specs=hbm,
        scratch_shapes=[
            pltpu.VMEM((n_entries + 1, PACKED * block, block), dtype),
            pltpu.VMEM((depth + 1, block, block), dtype),
            pltpu.VMEM((BATCH, block, block), jnp.float32),
            pltpu.VMEM((2 * BATCH, block, block), dtype),
            pltpu.SemaphoreType.DMA((len(loads),)),
            pltpu.SemaphoreType.DMA((depth,)),
            pltpu.SemaphoreType.DMA((2 * BATCH,)),
        ],
        input_output_aliases=aliases,
        compiler_params=pltpu.CompilerParams(vmem_limit_bytes=vmem),
    )(*operands)


def shift(array, pairs):
    return lax.ppermute(array, "col", pairs)


def gather_line(part):
    first = shift(part, [(0, 1), (1, 0), (2, 3), (3, 2)])
    middle = shift(part, [(1, 2), (2, 1)])
    end_two = shift(middle, [(1, 0), (2, 3)])
    middle_two = shift(first, [(1, 2), (2, 1)])
    end_three = shift(middle_two, [(1, 0), (2, 3)])
    return {
        "first": first,
        "middle": middle,
        "end_two": end_two,
        "middle_two": middle_two,
        "end_three": end_three,
    }


def running_count(fill):
    count = fill.shape[-1]
    before = jnp.arange(count)[:, None] < jnp.arange(count)[None, :]
    return jnp.sum(jnp.where(before, fill[..., :, None], 0), axis=-2)


def places(cols):
    flat = (cols >= 0).astype(jnp.int32).reshape(cols.shape[:-2] + (-1,))
    return running_count(flat).reshape(cols.shape)


def make_table(left_of, right_of, owns, flags, chosen, width, wanted):
    kept = right_of.shape[0] // left_of.shape[0]
    outputs = right_of.shape[0]
    left_of = jnp.repeat(left_of, kept, axis=0)
    live = (left_of > 0) & (right_of > 0) & chosen[:, None]
    counts = jnp.sum(live.astype(jnp.int32), axis=1)
    term = jnp.where(live, running_count(live.astype(jnp.int32)), -1)
    across = jnp.arange(width, dtype=jnp.int32)
    pick = term[:, None, :] == across[:, None]
    lefts = jnp.sum(jnp.where(pick, left_of[:, None, :] - 1, 0), axis=2)
    rights = jnp.sum(jnp.where(pick, right_of[:, None, :] - 1, 0), axis=2)
    flat = jnp.where(across < counts[:, None], running_count(counts)[:, None] + across, -1)
    pick = flat[None] == jnp.arange(PACKED * width, dtype=jnp.int32)[:, None, None]
    lefts = jnp.sum(jnp.where(pick, lefts, 0), axis=(1, 2))
    rights = jnp.sum(jnp.where(pick, rights, 0), axis=(1, 2))
    every = jnp.arange(outputs, dtype=jnp.int32)
    number = jnp.where(chosen, running_count(chosen.astype(jnp.int32)), -1)
    pick = number[None, :] == every[:, None]
    outs = jnp.sum(jnp.where(pick, every, 0), axis=1)
    ordered = jnp.sum(jnp.where(pick, counts, 0), axis=1)
    sizes = jnp.stack([jnp.sum(chosen.astype(jnp.int32)), jnp.sum(counts)])
    spare = jnp.zeros((BATCH,), jnp.int32)
    lists = {
        "sizes": sizes,
        "wanted": wanted,
        "outs": jnp.concatenate([outs, spare]),
        "counts": jnp.concatenate([ordered, spare]),
        "lefts": lefts,
        "rights": rights,
        "owns": owns,
        "flags": flags,
    }
    layout = {}
    first = 0
    for name, values in lists.items():
        layout[name] = first
        first += values.shape[0]
    return jnp.concatenate(list(lists.values())), layout


def per_device(x_blocks, x_cols, out_cols, branch_flag):
    rows, slots = x_cols.shape
    kept = out_cols.shape[1]
    block = x_blocks.shape[-1]
    dtype = x_blocks.dtype
    n_row = lax.axis_size("row")
    n_col = lax.axis_size("col")
    row = lax.axis_index("row")
    col = lax.axis_index("col")
    n_blocks = n_row * rows
    width = n_col * slots
    shape = (rows, kept, block, dtype)

    part_a, part_b, full = pack(x_blocks, x_cols, branch_flag, row * rows)

    def facts(array):
        first = array.shape[-2] - NOTE_ROWS
        return array[..., first : first + rows, :slots].astype(jnp.int32)

    plane = lax.all_gather(full, "row", axis=0)
    plane_cols = facts(plane)

    own_trace = jnp.sum(plane[:, PACKED * block + rows, :3].astype(jnp.float32))
    heights = jnp.arange(n_col, dtype=jnp.int32)
    traces = jnp.where(heights == col, own_trace, 0.0)
    for step in range(1, n_col):
        other = shift(own_trace, [(i, i ^ step) for i in range(n_col)])
        traces = jnp.where(heights == jnp.bitwise_xor(col, step), other, traces)
    trace = jnp.sum(traces).reshape(1)

    targets = out_cols.reshape(rows * kept)
    right_at = places(plane_cols) + STRIDE * jnp.arange(n_row, dtype=jnp.int32)[:, None, None]
    hit = plane_cols.reshape(n_blocks, slots)[None] == targets[:, None, None]
    right_of = jnp.sum(jnp.where(hit, right_at.reshape(n_blocks, slots) + 1, 0), axis=2)
    hit = x_cols[:, None, :] == out_cols[:, :, None]
    owns = jnp.sum(jnp.where(hit, places(x_cols)[:, None, :] + 1, 0), axis=2) - 1
    owns = owns.reshape(rows * kept)

    every = jnp.arange(n_blocks, dtype=jnp.int32)

    def straight(cols, entries, wanted):
        at = places(cols) + STRIDE * entries[:, None, None]
        hit = (cols[..., None] == every) & (wanted[:, None, None, None] != 0)
        return jnp.sum(jnp.where(hit, at[..., None] + 1, 0), axis=(0, 2))

    everything = jnp.ones((rows * kept,), bool)
    one = jnp.ones((1,), jnp.int32)
    if n_col != 4:
        line = lax.all_gather(full, "col", axis=0)
        entries = 1 + jnp.arange(n_col, dtype=jnp.int32)
        left_of = straight(facts(line), entries, jnp.ones((n_col,), jnp.int32))
        table, layout = make_table(
            left_of, right_of, owns, branch_flag, everything, width, one
        )
        loads = [(2, None, 0, 0, PACKED, 2)]
        loads += [(1, c, 1 + c, 0, PACKED, 2) for c in range(n_col)]
        purified = multiply([plane, line, full], tuple(loads), 1 + n_col, layout, table, shape)
        return purified.reshape(rows, kept, block, block), trace

    line = [gather_line(part) for part in (part_a, part_b)]
    note = {name: facts(array) for name, array in line[0].items()}
    at_end = (col == 0) | (col == n_col - 1)
    end = at_end.astype(jnp.int32)
    wanted = jnp.stack([jnp.int32(1), end, 1 - end])
    always, at_ends, inside = 2, 3, 4

    arrays = [plane, full]
    loads = [(1, None, 0, 0, PACKED, always)]

    def add(name, entry, wanted):
        spans = ((0, SPLIT), (SPLIT, PACKED - SPLIT))
        for which in range(2):
            loads.append((len(arrays), None, entry) + spans[which] + (wanted,))
            arrays.append(line[which][name])

    early_cols = [x_cols, note["first"], jnp.where(at_end, note["end_two"], note["middle"])]
    early_cols = jnp.stack(early_cols + [note["middle_two"]])
    early_wanted = jnp.stack([jnp.int32(1)] * 3 + [1 - end])
    early = straight(early_cols, jnp.arange(4, dtype=jnp.int32), early_wanted)
    add("first", 1, always)
    add("middle", 2, inside)
    add("end_two", 2, at_ends)
    add("middle_two", 3, inside)
    table, layout = make_table(early, right_of, owns, branch_flag, everything, width, wanted)
    purified = multiply(list(arrays), tuple(loads), 4, layout, table, shape)

    late = straight(note["end_three"][None], jnp.array([3], jnp.int32), end[None])
    meets = (jnp.repeat(late, kept, axis=0) > 0) & (right_of > 0)
    chosen = jnp.any(meets, axis=1)
    add("end_three", 3, at_ends)
    table, layout = make_table(early + late, right_of, owns, branch_flag, chosen, width, wanted)
    before = (purified, trace)
    purified = multiply(list(arrays), tuple(loads), 4, layout, table, shape, before)
    return purified.reshape(rows, kept, block, block), trace


def solution(mesh):
    in_specs = (P("row", "col", None, None), P("row", "col"), P("row", "col"), P("row"))
    out_specs = (P("row", "col", None, None), P())
    return jax.shard_map(
        per_device, mesh=mesh, in_specs=in_specs, out_specs=out_specs, check_vma=False
    )
```

```python
import functools

import jax
import jax.numpy as jnp
from jax import lax
from jax.experimental import pallas as pl
from jax.experimental.pallas import tpu as pltpu
from jax.sharding import PartitionSpec as P

PACKED = 13
SPLIT = (PACKED + 1) // 2
STRIDE = 1 << (PACKED - 1).bit_length()
NOTE_ROWS = 16


def pack_kernel(
    cols_ref, flag_ref, first_ref, x_ref, part_a, part_b, full, note, norm, zeros, sems
):
    count, block, _ = x_ref.shape
    slots = cols_ref.shape[0]
    rows = count // slots
    sends = []
    place = jnp.int32(0)
    for index in range(count):
        filled = cols_ref[index % slots, index // slots] >= 0
        targets = (
            (full, filled, place),
            (part_a, filled & (place < SPLIT), place),
            (part_b, filled & (place >= SPLIT), place - SPLIT),
        )
        for which, (out, wanted, target) in enumerate(targets):
            target = pl.multiple_of(jnp.where(wanted, target, 0) * block, block)
            copy = pltpu.make_async_copy(
                x_ref.at[index], out.at[pl.ds(target, block)], sems.at[which, index]
            )
            pl.when(wanted)(copy.start)
            sends.append((wanted, copy))
        place = place + filled.astype(jnp.int32)

    blank = pltpu.make_async_copy(zeros, full.at[pl.ds(0, block)], sems.at[0, count + 1])

    @pl.when(place == 0)
    def _():
        zeros[...] = jnp.zeros_like(zeros)
        blank.start()

    sends.append((place == 0, blank))

    norm[...] = jnp.zeros_like(norm)
    eye_rows = lax.broadcasted_iota(jnp.int32, (block, block), 0)
    eye = eye_rows == lax.broadcasted_iota(jnp.int32, (block, block), 1)
    for index in range(count):
        row = index // slots
        col = cols_ref[index % slots, row]
        flag = flag_ref[row]

        @pl.when(col >= 0)
        def _():
            values = x_ref[index].astype(jnp.float32)
            weight = (1 - 2 * flag).astype(jnp.float32)
            norm[...] += weight * jnp.sum(values * values, axis=0, keepdims=True)

        @pl.when((col == first_ref[0] + row) & (flag != 0))
        def _():
            values = x_ref[index].astype(jnp.float32)
            norm[...] += 2.0 * jnp.sum(jnp.where(eye, values, 0.0), axis=0, keepdims=True)

    trace = jnp.full(note.shape, jnp.sum(norm[...]), jnp.float32)
    high = trace.astype(note.dtype).astype(jnp.float32)
    middle = (trace - high).astype(note.dtype).astype(jnp.float32)
    low = trace - high - middle
    down = lax.broadcasted_iota(jnp.int32, note.shape, 0)
    across = lax.broadcasted_iota(jnp.int32, note.shape, 1)
    facts = jnp.where(across == 0, high, jnp.where(across == 1, middle, low))
    facts = jnp.where((down == rows) & (across < 3), facts, 0.0)
    for index in range(count):
        here = (down == index // slots) & (across == index % slots)
        facts = jnp.where(here, cols_ref[index % slots, index // slots].astype(jnp.float32), facts)
    note[...] = facts.astype(note.dtype)
    for which, out in enumerate((full, part_a, part_b)):
        target = out.at[pl.ds(out.shape[0] - NOTE_ROWS, NOTE_ROWS)]
        copy = pltpu.make_async_copy(note, target, sems.at[which, count])
        copy.start()
        sends.append((None, copy))
    for wanted, copy in sends:
        copy.wait() if wanted is None else pl.when(wanted)(copy.wait)


def pack(x_blocks, x_cols, branch_flag, first_row):
    rows, slots, block, _ = x_blocks.shape
    count = rows * slots
    smem = pl.BlockSpec(memory_space=pltpu.SMEM)
    hbm = pl.BlockSpec(memory_space=pltpu.HBM)
    return pl.pallas_call(
        pack_kernel,
        out_shape=[
            jax.ShapeDtypeStruct((size * block + NOTE_ROWS, block), x_blocks.dtype)
            for size in (SPLIT, PACKED - SPLIT, PACKED)
        ],
        in_specs=[smem, smem, smem, pl.BlockSpec(memory_space=pltpu.VMEM)],
        out_specs=[hbm] * 3,
        scratch_shapes=[
            pltpu.VMEM((NOTE_ROWS, block), x_blocks.dtype),
            pltpu.VMEM((1, block), jnp.float32),
            pltpu.VMEM((block, block), x_blocks.dtype),
            pltpu.SemaphoreType.DMA((3, count + 2)),
        ],
        compiler_params=pltpu.CompilerParams(vmem_limit_bytes=(4 * count * block * block) + (8 << 20)),
    )(x_cols.T, branch_flag, first_row.reshape(1), x_blocks.reshape(count, block, block))


BATCH = 4


def multiply_kernel(loads, kept, layout, table, *refs):
    n_arrays = 1 + max(load[0] for load in loads)
    plane = refs[0]
    arrays = refs[:n_arrays]
    out_ref, pool, more, done, in_sem, out_sem = refs[-6:]
    block = out_ref.shape[-1]
    n_out = table[0]
    zero_entry = pool.shape[0] - 1

    copies = []
    for number, (which, at, entry, first, size, wanted) in enumerate(loads):
        source = arrays[which] if at is None else arrays[which].at[at]
        copy = pltpu.make_async_copy(
            source.at[pl.ds(0, size * block)],
            pool.at[entry, pl.ds(first * block, size * block)],
            in_sem.at[number],
        )
        copies.append(((table[wanted] != 0) & (n_out > 0), copy))
    for here, copy in copies:
        pl.when(here)(copy.start)

    def decode(index):
        entry = lax.shift_right_logical(index, STRIDE.bit_length() - 1)
        return entry, pl.multiple_of(jnp.bitwise_and(index, STRIDE - 1) * block, block)

    pool[zero_entry, pl.ds(0, block)] = jnp.zeros((block, block), pool.dtype)
    for here, copy in copies:
        pl.when(here)(copy.wait)

    def product(term, live):
        entry, first = decode(
            jnp.where(live, table[layout["lefts"] + term], zero_entry * STRIDE)
        )
        left = pool[entry, pl.ds(first, block)]
        entry, first = decode(jnp.where(live, table[layout["rights"] + term], 0))
        return jnp.dot(left, plane[entry, pl.ds(first, block)], preferred_element_type=jnp.float32)

    def write(number, slot):
        output = table[layout["outs"] + number]
        return pltpu.make_async_copy(done.at[slot], out_ref.at[output], out_sem.at[slot])

    def one_batch(batch, term):
        begins, counts = [], []
        last = term
        for local in range(BATCH):
            begins.append(last)
            counts.append(table[layout["counts"] + batch * BATCH + local])
            last = last + counts[local]

        half = lax.rem(batch, 2) * BATCH
        for local in range(BATCH):
            @pl.when(batch >= 2)
            def _():
                write((batch - 2) * BATCH + local, half + local).wait()

            @pl.when(counts[local] > 2)
            def _():
                more[local] = product(begins[local] + 2, True)

                def one_term(number, carry):
                    more[local] += product(number, True)
                    return carry

                lax.fori_loop(begins[local] + 3, begins[local] + counts[local], one_term, 0)

            @pl.when(counts[local] <= 2)
            def _():
                more[local] = jnp.zeros_like(more[local])

        for local in range(BATCH):
            output = table[layout["outs"] + batch * BATCH + local]
            square = more[local]
            for place in range(2):
                live = counts[local] > place
                square = square + product(jnp.where(live, begins[local] + place, 0), live)
            flag = table[layout["flags"] + output // kept].astype(jnp.float32)
            own = table[layout["owns"] + output]
            entry, first = decode(jnp.where(own >= 0, own, zero_entry * STRIDE))
            mine = pool[entry, pl.ds(first, block)].astype(jnp.float32)
            result = (2.0 * flag) * mine + (1.0 - 2.0 * flag) * square
            done[half + local] = result.astype(done.dtype)
        for local in range(BATCH):
            @pl.when(batch * BATCH + local < n_out)
            def _():
                write(batch * BATCH + local, half + local).start()

        return last

    n_batches = (n_out + BATCH - 1) // BATCH
    lax.fori_loop(0, n_batches, one_batch, jnp.int32(0))
    for back in range(2):
        batch = n_batches - 1 - back
        for local in range(BATCH):
            number = jnp.maximum(batch, 0) * BATCH + local

            @pl.when((batch >= 0) & (number < n_out))
            def _():
                write(number, lax.rem(batch, 2) * BATCH + local).wait()


def multiply(arrays, loads, n_entries, layout, table, shape, before=None):
    rows, kept, block, dtype = shape
    outputs = rows * kept
    smem = pl.BlockSpec(memory_space=pltpu.SMEM)
    hbm = pl.BlockSpec(memory_space=pltpu.HBM)
    blocks = (n_entries + 1 + arrays[0].shape[0]) * PACKED + 4 * BATCH
    vmem = blocks * block * block * 2 + (6 << 20)
    operands = [table, *arrays]
    whole = pl.BlockSpec(memory_space=pltpu.VMEM)
    in_specs = [smem, whole] + [hbm] * (len(arrays) - 1)
    aliases = {}
    if before is not None:
        operands += [before[1], before[0]]
        in_specs += [smem, hbm]
        aliases = {len(operands) - 1: 0}
    return pl.pallas_call(
        functools.partial(multiply_kernel, loads, kept, layout),
        out_shape=jax.ShapeDtypeStruct((outputs, block, block), dtype),
        in_specs=in_specs,
        out_specs=hbm,
        scratch_shapes=[
            pltpu.VMEM((n_entries + 1, PACKED * block, block), dtype),
            pltpu.VMEM((BATCH, block, block), jnp.float32),
            pltpu.VMEM((2 * BATCH, block, block), dtype),
            pltpu.SemaphoreType.DMA((len(loads),)),
            pltpu.SemaphoreType.DMA((2 * BATCH,)),
        ],
        input_output_aliases=aliases,
        compiler_params=pltpu.CompilerParams(vmem_limit_bytes=vmem),
    )(*operands)


def shift(array, pairs):
    return lax.ppermute(array, "col", pairs)


def gather_line(part):
    first = shift(part, [(0, 1), (1, 0), (2, 3), (3, 2)])
    middle = shift(part, [(1, 2), (2, 1)])
    end_two = shift(middle, [(1, 0), (2, 3)])
    middle_two = shift(first, [(1, 2), (2, 1)])
    end_three = shift(middle_two, [(1, 0), (2, 3)])
    return {
        "first": first,
        "middle": middle,
        "end_two": end_two,
        "middle_two": middle_two,
        "end_three": end_three,
    }


def running_count(fill):
    count = fill.shape[-1]
    before = jnp.arange(count)[:, None] < jnp.arange(count)[None, :]
    return jnp.sum(jnp.where(before, fill[..., :, None], 0), axis=-2)


def places(cols):
    flat = (cols >= 0).astype(jnp.int32).reshape(cols.shape[:-2] + (-1,))
    return running_count(flat).reshape(cols.shape)


def make_table(left_of, right_of, owns, flags, chosen, width, wanted):
    kept = right_of.shape[0] // left_of.shape[0]
    outputs = right_of.shape[0]
    left_of = jnp.repeat(left_of, kept, axis=0)
    live = (left_of > 0) & (right_of > 0) & chosen[:, None]
    counts = jnp.sum(live.astype(jnp.int32), axis=1)
    term = jnp.where(live, running_count(live.astype(jnp.int32)), -1)
    across = jnp.arange(width, dtype=jnp.int32)
    pick = term[:, None, :] == across[:, None]
    lefts = jnp.sum(jnp.where(pick, left_of[:, None, :] - 1, 0), axis=2)
    rights = jnp.sum(jnp.where(pick, right_of[:, None, :] - 1, 0), axis=2)
    flat = jnp.where(across < counts[:, None], running_count(counts)[:, None] + across, -1)
    pick = flat[None] == jnp.arange(PACKED * width, dtype=jnp.int32)[:, None, None]
    lefts = jnp.sum(jnp.where(pick, lefts, 0), axis=(1, 2))
    rights = jnp.sum(jnp.where(pick, rights, 0), axis=(1, 2))
    every = jnp.arange(outputs, dtype=jnp.int32)
    number = jnp.where(chosen, running_count(chosen.astype(jnp.int32)), -1)
    pick = number[None, :] == every[:, None]
    outs = jnp.sum(jnp.where(pick, every, 0), axis=1)
    ordered = jnp.sum(jnp.where(pick, counts, 0), axis=1)
    sizes = jnp.stack([jnp.sum(chosen.astype(jnp.int32)), jnp.sum(counts)])
    spare = jnp.zeros((BATCH,), jnp.int32)
    lists = {
        "sizes": sizes,
        "wanted": wanted,
        "outs": jnp.concatenate([outs, spare]),
        "counts": jnp.concatenate([ordered, spare]),
        "lefts": lefts,
        "rights": rights,
        "owns": owns,
        "flags": flags,
    }
    layout = {}
    first = 0
    for name, values in lists.items():
        layout[name] = first
        first += values.shape[0]
    return jnp.concatenate(list(lists.values())), layout


def per_device(x_blocks, x_cols, out_cols, branch_flag):
    rows, slots = x_cols.shape
    kept = out_cols.shape[1]
    block = x_blocks.shape[-1]
    dtype = x_blocks.dtype
    n_row = lax.axis_size("row")
    n_col = lax.axis_size("col")
    row = lax.axis_index("row")
    col = lax.axis_index("col")
    n_blocks = n_row * rows
    width = n_col * slots
    shape = (rows, kept, block, dtype)

    part_a, part_b, full = pack(x_blocks, x_cols, branch_flag, row * rows)

    def facts(array):
        first = array.shape[-2] - NOTE_ROWS
        return array[..., first : first + rows, :slots].astype(jnp.int32)

    plane = lax.all_gather(full, "row", axis=0)
    plane_cols = facts(plane)

    own_trace = jnp.sum(plane[:, PACKED * block + rows, :3].astype(jnp.float32))
    heights = jnp.arange(n_col, dtype=jnp.int32)
    traces = jnp.where(heights == col, own_trace, 0.0)
    for step in range(1, n_col):
        other = shift(own_trace, [(i, i ^ step) for i in range(n_col)])
        traces = jnp.where(heights == jnp.bitwise_xor(col, step), other, traces)
    trace = jnp.sum(traces).reshape(1)

    targets = out_cols.reshape(rows * kept)
    right_at = places(plane_cols) + STRIDE * jnp.arange(n_row, dtype=jnp.int32)[:, None, None]
    hit = plane_cols.reshape(n_blocks, slots)[None] == targets[:, None, None]
    right_of = jnp.sum(jnp.where(hit, right_at.reshape(n_blocks, slots) + 1, 0), axis=2)
    hit = x_cols[:, None, :] == out_cols[:, :, None]
    owns = jnp.sum(jnp.where(hit, places(x_cols)[:, None, :] + 1, 0), axis=2) - 1
    owns = owns.reshape(rows * kept)

    every = jnp.arange(n_blocks, dtype=jnp.int32)

    def straight(cols, entries, wanted):
        at = places(cols) + STRIDE * entries[:, None, None]
        hit = (cols[..., None] == every) & (wanted[:, None, None, None] != 0)
        return jnp.sum(jnp.where(hit, at[..., None] + 1, 0), axis=(0, 2))

    everything = jnp.ones((rows * kept,), bool)
    one = jnp.ones((1,), jnp.int32)
    if n_col != 4:
        line = lax.all_gather(full, "col", axis=0)
        entries = 1 + jnp.arange(n_col, dtype=jnp.int32)
        left_of = straight(facts(line), entries, jnp.ones((n_col,), jnp.int32))
        table, layout = make_table(
            left_of, right_of, owns, branch_flag, everything, width, one
        )
        loads = [(2, None, 0, 0, PACKED, 2)]
        loads += [(1, c, 1 + c, 0, PACKED, 2) for c in range(n_col)]
        purified = multiply([plane, line, full], tuple(loads), 1 + n_col, layout, table, shape)
        return purified.reshape(rows, kept, block, block), trace

    line = [gather_line(part) for part in (part_a, part_b)]
    note = {name: facts(array) for name, array in line[0].items()}
    at_end = (col == 0) | (col == n_col - 1)
    end = at_end.astype(jnp.int32)
    wanted = jnp.stack([jnp.int32(1), end, 1 - end])
    always, at_ends, inside = 2, 3, 4

    arrays = [plane, full]
    loads = [(1, None, 0, 0, PACKED, always)]

    def add(name, entry, wanted):
        spans = ((0, SPLIT), (SPLIT, PACKED - SPLIT))
        for which in range(2):
            loads.append((len(arrays), None, entry) + spans[which] + (wanted,))
            arrays.append(line[which][name])

    early_cols = [x_cols, note["first"], jnp.where(at_end, note["end_two"], note["middle"])]
    early_cols = jnp.stack(early_cols + [note["middle_two"]])
    early_wanted = jnp.stack([jnp.int32(1)] * 3 + [1 - end])
    early = straight(early_cols, jnp.arange(4, dtype=jnp.int32), early_wanted)
    add("first", 1, always)
    add("middle", 2, inside)
    add("end_two", 2, at_ends)
    add("middle_two", 3, inside)
    table, layout = make_table(early, right_of, owns, branch_flag, everything, width, wanted)
    purified = multiply(list(arrays), tuple(loads), 4, layout, table, shape)

    farthest, purified = lax.optimization_barrier((note["end_three"], purified))
    late = straight(farthest[None], jnp.array([3], jnp.int32), end[None])
    meets = (jnp.repeat(late, kept, axis=0) > 0) & (right_of > 0)
    chosen = jnp.any(meets, axis=1)
    add("end_three", 3, at_ends)
    table, layout = make_table(early + late, right_of, owns, branch_flag, chosen, width, wanted)
    before = (purified, trace)
    purified = multiply(list(arrays), tuple(loads), 4, layout, table, shape, before)
    return purified.reshape(rows, kept, block, block), trace


def solution(mesh):
    in_specs = (P("row", "col", None, None), P("row", "col"), P("row", "col"), P("row"))
    out_specs = (P("row", "col", None, None), P())
    return jax.shard_map(
        per_device, mesh=mesh, in_specs=in_specs, out_specs=out_specs, check_vma=False
    )
```

```python
import functools

import jax
import jax.numpy as jnp
from jax import lax
from jax.experimental import pallas as pl
from jax.experimental.pallas import tpu as pltpu
from jax.sharding import PartitionSpec as P

PACKED = 13
SPLIT = (PACKED + 1) // 2
STRIDE = 1 << (PACKED - 1).bit_length()
NOTE_ROWS = 16


def pack_kernel(
    cols_ref, flag_ref, first_ref, x_ref, part_a, part_b, full, note, norm, zeros, sems
):
    count, block, _ = x_ref.shape
    slots = cols_ref.shape[0]
    rows = count // slots
    sends = []
    place = jnp.int32(0)
    for index in range(count):
        filled = cols_ref[index % slots, index // slots] >= 0
        targets = (
            (full, filled, place),
            (part_a, filled & (place < SPLIT), place),
            (part_b, filled & (place >= SPLIT), place - SPLIT),
        )
        for which, (out, wanted, target) in enumerate(targets):
            target = pl.multiple_of(jnp.where(wanted, target, 0) * block, block)
            copy = pltpu.make_async_copy(
                x_ref.at[index], out.at[pl.ds(target, block)], sems.at[which, index]
            )
            pl.when(wanted)(copy.start)
            sends.append((wanted, copy))
        place = place + filled.astype(jnp.int32)

    blank = pltpu.make_async_copy(zeros, full.at[pl.ds(0, block)], sems.at[0, count + 1])

    @pl.when(place == 0)
    def _():
        zeros[...] = jnp.zeros_like(zeros)
        blank.start()

    sends.append((place == 0, blank))

    norm[...] = jnp.zeros_like(norm)
    eye_rows = lax.broadcasted_iota(jnp.int32, (block, block), 0)
    eye = eye_rows == lax.broadcasted_iota(jnp.int32, (block, block), 1)
    for index in range(count):
        row = index // slots
        col = cols_ref[index % slots, row]
        flag = flag_ref[row]

        @pl.when(col >= 0)
        def _():
            values = x_ref[index].astype(jnp.float32)
            weight = (1 - 2 * flag).astype(jnp.float32)
            norm[...] += weight * jnp.sum(values * values, axis=0, keepdims=True)

        @pl.when((col == first_ref[0] + row) & (flag != 0))
        def _():
            values = x_ref[index].astype(jnp.float32)
            norm[...] += 2.0 * jnp.sum(jnp.where(eye, values, 0.0), axis=0, keepdims=True)

    trace = jnp.full(note.shape, jnp.sum(norm[...]), jnp.float32)
    high = trace.astype(note.dtype).astype(jnp.float32)
    middle = (trace - high).astype(note.dtype).astype(jnp.float32)
    low = trace - high - middle
    down = lax.broadcasted_iota(jnp.int32, note.shape, 0)
    across = lax.broadcasted_iota(jnp.int32, note.shape, 1)
    facts = jnp.where(across == 0, high, jnp.where(across == 1, middle, low))
    facts = jnp.where((down == rows) & (across < 3), facts, 0.0)
    for index in range(count):
        here = (down == index // slots) & (across == index % slots)
        facts = jnp.where(here, cols_ref[index % slots, index // slots].astype(jnp.float32), facts)
    note[...] = facts.astype(note.dtype)
    for which, out in enumerate((full, part_a, part_b)):
        target = out.at[pl.ds(out.shape[0] - NOTE_ROWS, NOTE_ROWS)]
        copy = pltpu.make_async_copy(note, target, sems.at[which, count])
        copy.start()
        sends.append((None, copy))
    for wanted, copy in sends:
        copy.wait() if wanted is None else pl.when(wanted)(copy.wait)


def pack(x_blocks, x_cols, branch_flag, first_row):
    rows, slots, block, _ = x_blocks.shape
    count = rows * slots
    smem = pl.BlockSpec(memory_space=pltpu.SMEM)
    hbm = pl.BlockSpec(memory_space=pltpu.HBM)
    return pl.pallas_call(
        pack_kernel,
        out_shape=[
            jax.ShapeDtypeStruct((size * block + NOTE_ROWS, block), x_blocks.dtype)
            for size in (SPLIT, PACKED - SPLIT, PACKED)
        ],
        in_specs=[smem, smem, smem, pl.BlockSpec(memory_space=pltpu.VMEM)],
        out_specs=[hbm] * 3,
        scratch_shapes=[
            pltpu.VMEM((NOTE_ROWS, block), x_blocks.dtype),
            pltpu.VMEM((1, block), jnp.float32),
            pltpu.VMEM((block, block), x_blocks.dtype),
            pltpu.SemaphoreType.DMA((3, count + 2)),
        ],
        compiler_params=pltpu.CompilerParams(vmem_limit_bytes=(4 * count * block * block) + (8 << 20)),
    )(x_cols.T, branch_flag, first_row.reshape(1), x_blocks.reshape(count, block, block))


BATCH = 4


def multiply_kernel(loads, kept, layout, turned, early, table, plane, *refs):
    arrays = refs[: 1 + max(load[0] for load in loads)]
    if early:
        out_ref, token, pool, more, done, in_sem, out_sem = refs[-7:]
        token[0] = 0
    else:
        out_ref, pool, more, done, in_sem, out_sem, ring, ring_sem = refs[-8:]
        depth = ring.shape[0] - 1
    block = out_ref.shape[-1]
    n_out = table[0]
    n_terms = table[1]
    zero_entry = pool.shape[0] - 1

    copies = []
    for number, (which, at, entry, first, size, wanted) in enumerate(loads):
        source = arrays[which] if at is None else arrays[which].at[at]
        copy = pltpu.make_async_copy(
            source.at[pl.ds(0, size * block)],
            pool.at[entry, pl.ds(first * block, size * block)],
            in_sem.at[number],
        )
        copies.append(((table[wanted] != 0) & (n_out > 0), copy))
    for here, copy in copies:
        pl.when(here)(copy.start)

    def decode(index):
        entry = lax.shift_right_logical(index, STRIDE.bit_length() - 1)
        return entry, pl.multiple_of(jnp.bitwise_and(index, STRIDE - 1) * block, block)

    def fetch(term):
        entry, first = decode(table[layout["rights"] + term])
        slot = lax.rem(term, depth)
        return pltpu.make_async_copy(
            plane.at[entry, pl.ds(first, block)], ring.at[slot], ring_sem.at[slot]
        )

    if not early:
        def begin(term, carry):
            fetch(term).start()
            return carry

        lax.fori_loop(0, jnp.minimum(depth, n_terms), begin, 0)
        ring[depth] = jnp.zeros((block, block), ring.dtype)

    pool[zero_entry, pl.ds(0, block)] = jnp.zeros((block, block), pool.dtype)

    if turned is not None:
        is_wanted, at, target = turned

        @pl.when(table[is_wanted] != 0)
        def _():
            down = lax.broadcasted_iota(jnp.int32, (block, block), 0)
            eye = down == lax.broadcasted_iota(jnp.int32, (block, block), 1)
            eye = eye.astype(jnp.float32).astype(pool.dtype)

            def turn(place, carry):
                first = pl.multiple_of(place * block, block)
                for entry in range(2):
                    straight = plane[table[at] + entry, pl.ds(first, block)]
                    pool[target + entry, pl.ds(first, block)] = lax.dot_general(
                        eye, straight, (((1,), (1,)), ((), ())), preferred_element_type=jnp.float32
                    ).astype(pool.dtype)
                return carry

            lax.fori_loop(0, PACKED, turn, 0)

    for here, copy in copies:
        pl.when(here)(copy.wait)

    def product(term, live):
        entry, first = decode(
            jnp.where(live, table[layout["lefts"] + term], zero_entry * STRIDE)
        )
        left = pool[entry, pl.ds(first, block)]
        if early:
            entry, first = decode(jnp.where(live, table[layout["rights"] + term], 0))
            right = plane[entry, pl.ds(first, block)]
        else:
            right = ring[jnp.where(live, lax.rem(term, depth), depth)]
        return jnp.dot(left, right, preferred_element_type=jnp.float32)

    def write(number, slot):
        output = table[layout["outs"] + number]
        return pltpu.make_async_copy(done.at[slot], out_ref.at[output], out_sem.at[slot])

    def one_batch(batch, term):
        begins, counts = [], []
        last = term
        for local in range(BATCH):
            begins.append(last)
            counts.append(table[layout["counts"] + batch * BATCH + local])
            last = last + counts[local]

        if not early:
            def arrived(number, carry):
                fetch(number).wait()
                return carry

            lax.fori_loop(term, last, arrived, 0)
        half = lax.rem(batch, 2) * BATCH
        for local in range(BATCH):
            @pl.when(batch >= 2)
            def _():
                write((batch - 2) * BATCH + local, half + local).wait()

            more[local] = jnp.zeros_like(more[local])

            def two_terms(pair, carry):
                number = begins[local] + 2 + 2 * pair
                second = number + 1 < begins[local] + counts[local]
                more[local] += product(number, True) + product(
                    jnp.where(second, number + 1, 0), second
                )
                return carry

            lax.fori_loop(0, (counts[local] - 1) // 2, two_terms, 0)

        for local in range(BATCH):
            output = table[layout["outs"] + batch * BATCH + local]
            square = more[local]
            for place in range(2):
                live = counts[local] > place
                square = square + product(jnp.where(live, begins[local] + place, 0), live)
            flag = table[layout["flags"] + output // kept].astype(jnp.float32)
            own = table[layout["owns"] + output]
            entry, first = decode(jnp.where(own >= 0, own, zero_entry * STRIDE))
            mine = pool[entry, pl.ds(first, block)].astype(jnp.float32)
            result = (2.0 * flag) * mine + (1.0 - 2.0 * flag) * square
            done[half + local] = result.astype(done.dtype)
        for local in range(BATCH):
            @pl.when(batch * BATCH + local < n_out)
            def _():
                write(batch * BATCH + local, half + local).start()

        if not early:
            def refill(number, carry):
                fetch(number + depth).start()
                return carry

            lax.fori_loop(term, jnp.clip(n_terms - depth, term, last), refill, 0)
        return last

    n_batches = (n_out + BATCH - 1) // BATCH
    lax.fori_loop(0, n_batches, one_batch, jnp.int32(0))
    for back in range(2):
        batch = n_batches - 1 - back
        for local in range(BATCH):
            number = jnp.maximum(batch, 0) * BATCH + local

            @pl.when((batch >= 0) & (number < n_out))
            def _():
                write(number, lax.rem(batch, 2) * BATCH + local).wait()


def multiply(plane, arrays, loads, n_entries, layout, table, shape, turned=None, before=None):
    rows, kept, block, dtype = shape
    outputs = rows * kept
    early = before is None
    smem = pl.BlockSpec(memory_space=pltpu.SMEM)
    hbm = pl.BlockSpec(memory_space=pltpu.HBM)
    scratch = [
        pltpu.VMEM((n_entries + 1, PACKED * block, block), dtype),
        pltpu.VMEM((BATCH, block, block), jnp.float32),
        pltpu.VMEM((2 * BATCH, block, block), dtype),
        pltpu.SemaphoreType.DMA((len(loads),)),
        pltpu.SemaphoreType.DMA((2 * BATCH,)),
    ]
    operands = [table, plane, *arrays]
    in_specs = [smem, pl.BlockSpec(memory_space=pltpu.VMEM)] + [hbm] * len(arrays)
    out_shape = [jax.ShapeDtypeStruct((outputs, block, block), dtype)]
    out_specs = [hbm]
    aliases = {}
    if early:
        out_shape.append(jax.ShapeDtypeStruct((1,), jnp.int32))
        out_specs.append(smem)
        blocks = (n_entries + 1 + plane.shape[0]) * PACKED + 4 * BATCH
        vmem = blocks * block * block * 2 + (6 << 20)
    else:
        depth = 32
        scratch += [
            pltpu.VMEM((depth + 1, block, block), dtype),
            pltpu.SemaphoreType.DMA((depth,)),
        ]
        in_specs[1] = hbm
        operands += [before[1], before[0]]
        in_specs += [smem, hbm]
        aliases = {len(operands) - 1: 0}
        vmem = 58 << 20
    return pl.pallas_call(
        functools.partial(multiply_kernel, loads, kept, layout, turned, early),
        out_shape=out_shape,
        in_specs=in_specs,
        out_specs=out_specs,
        scratch_shapes=scratch,
        input_output_aliases=aliases,
        compiler_params=pltpu.CompilerParams(vmem_limit_bytes=vmem),
    )(*operands)


def shift(array, pairs):
    return lax.ppermute(array, "col", pairs)


def gather_line(part):
    first = shift(part, [(0, 1), (1, 0), (2, 3), (3, 2)])
    middle = shift(part, [(1, 2), (2, 1)])
    end_two = shift(middle, [(1, 0), (2, 3)])
    middle_two = shift(first, [(1, 2), (2, 1)])
    pairs = []
    for row in range(lax.axis_size("row")):
        pairs += [(4 * row + 1, 4 * row)] * (row // 2 != 0) + [(4 * row + 2, 4 * row + 3)] * (row // 2 != 3)
    end_three = lax.ppermute(middle_two, ("row", "col"), pairs)
    return {
        "first": first,
        "middle": middle,
        "end_two": end_two,
        "middle_two": middle_two,
        "end_three": end_three,
    }


def running_count(fill):
    count = fill.shape[-1]
    before = jnp.arange(count)[:, None] < jnp.arange(count)[None, :]
    return jnp.sum(jnp.where(before, fill[..., :, None], 0), axis=-2)


def places(cols):
    flat = (cols >= 0).astype(jnp.int32).reshape(cols.shape[:-2] + (-1,))
    return running_count(flat).reshape(cols.shape)


def make_table(left_of, right_of, owns, flags, chosen, width, wanted):
    kept = right_of.shape[0] // left_of.shape[0]
    outputs = right_of.shape[0]
    left_of = jnp.repeat(left_of, kept, axis=0)
    live = (left_of > 0) & (right_of > 0) & chosen[:, None]
    counts = jnp.sum(live.astype(jnp.int32), axis=1)
    term = jnp.where(live, running_count(live.astype(jnp.int32)), -1)
    across = jnp.arange(width, dtype=jnp.int32)
    pick = term[:, None, :] == across[:, None]
    lefts = jnp.sum(jnp.where(pick, left_of[:, None, :] - 1, 0), axis=2)
    rights = jnp.sum(jnp.where(pick, right_of[:, None, :] - 1, 0), axis=2)
    flat = jnp.where(across < counts[:, None], running_count(counts)[:, None] + across, -1)
    pick = flat[None] == jnp.arange(PACKED * width, dtype=jnp.int32)[:, None, None]
    lefts = jnp.sum(jnp.where(pick, lefts, 0), axis=(1, 2))
    rights = jnp.sum(jnp.where(pick, rights, 0), axis=(1, 2))
    every = jnp.arange(outputs, dtype=jnp.int32)
    number = jnp.where(chosen, running_count(chosen.astype(jnp.int32)), -1)
    pick = number[None, :] == every[:, None]
    outs = jnp.sum(jnp.where(pick, every, 0), axis=1)
    ordered = jnp.sum(jnp.where(pick, counts, 0), axis=1)
    sizes = jnp.stack([jnp.sum(chosen.astype(jnp.int32)), jnp.sum(counts)])
    spare = jnp.zeros((BATCH,), jnp.int32)
    lists = {
        "sizes": sizes,
        "wanted": wanted,
        "outs": jnp.concatenate([outs, spare]),
        "counts": jnp.concatenate([ordered, spare]),
        "lefts": lefts,
        "rights": rights,
        "owns": owns,
        "flags": flags,
    }
    layout = {}
    first = 0
    for name, values in lists.items():
        layout[name] = first
        first += values.shape[0]
    return jnp.concatenate(list(lists.values())), layout


def per_device(x_blocks, x_cols, out_cols, branch_flag):
    rows, slots = x_cols.shape
    kept = out_cols.shape[1]
    block = x_blocks.shape[-1]
    dtype = x_blocks.dtype
    n_row = lax.axis_size("row")
    n_col = lax.axis_size("col")
    row = lax.axis_index("row")
    col = lax.axis_index("col")
    n_blocks = n_row * rows
    width = n_col * slots
    shape = (rows, kept, block, dtype)

    part_a, part_b, full = pack(x_blocks, x_cols, branch_flag, row * rows)

    def facts(array):
        first = array.shape[-2] - NOTE_ROWS
        return array[..., first : first + rows, :slots].astype(jnp.int32)

    plane = lax.all_gather(full, "row", axis=0)
    plane_cols = facts(plane)

    own_trace = jnp.sum(plane[:, PACKED * block + rows, :3].astype(jnp.float32))
    heights = jnp.arange(n_col, dtype=jnp.int32)
    traces = jnp.where(heights == col, own_trace, 0.0)
    for step in range(1, n_col):
        other = shift(own_trace, [(i, i ^ step) for i in range(n_col)])
        traces = jnp.where(heights == jnp.bitwise_xor(col, step), other, traces)
    trace = jnp.sum(traces).reshape(1)

    targets = out_cols.reshape(rows * kept)
    right_at = places(plane_cols) + STRIDE * jnp.arange(n_row, dtype=jnp.int32)[:, None, None]
    hit = plane_cols.reshape(n_blocks, slots)[None] == targets[:, None, None]
    right_of = jnp.sum(jnp.where(hit, right_at.reshape(n_blocks, slots) + 1, 0), axis=2)
    hit = x_cols[:, None, :] == out_cols[:, :, None]
    owns = jnp.sum(jnp.where(hit, places(x_cols)[:, None, :] + 1, 0), axis=2) - 1
    owns = owns.reshape(rows * kept)

    every = jnp.arange(n_blocks, dtype=jnp.int32)

    def straight(cols, entries, wanted):
        at = places(cols) + STRIDE * entries[:, None, None]
        hit = (cols[..., None] == every) & (wanted[:, None, None, None] != 0)
        return jnp.sum(jnp.where(hit, at[..., None] + 1, 0), axis=(0, 2))

    def turned(cols, entry, device, wanted):
        at = places(cols) + STRIDE * (entry + jnp.arange(2, dtype=jnp.int32)[:, None, None])
        own = row * rows + jnp.arange(rows, dtype=jnp.int32)
        hit = (cols[..., None] == own) & wanted
        found = jnp.sum(jnp.where(hit, at[..., None] + 1, 0), axis=2)
        names = device * rows + jnp.arange(2 * rows, dtype=jnp.int32).reshape(2, rows)
        found = jnp.where(names[:, :, None, None] == every, found[..., None], 0)
        return jnp.sum(found, axis=(0, 1))

    everything = jnp.ones((rows * kept,), bool)
    one = jnp.ones((1,), jnp.int32)
    if not (n_col == 4 and n_row == 8):
        line = lax.all_gather(full, "col", axis=0)
        entries = 1 + jnp.arange(n_col, dtype=jnp.int32)
        left_of = straight(facts(line), entries, jnp.ones((n_col,), jnp.int32))
        table, layout = make_table(
            left_of, right_of, owns, branch_flag, everything, width, one
        )
        loads = [(1, None, 0, 0, PACKED, 2)]
        loads += [(0, c, 1 + c, 0, PACKED, 2) for c in range(n_col)]
        purified, _ = multiply(
            plane, [line, full], tuple(loads), 1 + n_col, layout, table, shape
        )
        return purified.reshape(rows, kept, block, block), trace

    line = [gather_line(part) for part in (part_a, part_b)]
    note = {name: facts(array) for name, array in line[0].items()}
    at_end = (col == 0) | (col == n_col - 1)
    corner = at_end & (row // 2 == col)
    end = at_end.astype(jnp.int32)
    turn_row = 2 * (n_col - 1 - col)
    wanted = [jnp.int32(1), end, 1 - end, end - corner, corner, turn_row]
    wanted = jnp.stack([value.astype(jnp.int32) for value in wanted])
    always, at_ends, inside, at_far, at_corner, turn_at = range(2, 8)

    arrays = [full]
    loads = [(0, None, 0, 0, PACKED, always)]

    def add(name, entry, wanted):
        spans = ((0, SPLIT), (SPLIT, PACKED - SPLIT))
        for which in range(2):
            loads.append((len(arrays), None, entry) + spans[which] + (wanted,))
            arrays.append(line[which][name])

    early_cols = [x_cols, note["first"], jnp.where(at_end, note["end_two"], note["middle"])]
    early_cols = jnp.stack(early_cols + [note["middle_two"]])
    early_wanted = jnp.stack([jnp.int32(1)] * 3 + [1 - end])
    early = straight(early_cols, jnp.arange(4, dtype=jnp.int32), early_wanted)
    turn_cols = lax.dynamic_slice_in_dim(plane_cols, turn_row, 2, 0)
    early = early + turned(turn_cols, 4, turn_row, corner)
    add("first", 1, always)
    add("middle", 2, inside)
    add("end_two", 2, at_ends)
    add("middle_two", 3, inside)
    table, layout = make_table(early, right_of, owns, branch_flag, everything, width, wanted)
    purified, token = multiply(
        plane, list(arrays), tuple(loads), 6, layout, table, shape, (at_corner, turn_at, 4)
    )

    far_cols = (note["end_three"] + token)[None]
    late = straight(far_cols, jnp.array([3], jnp.int32), wanted[None, at_far - 2])
    meets = (jnp.repeat(late, kept, axis=0) > 0) & (right_of > 0)
    chosen = jnp.any(meets, axis=1)
    add("end_three", 3, at_far)
    table, layout = make_table(early + late, right_of, owns, branch_flag, chosen, width, wanted)
    (purified,) = multiply(
        plane, list(arrays), tuple(loads), 4, layout, table, shape, None, (purified, trace)
    )
    return purified.reshape(rows, kept, block, block), trace


def solution(mesh):
    in_specs = (P("row", "col", None, None), P("row", "col"), P("row", "col"), P("row"))
    out_specs = (P("row", "col", None, None), P())
    return jax.shard_map(
        per_device, mesh=mesh, in_specs=in_specs, out_specs=out_specs, check_vma=False
    )
```

```python
import functools

import jax
import jax.numpy as jnp
from jax import lax
from jax.experimental import pallas as pl
from jax.experimental.pallas import tpu as pltpu
from jax.sharding import PartitionSpec as P

PACKED = 13
SPLIT = (PACKED + 1) // 2
STRIDE = 1 << (PACKED - 1).bit_length()
VMEM_LIMIT = 58 << 20


def pack_kernel(cols_ref, x_ref, part_a, part_b, full, held, in_sems, sems):
    count, block, _ = x_ref.shape
    slots = cols_ref.shape[0]
    moves = []
    place = jnp.int32(0)
    for index in range(count):
        filled = cols_ref[index % slots, index // slots] >= 0
        load = pltpu.make_async_copy(x_ref.at[index], held.at[index], in_sems.at[index])
        pl.when(filled)(load.start)
        moves.append((filled, place, load))
        place = place + filled.astype(jnp.int32)
    sends = []
    for index, (filled, place, load) in enumerate(moves):
        pl.when(filled)(load.wait)
        targets = (
            (full, filled, place),
            (part_a, filled & (place < SPLIT), place),
            (part_b, filled & (place >= SPLIT), place - SPLIT),
        )
        for which, (out, wanted, target) in enumerate(targets):
            target = pl.multiple_of(jnp.where(wanted, target, 0) * block, block)
            copy = pltpu.make_async_copy(
                held.at[index], out.at[pl.ds(target, block)], sems.at[which, index]
            )
            pl.when(wanted)(copy.start)
            sends.append((wanted, copy))
    for wanted, copy in sends:
        pl.when(wanted)(copy.wait)


def pack(x_blocks, x_cols):
    rows, slots, block, _ = x_blocks.shape
    count = rows * slots
    hbm = pl.BlockSpec(memory_space=pltpu.HBM)
    return pl.pallas_call(
        pack_kernel,
        out_shape=[
            jax.ShapeDtypeStruct((size * block, block), x_blocks.dtype)
            for size in (SPLIT, PACKED - SPLIT, PACKED)
        ],
        in_specs=[pl.BlockSpec(memory_space=pltpu.SMEM), hbm],
        out_specs=[hbm] * 3,
        scratch_shapes=[
            pltpu.VMEM((count, block, block), x_blocks.dtype),
            pltpu.SemaphoreType.DMA((count,)),
            pltpu.SemaphoreType.DMA((3, count)),
        ],
        compiler_params=pltpu.CompilerParams(vmem_limit_bytes=VMEM_LIMIT),
    )(x_cols.T, x_blocks.reshape(count, block, block))


BATCH = 4


def multiply_kernel(loads, kept, layout, turned, table, plane, *refs):
    arrays = refs[: 1 + max(load[0] for load in loads)]
    out_ref, pool, ring, more, done, in_sem, turn_sem, ring_sem, out_sem = refs[-9:]
    depth = ring.shape[0] - 1
    block = out_ref.shape[-1]
    n_out = table[0]
    n_terms = table[1]
    zero_entry = pool.shape[0] - 1

    copies = []
    for number, (which, at, entry, first, size, wanted) in enumerate(loads):
        source = arrays[which] if at is None else arrays[which].at[at]
        copy = pltpu.make_async_copy(
            source.at[pl.ds(0, size * block)],
            pool.at[entry, pl.ds(first * block, size * block)],
            in_sem.at[number],
        )
        copies.append(((table[wanted] != 0) & (n_out > 0), copy))
    for here, copy in copies:
        pl.when(here)(copy.start)

    def decode(index):
        entry = lax.shift_right_logical(index, STRIDE.bit_length() - 1)
        return entry, pl.multiple_of(jnp.bitwise_and(index, STRIDE - 1) * block, block)

    def fetch(term):
        entry, first = decode(table[layout["rights"] + term])
        slot = lax.rem(term, depth)
        return pltpu.make_async_copy(
            plane.at[entry, pl.ds(first, block)], ring.at[slot], ring_sem.at[slot]
        )

    def begin(term, carry):
        fetch(term).start()
        return carry

    if turned is not None:
        is_wanted, at, target = turned
        rows = pltpu.make_async_copy(
            plane.at[pl.ds(table[at], 2)], pool.at[pl.ds(target, 2)], turn_sem
        )
        pl.when(table[is_wanted] != 0)(rows.start)
    lax.fori_loop(0, jnp.minimum(depth, n_terms), begin, 0)
    ring[depth] = jnp.zeros((block, block), ring.dtype)
    pool[zero_entry, pl.ds(0, block)] = jnp.zeros((block, block), pool.dtype)

    if turned is not None:
        @pl.when(table[is_wanted] != 0)
        def _():
            down = lax.broadcasted_iota(jnp.int32, (block, block), 0)
            eye = down == lax.broadcasted_iota(jnp.int32, (block, block), 1)
            eye = eye.astype(jnp.float32).astype(pool.dtype)
            rows.wait()

            def turn(place, carry):
                first = pl.multiple_of(place * block, block)
                for entry in range(target, target + 2):
                    pool[entry, pl.ds(first, block)] = lax.dot_general(
                        eye,
                        pool[entry, pl.ds(first, block)],
                        (((1,), (1,)), ((), ())),
                        preferred_element_type=jnp.float32,
                    ).astype(pool.dtype)
                return carry

            lax.fori_loop(0, PACKED, turn, 0)

    for here, copy in copies:
        pl.when(here)(copy.wait)

    def product(term, live):
        entry, first = decode(
            jnp.where(live, table[layout["lefts"] + term], zero_entry * STRIDE)
        )
        left = pool[entry, pl.ds(first, block)]
        right = ring[jnp.where(live, lax.rem(term, depth), depth)]
        return jnp.dot(left, right, preferred_element_type=jnp.float32)

    def write(number, slot):
        output = table[layout["outs"] + number]
        return pltpu.make_async_copy(done.at[slot], out_ref.at[output], out_sem.at[slot])

    def one_batch(batch, term):
        begins, counts = [], []
        last = term
        for local in range(BATCH):
            begins.append(last)
            counts.append(table[layout["counts"] + batch * BATCH + local])
            last = last + counts[local]

        def arrived(number, carry):
            fetch(number).wait()
            return carry

        lax.fori_loop(term, last, arrived, 0)
        half = lax.rem(batch, 2) * BATCH
        for local in range(BATCH):
            @pl.when(batch >= 2)
            def _():
                write((batch - 2) * BATCH + local, half + local).wait()

            more[local] = jnp.zeros_like(more[local])

            def two_terms(pair, carry):
                number = begins[local] + 2 + 2 * pair
                second = number + 1 < begins[local] + counts[local]
                more[local] += product(number, True) + product(
                    jnp.where(second, number + 1, 0), second
                )
                return carry

            lax.fori_loop(0, (counts[local] - 1) // 2, two_terms, 0)

        for local in range(BATCH):
            output = table[layout["outs"] + batch * BATCH + local]
            square = more[local]
            for place in range(2):
                live = counts[local] > place
                square = square + product(jnp.where(live, begins[local] + place, 0), live)
            flag = table[layout["flags"] + output // kept].astype(jnp.float32)
            own = table[layout["owns"] + output]
            entry, first = decode(jnp.where(own >= 0, own, zero_entry * STRIDE))
            mine = pool[entry, pl.ds(first, block)].astype(jnp.float32)
            result = (2.0 * flag) * mine + (1.0 - 2.0 * flag) * square
            done[half + local] = result.astype(done.dtype)
        for local in range(BATCH):
            @pl.when(batch * BATCH + local < n_out)
            def _():
                write(batch * BATCH + local, half + local).start()

        def refill(number, carry):
            fetch(number + depth).start()
            return carry

        lax.fori_loop(term, jnp.clip(n_terms - depth, term, last), refill, 0)
        return last

    n_batches = (n_out + BATCH - 1) // BATCH
    lax.fori_loop(0, n_batches, one_batch, jnp.int32(0))
    for back in range(2):
        batch = n_batches - 1 - back
        for local in range(BATCH):
            number = jnp.maximum(batch, 0) * BATCH + local

            @pl.when((batch >= 0) & (number < n_out))
            def _():
                write(number, lax.rem(batch, 2) * BATCH + local).wait()


def multiply(plane, arrays, loads, n_entries, layout, table, shape, turned=None, before=None):
    rows, kept, block, dtype = shape
    outputs = rows * kept
    depth = 48
    smem = pl.BlockSpec(memory_space=pltpu.SMEM)
    hbm = pl.BlockSpec(memory_space=pltpu.HBM)
    operands = [table, plane, *arrays]
    aliases = {}
    if before is not None:
        operands.append(before)
        aliases = {len(operands) - 1: 0}
    return pl.pallas_call(
        functools.partial(multiply_kernel, loads, kept, layout, turned),
        out_shape=jax.ShapeDtypeStruct((outputs, block, block), dtype),
        in_specs=[smem] + [hbm] * (len(operands) - 1),
        out_specs=hbm,
        scratch_shapes=[
            pltpu.VMEM((n_entries + 1, PACKED * block, block), dtype),
            pltpu.VMEM((depth + 1, block, block), dtype),
            pltpu.VMEM((BATCH, block, block), jnp.float32),
            pltpu.VMEM((2 * BATCH, block, block), dtype),
            pltpu.SemaphoreType.DMA((len(loads),)),
            pltpu.SemaphoreType.DMA,
            pltpu.SemaphoreType.DMA((depth,)),
            pltpu.SemaphoreType.DMA((2 * BATCH,)),
        ],
        input_output_aliases=aliases,
        compiler_params=pltpu.CompilerParams(vmem_limit_bytes=VMEM_LIMIT),
    )(*operands)


def shift(array, pairs):
    return lax.ppermute(array, "col", pairs)


def gather_line(part):
    first = shift(part, [(0, 1), (1, 0), (2, 3), (3, 2)])
    middle = shift(part, [(1, 2), (2, 1)])
    end_two = shift(middle, [(1, 0), (2, 3)])
    middle_two = shift(first, [(1, 2), (2, 1)])
    pairs = []
    for row in range(lax.axis_size("row")):
        pairs += [(4 * row + 1, 4 * row)] * (row // 2 != 0) + [(4 * row + 2, 4 * row + 3)] * (row // 2 != 3)
    end_three = lax.ppermute(middle_two, ("row", "col"), pairs)
    return {
        "first": first,
        "middle": middle,
        "end_two": end_two,
        "middle_two": middle_two,
        "end_three": end_three,
    }


def running_count(fill):
    count = fill.shape[-1]
    before = jnp.arange(count)[:, None] < jnp.arange(count)[None, :]
    return jnp.sum(jnp.where(before, fill[..., :, None], 0), axis=-2)


def places(cols):
    flat = (cols >= 0).astype(jnp.int32).reshape(cols.shape[:-2] + (-1,))
    return running_count(flat).reshape(cols.shape)


def make_table(left_of, right_of, owns, flags, chosen, width, wanted):
    kept = right_of.shape[0] // left_of.shape[0]
    outputs = right_of.shape[0]
    left_of = jnp.repeat(left_of, kept, axis=0)
    live = (left_of > 0) & (right_of > 0) & chosen[:, None]
    counts = jnp.sum(live.astype(jnp.int32), axis=1)
    term = jnp.where(live, running_count(live.astype(jnp.int32)), -1)
    across = jnp.arange(width, dtype=jnp.int32)
    pick = term[:, None, :] == across[:, None]
    lefts = jnp.sum(jnp.where(pick, left_of[:, None, :] - 1, 0), axis=2)
    rights = jnp.sum(jnp.where(pick, right_of[:, None, :] - 1, 0), axis=2)
    flat = jnp.where(across < counts[:, None], running_count(counts)[:, None] + across, -1)
    pick = flat[None] == jnp.arange(PACKED * width, dtype=jnp.int32)[:, None, None]
    lefts = jnp.sum(jnp.where(pick, lefts, 0), axis=(1, 2))
    rights = jnp.sum(jnp.where(pick, rights, 0), axis=(1, 2))
    every = jnp.arange(outputs, dtype=jnp.int32)
    number = jnp.where(chosen, running_count(chosen.astype(jnp.int32)), -1)
    pick = number[None, :] == every[:, None]
    outs = jnp.sum(jnp.where(pick, every, 0), axis=1)
    ordered = jnp.sum(jnp.where(pick, counts, 0), axis=1)
    sizes = jnp.stack([jnp.sum(chosen.astype(jnp.int32)), jnp.sum(counts)])
    spare = jnp.zeros((BATCH,), jnp.int32)
    lists = {
        "sizes": sizes,
        "wanted": wanted,
        "outs": jnp.concatenate([outs, spare]),
        "counts": jnp.concatenate([ordered, spare]),
        "lefts": lefts,
        "rights": rights,
        "owns": owns,
        "flags": flags,
    }
    layout = {}
    first = 0
    for name, values in lists.items():
        layout[name] = first
        first += values.shape[0]
    return jnp.concatenate(list(lists.values())), layout


def local_trace(x_blocks, x_cols, branch_flag, first_row):
    rows, slots, block, _ = x_blocks.shape
    own_row = first_row + jnp.arange(rows, dtype=jnp.int32)
    flag = branch_flag.astype(jnp.float32)[:, None]
    norm_weight = jnp.where(x_cols >= 0, 1.0 - 2.0 * flag, 0.0)
    diag_weight = jnp.where(x_cols == own_row[:, None], 2.0 * flag, 0.0)
    values = x_blocks.astype(jnp.float32)
    eye = jnp.eye(block, dtype=jnp.float32)
    weight = norm_weight[:, :, None, None] * values + diag_weight[:, :, None, None] * eye
    return jnp.sum(weight * values)


def gather_facts(values):
    n_row = lax.axis_size("row")
    n_col = lax.axis_size("col")
    down, across = values.shape
    padded = jnp.pad(values.astype(jnp.float32), [(0, 0), (0, 128 - across)])
    every = lax.all_gather(padded, ("row", "col"), axis=0, tiled=True)
    return every.reshape(n_row, n_col, down, 128)[..., :across]


def per_device(x_blocks, x_cols, out_cols, branch_flag):
    rows, slots = x_cols.shape
    kept = out_cols.shape[1]
    block = x_blocks.shape[-1]
    dtype = x_blocks.dtype
    n_row = lax.axis_size("row")
    n_col = lax.axis_size("col")
    row = lax.axis_index("row")
    col = lax.axis_index("col")
    n_blocks = n_row * rows
    width = n_col * slots
    shape = (rows, kept, block, dtype)

    all_cols = gather_facts(x_cols).astype(jnp.int32)
    all_places = places(all_cols)
    part_a, part_b, full = pack(x_blocks, x_cols)
    plane = lax.all_gather(full, "row", axis=0)

    trace = local_trace(x_blocks, x_cols, branch_flag, row * rows)
    trace = jnp.sum(gather_facts(jnp.pad(trace.reshape(1, 1), [(0, 7), (0, 0)]))).reshape(1)

    plane_cols = lax.dynamic_index_in_dim(all_cols, col, 1, keepdims=False)
    plane_places = lax.dynamic_index_in_dim(all_places, col, 1, keepdims=False)
    targets = out_cols.reshape(rows * kept)
    right_at = plane_places + STRIDE * jnp.arange(n_row, dtype=jnp.int32)[:, None, None]
    hit = plane_cols.reshape(n_blocks, slots)[None] == targets[:, None, None]
    right_of = jnp.sum(jnp.where(hit, right_at.reshape(n_blocks, slots) + 1, 0), axis=2)
    hit = x_cols[:, None, :] == out_cols[:, :, None]
    owns = jnp.sum(jnp.where(hit, places(x_cols)[:, None, :] + 1, 0), axis=2) - 1
    owns = owns.reshape(rows * kept)

    every = jnp.arange(n_blocks, dtype=jnp.int32)
    line_cols = lax.dynamic_index_in_dim(all_cols, row, 0, keepdims=False)
    line_places = lax.dynamic_index_in_dim(all_places, row, 0, keepdims=False)

    def straight(entries, wanted):
        at = line_places + STRIDE * entries[:, None, None]
        hit = (line_cols[..., None] == every) & wanted[:, None, None, None]
        return jnp.sum(jnp.where(hit, at[..., None] + 1, 0), axis=(0, 2))

    def turned(entry, device, wanted):
        cols = lax.dynamic_slice_in_dim(plane_cols, device, 2, 0)
        at = lax.dynamic_slice_in_dim(plane_places, device, 2, 0)
        at = at + STRIDE * (entry + jnp.arange(2, dtype=jnp.int32)[:, None, None])
        own = row * rows + jnp.arange(rows, dtype=jnp.int32)
        hit = (cols[..., None] == own) & wanted
        found = jnp.sum(jnp.where(hit, at[..., None] + 1, 0), axis=2)
        names = device * rows + jnp.arange(2 * rows, dtype=jnp.int32).reshape(2, rows)
        found = jnp.where(names[:, :, None, None] == every, found[..., None], 0)
        return jnp.sum(found, axis=(0, 1))

    heights = jnp.arange(n_col, dtype=jnp.int32)
    if not (n_col == 4 and n_row == 8):
        line = lax.all_gather(full, "col", axis=0)
        left_of = straight(1 + heights, heights >= 0)
        everything = jnp.ones((rows * kept,), bool)
        one = jnp.ones((1,), jnp.int32)
        table, layout = make_table(left_of, right_of, owns, branch_flag, everything, width, one)
        loads = [(0, None, 0, 0, PACKED, 2)]
        loads += [(1, c, 1 + c, 0, PACKED, 2) for c in range(n_col)]
        purified = multiply(plane, [full, line], tuple(loads), 1 + n_col, layout, table, shape)
        return purified.reshape(rows, kept, block, block), trace

    line = [gather_line(part) for part in (part_a, part_b)]
    at_end = (col == 0) | (col == n_col - 1)
    corner = at_end & (row // 2 == col)
    far = at_end & ~corner
    turn_row = 2 * (n_col - 1 - col)
    wanted = [at_end | True, at_end, ~at_end, far, corner, turn_row]
    wanted = jnp.stack([value.astype(jnp.int32) for value in wanted])
    always, at_ends, inside, at_far, at_corner, turn_at = range(2, 8)

    second = jnp.where(col < 2, 2, 1)
    entries = jnp.where(heights == second, 2, 3)
    entries = jnp.where(heights == jnp.bitwise_xor(col, 1), 1, entries)
    entries = jnp.where(heights == col, 0, entries)
    early = straight(entries, (entries < 3) | ~at_end) + turned(4, turn_row, corner)
    late = straight(entries, (entries == 3) & far)
    meets = (jnp.repeat(late, kept, axis=0) > 0) & (right_of > 0)
    is_late = jnp.any(meets, axis=1)

    arrays = [full]
    loads = [(0, None, 0, 0, PACKED, always)]

    def add(name, entry, wanted):
        spans = ((0, SPLIT), (SPLIT, PACKED - SPLIT))
        for which in range(2):
            loads.append((len(arrays), None, entry) + spans[which] + (wanted,))
            arrays.append(line[which][name])

    def call(left_of, chosen, before=None):
        table, layout = make_table(left_of, right_of, owns, branch_flag, chosen, width, wanted)
        turn = (at_corner, turn_at, 4) if before is None else None
        return multiply(
            plane, list(arrays), tuple(loads), 6, layout, table, shape, turn, before
        )

    add("first", 1, always)
    add("middle", 2, inside)
    add("end_two", 2, at_ends)
    add("middle_two", 3, inside)
    purified = call(early, ~is_late)
    add("end_three", 3, at_far)
    purified = call(early + late, is_late, purified)
    return purified.reshape(rows, kept, block, block), trace


def solution(mesh):
    in_specs = (P("row", "col", None, None), P("row", "col"), P("row", "col"), P("row"))
    out_specs = (P("row", "col", None, None), P())
    return jax.shard_map(
        per_device, mesh=mesh, in_specs=in_specs, out_specs=out_specs, check_vma=False
    )
```

```python
import functools

import jax
import jax.numpy as jnp
from jax import lax
from jax.experimental import pallas as pl
from jax.experimental.pallas import tpu as pltpu
from jax.sharding import PartitionSpec as P

PACKED = 13
SPLIT = (PACKED + 1) // 2
STRIDE = 1 << (PACKED - 1).bit_length()
VMEM_LIMIT = 58 << 20


def pack_kernel(
    cols_ref, flag_ref, first_ref, x_ref, part_a, part_b, full, facts, held, norm, in_sems, sems
):
    count, block, _ = x_ref.shape
    slots = cols_ref.shape[0]
    loads = []
    place = jnp.int32(0)
    for index in range(count):
        filled = cols_ref[index % slots, index // slots] >= 0
        load = pltpu.make_async_copy(x_ref.at[index], held.at[index], in_sems.at[index])
        pl.when(filled)(load.start)
        loads.append((filled, place, load))
        place = place + filled.astype(jnp.int32)
    sends = []
    for index, (filled, place, load) in enumerate(loads):
        pl.when(filled)(load.wait)
        targets = (
            (full, filled, place),
            (part_a, filled & (place < SPLIT), place),
            (part_b, filled & (place >= SPLIT), place - SPLIT),
        )
        for which, (out, wanted, target) in enumerate(targets):
            target = pl.multiple_of(jnp.where(wanted, target, 0) * block, block)
            copy = pltpu.make_async_copy(
                held.at[index], out.at[pl.ds(target, block)], sems.at[which, index]
            )
            pl.when(wanted)(copy.start)
            sends.append((wanted, copy))

    norm[...] = jnp.zeros_like(norm)
    for index in range(count):
        row = index // slots
        col = cols_ref[index % slots, row]
        flag = flag_ref[row]

        @pl.when(col >= 0)
        def _():
            values = held[index].astype(jnp.float32)
            weight = (1 - 2 * flag).astype(jnp.float32)
            norm[...] += weight * jnp.sum(values * values, axis=0, keepdims=True)

        @pl.when((col == first_ref[0] + row) & (flag != 0))
        def _():
            values = held[index].astype(jnp.float32)
            eye = lax.broadcasted_iota(jnp.int32, (block, block), 0)
            eye = eye == lax.broadcasted_iota(jnp.int32, (block, block), 1)
            norm[...] += 2.0 * jnp.sum(jnp.where(eye, values, 0.0), axis=0, keepdims=True)

    down = lax.broadcasted_iota(jnp.int32, facts.shape, 0)
    across = lax.broadcasted_iota(jnp.int32, facts.shape, 1)
    values = jnp.where((down == 0) & (across == slots), jnp.sum(norm[...]), 0.0)
    for index in range(count):
        here = (down == index // slots) & (across == index % slots)
        value = cols_ref[index % slots, index // slots].astype(jnp.float32)
        values = jnp.where(here, value, values)
    facts[...] = values
    for wanted, copy in sends:
        pl.when(wanted)(copy.wait)


def pack(x_blocks, x_cols, branch_flag, first_row):
    rows, slots, block, _ = x_blocks.shape
    count = rows * slots
    smem = pl.BlockSpec(memory_space=pltpu.SMEM)
    hbm = pl.BlockSpec(memory_space=pltpu.HBM)
    packed = [
        jax.ShapeDtypeStruct((size * block, block), x_blocks.dtype)
        for size in (SPLIT, PACKED - SPLIT, PACKED)
    ]
    return pl.pallas_call(
        pack_kernel,
        out_shape=packed + [jax.ShapeDtypeStruct((rows, 128), jnp.float32)],
        in_specs=[smem, smem, smem, hbm],
        out_specs=[hbm] * 3 + [pl.BlockSpec(memory_space=pltpu.VMEM)],
        scratch_shapes=[
            pltpu.VMEM((count, block, block), x_blocks.dtype),
            pltpu.VMEM((1, block), jnp.float32),
            pltpu.SemaphoreType.DMA((count,)),
            pltpu.SemaphoreType.DMA((3, count)),
        ],
        compiler_params=pltpu.CompilerParams(vmem_limit_bytes=VMEM_LIMIT),
    )(x_cols.T, branch_flag, first_row.reshape(1), x_blocks.reshape(count, block, block))


BATCH = 4


def multiply_kernel(loads, kept, layout, turned, table, plane, *refs):
    arrays = refs[: 1 + max(load[0] for load in loads)]
    out_ref, pool, ring, more, done, in_sem, turn_sem, ring_sem, out_sem = refs[-9:]
    depth = ring.shape[0] - 1
    block = out_ref.shape[-1]
    n_out = table[0]
    n_terms = table[1]
    zero_entry = pool.shape[0] - 1

    copies = []
    for number, (which, at, entry, first, size, wanted) in enumerate(loads):
        source = arrays[which] if at is None else arrays[which].at[at]
        copy = pltpu.make_async_copy(
            source.at[pl.ds(0, size * block)],
            pool.at[entry, pl.ds(first * block, size * block)],
            in_sem.at[number],
        )
        copies.append(((table[wanted] != 0) & (n_out > 0), copy))
    for here, copy in copies:
        pl.when(here)(copy.start)

    def decode(index):
        entry = lax.shift_right_logical(index, STRIDE.bit_length() - 1)
        return entry, pl.multiple_of(jnp.bitwise_and(index, STRIDE - 1) * block, block)

    def fetch(term):
        entry, first = decode(table[layout["rights"] + term])
        slot = lax.rem(term, depth)
        return pltpu.make_async_copy(
            plane.at[entry, pl.ds(first, block)], ring.at[slot], ring_sem.at[slot]
        )

    def begin(term, carry):
        fetch(term).start()
        return carry

    if turned is not None:
        is_wanted, at, target = turned
        rows = pltpu.make_async_copy(
            plane.at[pl.ds(table[at], 2)], pool.at[pl.ds(target, 2)], turn_sem
        )
        pl.when(table[is_wanted] != 0)(rows.start)
    lax.fori_loop(0, jnp.minimum(depth, n_terms), begin, 0)
    ring[depth] = jnp.zeros((block, block), ring.dtype)
    pool[zero_entry, pl.ds(0, block)] = jnp.zeros((block, block), pool.dtype)

    if turned is not None:
        @pl.when(table[is_wanted] != 0)
        def _():
            down = lax.broadcasted_iota(jnp.int32, (block, block), 0)
            eye = down == lax.broadcasted_iota(jnp.int32, (block, block), 1)
            eye = eye.astype(jnp.float32).astype(pool.dtype)
            rows.wait()

            def turn(place, carry):
                first = pl.multiple_of(place * block, block)
                for entry in range(target, target + 2):
                    pool[entry, pl.ds(first, block)] = lax.dot_general(
                        eye,
                        pool[entry, pl.ds(first, block)],
                        (((1,), (1,)), ((), ())),
                        preferred_element_type=jnp.float32,
                    ).astype(pool.dtype)
                return carry

            lax.fori_loop(0, PACKED, turn, 0)

    for here, copy in copies:
        pl.when(here)(copy.wait)

    def product(term, live):
        entry, first = decode(
            jnp.where(live, table[layout["lefts"] + term], zero_entry * STRIDE)
        )
        left = pool[entry, pl.ds(first, block)]
        right = ring[jnp.where(live, lax.rem(term, depth), depth)]
        return jnp.dot(left, right, preferred_element_type=jnp.float32)

    def write(number, slot):
        output = table[layout["outs"] + number]
        return pltpu.make_async_copy(done.at[slot], out_ref.at[output], out_sem.at[slot])

    def one_batch(batch, term):
        begins, counts = [], []
        last = term
        for local in range(BATCH):
            begins.append(last)
            counts.append(table[layout["counts"] + batch * BATCH + local])
            last = last + counts[local]

        def arrived(number, carry):
            fetch(number).wait()
            return carry

        lax.fori_loop(term, last, arrived, 0)
        half = lax.rem(batch, 2) * BATCH
        for local in range(BATCH):
            @pl.when(batch >= 2)
            def _():
                write((batch - 2) * BATCH + local, half + local).wait()

            more[local] = jnp.zeros_like(more[local])

            def two_terms(pair, carry):
                number = begins[local] + 2 + 2 * pair
                second = number + 1 < begins[local] + counts[local]
                more[local] += product(number, True) + product(
                    jnp.where(second, number + 1, 0), second
                )
                return carry

            lax.fori_loop(0, (counts[local] - 1) // 2, two_terms, 0)

        for local in range(BATCH):
            output = table[layout["outs"] + batch * BATCH + local]
            square = more[local]
            for place in range(2):
                live = counts[local] > place
                square = square + product(jnp.where(live, begins[local] + place, 0), live)
            flag = table[layout["flags"] + output // kept].astype(jnp.float32)
            own = table[layout["owns"] + output]
            entry, first = decode(jnp.where(own >= 0, own, zero_entry * STRIDE))
            mine = pool[entry, pl.ds(first, block)].astype(jnp.float32)
            result = (2.0 * flag) * mine + (1.0 - 2.0 * flag) * square
            done[half + local] = result.astype(done.dtype)
        for local in range(BATCH):
            @pl.when(batch * BATCH + local < n_out)
            def _():
                write(batch * BATCH + local, half + local).start()

        def refill(number, carry):
            fetch(number + depth).start()
            return carry

        lax.fori_loop(term, jnp.clip(n_terms - depth, term, last), refill, 0)
        return last

    n_batches = (n_out + BATCH - 1) // BATCH
    lax.fori_loop(0, n_batches, one_batch, jnp.int32(0))
    for back in range(2):
        batch = n_batches - 1 - back
        for local in range(BATCH):
            number = jnp.maximum(batch, 0) * BATCH + local

            @pl.when((batch >= 0) & (number < n_out))
            def _():
                write(number, lax.rem(batch, 2) * BATCH + local).wait()


def multiply(plane, arrays, loads, n_entries, layout, table, shape, turned=None, before=None):
    rows, kept, block, dtype = shape
    outputs = rows * kept
    depth = 48
    smem = pl.BlockSpec(memory_space=pltpu.SMEM)
    hbm = pl.BlockSpec(memory_space=pltpu.HBM)
    operands = [table, plane, *arrays]
    aliases = {}
    if before is not None:
        operands.append(before)
        aliases = {len(operands) - 1: 0}
    return pl.pallas_call(
        functools.partial(multiply_kernel, loads, kept, layout, turned),
        out_shape=jax.ShapeDtypeStruct((outputs, block, block), dtype),
        in_specs=[smem] + [hbm] * (len(operands) - 1),
        out_specs=hbm,
        scratch_shapes=[
            pltpu.VMEM((n_entries + 1, PACKED * block, block), dtype),
            pltpu.VMEM((depth + 1, block, block), dtype),
            pltpu.VMEM((BATCH, block, block), jnp.float32),
            pltpu.VMEM((2 * BATCH, block, block), dtype),
            pltpu.SemaphoreType.DMA((len(loads),)),
            pltpu.SemaphoreType.DMA,
            pltpu.SemaphoreType.DMA((depth,)),
            pltpu.SemaphoreType.DMA((2 * BATCH,)),
        ],
        input_output_aliases=aliases,
        compiler_params=pltpu.CompilerParams(vmem_limit_bytes=VMEM_LIMIT),
    )(*operands)


def shift(array, pairs):
    return lax.ppermute(array, "col", pairs)


def gather_line(part):
    first = shift(part, [(0, 1), (1, 0), (2, 3), (3, 2)])
    middle = shift(part, [(1, 2), (2, 1)])
    end_two = shift(middle, [(1, 0), (2, 3)])
    middle_two = shift(first, [(1, 2), (2, 1)])
    pairs = []
    for row in range(lax.axis_size("row")):
        pairs += [(4 * row + 1, 4 * row)] * (row // 2 != 0) + [(4 * row + 2, 4 * row + 3)] * (row // 2 != 3)
    end_three = lax.ppermute(middle_two, ("row", "col"), pairs)
    return {
        "first": first,
        "middle": middle,
        "end_two": end_two,
        "middle_two": middle_two,
        "end_three": end_three,
    }


def running_count(fill):
    count = fill.shape[-1]
    before = jnp.arange(count)[:, None] < jnp.arange(count)[None, :]
    return jnp.sum(jnp.where(before, fill[..., :, None], 0), axis=-2)


def places(cols):
    flat = (cols >= 0).astype(jnp.int32).reshape(cols.shape[:-2] + (-1,))
    return running_count(flat).reshape(cols.shape)


def make_table(left_of, right_of, owns, flags, chosen, width, wanted):
    kept = right_of.shape[0] // left_of.shape[0]
    outputs = right_of.shape[0]
    left_of = jnp.repeat(left_of, kept, axis=0)
    live = (left_of > 0) & (right_of > 0) & chosen[:, None]
    counts = jnp.sum(live.astype(jnp.int32), axis=1)
    term = jnp.where(live, running_count(live.astype(jnp.int32)), -1)
    across = jnp.arange(width, dtype=jnp.int32)
    pick = term[:, None, :] == across[:, None]
    lefts = jnp.sum(jnp.where(pick, left_of[:, None, :] - 1, 0), axis=2)
    rights = jnp.sum(jnp.where(pick, right_of[:, None, :] - 1, 0), axis=2)
    flat = jnp.where(across < counts[:, None], running_count(counts)[:, None] + across, -1)
    pick = flat[None] == jnp.arange(PACKED * width, dtype=jnp.int32)[:, None, None]
    lefts = jnp.sum(jnp.where(pick, lefts, 0), axis=(1, 2))
    rights = jnp.sum(jnp.where(pick, rights, 0), axis=(1, 2))
    every = jnp.arange(outputs, dtype=jnp.int32)
    number = jnp.where(chosen, running_count(chosen.astype(jnp.int32)), -1)
    pick = number[None, :] == every[:, None]
    outs = jnp.sum(jnp.where(pick, every, 0), axis=1)
    ordered = jnp.sum(jnp.where(pick, counts, 0), axis=1)
    sizes = jnp.stack([jnp.sum(chosen.astype(jnp.int32)), jnp.sum(counts)])
    spare = jnp.zeros((BATCH,), jnp.int32)
    lists = {
        "sizes": sizes,
        "wanted": wanted,
        "outs": jnp.concatenate([outs, spare]),
        "counts": jnp.concatenate([ordered, spare]),
        "lefts": lefts,
        "rights": rights,
        "owns": owns,
        "flags": flags,
    }
    layout = {}
    first = 0
    for name, values in lists.items():
        layout[name] = first
        first += values.shape[0]
    return jnp.concatenate(list(lists.values())), layout


def per_device(x_blocks, x_cols, out_cols, branch_flag):
    rows, slots = x_cols.shape
    kept = out_cols.shape[1]
    block = x_blocks.shape[-1]
    dtype = x_blocks.dtype
    n_row = lax.axis_size("row")
    n_col = lax.axis_size("col")
    row = lax.axis_index("row")
    col = lax.axis_index("col")
    n_blocks = n_row * rows
    width = n_col * slots
    shape = (rows, kept, block, dtype)

    *packed, facts = pack(x_blocks, x_cols, branch_flag, row * rows)
    facts = lax.all_gather(facts, ("row", "col"), axis=0, tiled=True)
    *packed, facts = lax.optimization_barrier((*packed, facts))
    part_a, part_b, full = packed
    plane = lax.all_gather(full, "row", axis=0)
    facts = facts.reshape(n_row, n_col, rows, 128)
    trace = jnp.sum(facts[:, :, 0, slots]).reshape(1)
    all_cols = facts[..., :slots].astype(jnp.int32)
    all_places = places(all_cols)

    plane_cols = lax.dynamic_index_in_dim(all_cols, col, 1, keepdims=False)
    plane_places = lax.dynamic_index_in_dim(all_places, col, 1, keepdims=False)
    targets = out_cols.reshape(rows * kept)
    right_at = plane_places + STRIDE * jnp.arange(n_row, dtype=jnp.int32)[:, None, None]
    hit = plane_cols.reshape(n_blocks, slots)[None] == targets[:, None, None]
    right_of = jnp.sum(jnp.where(hit, right_at.reshape(n_blocks, slots) + 1, 0), axis=2)
    hit = x_cols[:, None, :] == out_cols[:, :, None]
    owns = jnp.sum(jnp.where(hit, places(x_cols)[:, None, :] + 1, 0), axis=2) - 1
    owns = owns.reshape(rows * kept)

    every = jnp.arange(n_blocks, dtype=jnp.int32)
    line_cols = lax.dynamic_index_in_dim(all_cols, row, 0, keepdims=False)
    line_places = lax.dynamic_index_in_dim(all_places, row, 0, keepdims=False)

    def straight(entries, wanted):
        at = line_places + STRIDE * entries[:, None, None]
        hit = (line_cols[..., None] == every) & wanted[:, None, None, None]
        return jnp.sum(jnp.where(hit, at[..., None] + 1, 0), axis=(0, 2))

    def turned(entry, device, wanted):
        cols = lax.dynamic_slice_in_dim(plane_cols, device, 2, 0)
        at = lax.dynamic_slice_in_dim(plane_places, device, 2, 0)
        at = at + STRIDE * (entry + jnp.arange(2, dtype=jnp.int32)[:, None, None])
        own = row * rows + jnp.arange(rows, dtype=jnp.int32)
        hit = (cols[..., None] == own) & wanted
        found = jnp.sum(jnp.where(hit, at[..., None] + 1, 0), axis=2)
        names = device * rows + jnp.arange(2 * rows, dtype=jnp.int32).reshape(2, rows)
        found = jnp.where(names[:, :, None, None] == every, found[..., None], 0)
        return jnp.sum(found, axis=(0, 1))

    heights = jnp.arange(n_col, dtype=jnp.int32)
    if not (n_col == 4 and n_row == 8):
        line = lax.all_gather(full, "col", axis=0)
        left_of = straight(1 + heights, heights >= 0)
        everything = jnp.ones((rows * kept,), bool)
        one = jnp.ones((1,), jnp.int32)
        table, layout = make_table(left_of, right_of, owns, branch_flag, everything, width, one)
        loads = [(0, None, 0, 0, PACKED, 2)]
        loads += [(1, c, 1 + c, 0, PACKED, 2) for c in range(n_col)]
        purified = multiply(plane, [full, line], tuple(loads), 1 + n_col, layout, table, shape)
        return purified.reshape(rows, kept, block, block), trace

    line = [gather_line(part) for part in (part_a, part_b)]
    at_end = (col == 0) | (col == n_col - 1)
    corner = at_end & (row // 2 == col)
    far = at_end & ~corner
    turn_row = 2 * (n_col - 1 - col)
    wanted = [at_end | True, at_end, ~at_end, far, corner, turn_row]
    wanted = jnp.stack([value.astype(jnp.int32) for value in wanted])
    always, at_ends, inside, at_far, at_corner, turn_at = range(2, 8)

    second = jnp.where(col < 2, 2, 1)
    entries = jnp.where(heights == second, 2, 3)
    entries = jnp.where(heights == jnp.bitwise_xor(col, 1), 1, entries)
    entries = jnp.where(heights == col, 0, entries)
    early = straight(entries, (entries < 3) | ~at_end) + turned(4, turn_row, corner)
    late = straight(entries, (entries == 3) & far)
    meets = (jnp.repeat(late, kept, axis=0) > 0) & (right_of > 0)
    is_late = jnp.any(meets, axis=1)

    arrays = [full]
    loads = [(0, None, 0, 0, PACKED, always)]

    def add(name, entry, wanted):
        spans = ((0, SPLIT), (SPLIT, PACKED - SPLIT))
        for which in range(2):
            loads.append((len(arrays), None, entry) + spans[which] + (wanted,))
            arrays.append(line[which][name])

    def call(left_of, chosen, before=None):
        table, layout = make_table(left_of, right_of, owns, branch_flag, chosen, width, wanted)
        turn = (at_corner, turn_at, 4) if before is None else None
        return multiply(
            plane, list(arrays), tuple(loads), 6, layout, table, shape, turn, before
        )

    add("first", 1, always)
    add("middle", 2, inside)
    add("end_two", 2, at_ends)
    add("middle_two", 3, inside)
    purified = call(early, ~is_late)
    add("end_three", 3, at_far)
    purified = call(early + late, is_late, purified)
    return purified.reshape(rows, kept, block, block), trace


def solution(mesh):
    in_specs = (P("row", "col", None, None), P("row", "col"), P("row", "col"), P("row"))
    out_specs = (P("row", "col", None, None), P())
    return jax.shard_map(
        per_device, mesh=mesh, in_specs=in_specs, out_specs=out_specs, check_vma=False
    )
```

```python
import functools

import jax
import jax.numpy as jnp
from jax import lax
from jax.experimental import pallas as pl
from jax.experimental.pallas import tpu as pltpu
from jax.sharding import PartitionSpec as P

PACKED = 13
SPLIT = (PACKED + 1) // 2
STRIDE = 1 << (PACKED - 1).bit_length()
VMEM_LIMIT = 58 << 20


def pack_kernel(
    cols_ref, flag_ref, first_ref, x_ref, part_a, part_b, full, facts, held, norm, in_sems, sems
):
    count, block, _ = x_ref.shape
    slots = cols_ref.shape[0]
    loads = []
    place = jnp.int32(0)
    for index in range(count):
        filled = cols_ref[index % slots, index // slots] >= 0
        load = pltpu.make_async_copy(x_ref.at[index], held.at[index], in_sems.at[index])
        pl.when(filled)(load.start)
        loads.append((filled, place, load))
        place = place + filled.astype(jnp.int32)
    sends = []
    for index, (filled, place, load) in enumerate(loads):
        pl.when(filled)(load.wait)
        targets = (
            (full, filled, place),
            (part_a, filled & (place < SPLIT), place),
            (part_b, filled & (place >= SPLIT), place - SPLIT),
        )
        for which, (out, wanted, target) in enumerate(targets):
            target = pl.multiple_of(jnp.where(wanted, target, 0) * block, block)
            copy = pltpu.make_async_copy(
                held.at[index], out.at[pl.ds(target, block)], sems.at[which, index]
            )
            pl.when(wanted)(copy.start)
            sends.append((wanted, copy))

    norm[...] = jnp.zeros_like(norm)
    for index in range(count):
        row = index // slots
        col = cols_ref[index % slots, row]
        flag = flag_ref[row]

        @pl.when(col >= 0)
        def _():
            values = held[index].astype(jnp.float32)
            weight = (1 - 2 * flag).astype(jnp.float32)
            norm[...] += weight * jnp.sum(values * values, axis=0, keepdims=True)

        @pl.when((col == first_ref[0] + row) & (flag != 0))
        def _():
            values = held[index].astype(jnp.float32)
            eye = lax.broadcasted_iota(jnp.int32, (block, block), 0)
            eye = eye == lax.broadcasted_iota(jnp.int32, (block, block), 1)
            norm[...] += 2.0 * jnp.sum(jnp.where(eye, values, 0.0), axis=0, keepdims=True)

    across = lax.broadcasted_iota(jnp.int32, facts.shape, 1)
    values = jnp.where(across == count, jnp.sum(norm[...]), 0.0)
    for index in range(count):
        value = cols_ref[index % slots, index // slots].astype(jnp.float32)
        values = jnp.where(across == index, value, values)
    facts[...] = values
    for wanted, copy in sends:
        pl.when(wanted)(copy.wait)


def pack(x_blocks, x_cols, branch_flag, first_row):
    rows, slots, block, _ = x_blocks.shape
    count = rows * slots
    smem = pl.BlockSpec(memory_space=pltpu.SMEM)
    hbm = pl.BlockSpec(memory_space=pltpu.HBM)
    packed = [
        jax.ShapeDtypeStruct((size * block, block), x_blocks.dtype)
        for size in (SPLIT, PACKED - SPLIT, PACKED)
    ]
    return pl.pallas_call(
        pack_kernel,
        out_shape=packed + [jax.ShapeDtypeStruct((1, 128), jnp.float32)],
        in_specs=[smem, smem, smem, hbm],
        out_specs=[hbm] * 3 + [pl.BlockSpec(memory_space=pltpu.VMEM)],
        scratch_shapes=[
            pltpu.VMEM((count, block, block), x_blocks.dtype),
            pltpu.VMEM((1, block), jnp.float32),
            pltpu.SemaphoreType.DMA((count,)),
            pltpu.SemaphoreType.DMA((3, count)),
        ],
        compiler_params=pltpu.CompilerParams(vmem_limit_bytes=VMEM_LIMIT),
    )(x_cols.T, branch_flag, first_row.reshape(1), x_blocks.reshape(count, block, block))


BATCH = 4


def multiply_kernel(loads, kept, layout, turned, table, plane, *refs):
    arrays = refs[: 1 + max(load[0] for load in loads)]
    out_ref, pool, ring, more, done, in_sem, turn_sem, ring_sem, out_sem = refs[-9:]
    depth = ring.shape[0] - 1
    block = out_ref.shape[-1]
    n_out = table[0]
    n_terms = table[1]
    zero_entry = pool.shape[0] - 1

    copies = []
    for number, (which, at, entry, first, size, wanted) in enumerate(loads):
        source = arrays[which] if at is None else arrays[which].at[at]
        copy = pltpu.make_async_copy(
            source.at[pl.ds(0, size * block)],
            pool.at[entry, pl.ds(first * block, size * block)],
            in_sem.at[number],
        )
        copies.append(((table[wanted] != 0) & (n_out > 0), copy))
    for here, copy in copies:
        pl.when(here)(copy.start)

    def decode(index):
        entry = lax.shift_right_logical(index, STRIDE.bit_length() - 1)
        return entry, pl.multiple_of(jnp.bitwise_and(index, STRIDE - 1) * block, block)

    def fetch(term):
        entry, first = decode(table[layout["rights"] + term])
        slot = lax.rem(term, depth)
        return pltpu.make_async_copy(
            plane.at[entry, pl.ds(first, block)], ring.at[slot], ring_sem.at[slot]
        )

    def begin(term, carry):
        fetch(term).start()
        return carry

    if turned is not None:
        is_wanted, at, target = turned
        rows = pltpu.make_async_copy(
            plane.at[pl.ds(table[at], 2)], pool.at[pl.ds(target, 2)], turn_sem
        )
        pl.when(table[is_wanted] != 0)(rows.start)
    lax.fori_loop(0, jnp.minimum(depth, n_terms), begin, 0)
    ring[depth] = jnp.zeros((block, block), ring.dtype)
    pool[zero_entry, pl.ds(0, block)] = jnp.zeros((block, block), pool.dtype)

    if turned is not None:
        @pl.when(table[is_wanted] != 0)
        def _():
            down = lax.broadcasted_iota(jnp.int32, (block, block), 0)
            eye = down == lax.broadcasted_iota(jnp.int32, (block, block), 1)
            eye = eye.astype(jnp.float32).astype(pool.dtype)
            rows.wait()

            def turn(place, carry):
                first = pl.multiple_of(place * block, block)
                for entry in range(target, target + 2):
                    pool[entry, pl.ds(first, block)] = lax.dot_general(
                        eye,
                        pool[entry, pl.ds(first, block)],
                        (((1,), (1,)), ((), ())),
                        preferred_element_type=jnp.float32,
                    ).astype(pool.dtype)
                return carry

            lax.fori_loop(0, PACKED, turn, 0)

    for here, copy in copies:
        pl.when(here)(copy.wait)

    def product(term, live):
        entry, first = decode(
            jnp.where(live, table[layout["lefts"] + term], zero_entry * STRIDE)
        )
        left = pool[entry, pl.ds(first, block)]
        right = ring[jnp.where(live, lax.rem(term, depth), depth)]
        return jnp.dot(left, right, preferred_element_type=jnp.float32)

    def write(number, slot):
        output = table[layout["outs"] + number]
        return pltpu.make_async_copy(done.at[slot], out_ref.at[output], out_sem.at[slot])

    def one_batch(batch, term):
        begins, counts = [], []
        last = term
        for local in range(BATCH):
            begins.append(last)
            counts.append(table[layout["counts"] + batch * BATCH + local])
            last = last + counts[local]

        def arrived(number, carry):
            fetch(number).wait()
            return carry

        lax.fori_loop(term, last, arrived, 0)
        half = lax.rem(batch, 2) * BATCH
        for local in range(BATCH):
            @pl.when(batch >= 2)
            def _():
                write((batch - 2) * BATCH + local, half + local).wait()

            more[local] = jnp.zeros_like(more[local])

            def two_terms(pair, carry):
                number = begins[local] + 2 + 2 * pair
                second = number + 1 < begins[local] + counts[local]
                more[local] += product(number, True) + product(
                    jnp.where(second, number + 1, 0), second
                )
                return carry

            lax.fori_loop(0, (counts[local] - 1) // 2, two_terms, 0)

        for local in range(BATCH):
            output = table[layout["outs"] + batch * BATCH + local]
            square = more[local]
            for place in range(2):
                live = counts[local] > place
                square = square + product(jnp.where(live, begins[local] + place, 0), live)
            flag = table[layout["flags"] + output // kept].astype(jnp.float32)
            own = table[layout["owns"] + output]
            entry, first = decode(jnp.where(own >= 0, own, zero_entry * STRIDE))
            mine = pool[entry, pl.ds(first, block)].astype(jnp.float32)
            result = (2.0 * flag) * mine + (1.0 - 2.0 * flag) * square
            done[half + local] = result.astype(done.dtype)
        for local in range(BATCH):
            @pl.when(batch * BATCH + local < n_out)
            def _():
                write(batch * BATCH + local, half + local).start()

        def refill(number, carry):
            fetch(number + depth).start()
            return carry

        lax.fori_loop(term, jnp.clip(n_terms - depth, term, last), refill, 0)
        return last

    n_batches = (n_out + BATCH - 1) // BATCH
    lax.fori_loop(0, n_batches, one_batch, jnp.int32(0))
    for back in range(2):
        batch = n_batches - 1 - back
        for local in range(BATCH):
            number = jnp.maximum(batch, 0) * BATCH + local

            @pl.when((batch >= 0) & (number < n_out))
            def _():
                write(number, lax.rem(batch, 2) * BATCH + local).wait()


def multiply(plane, arrays, loads, n_entries, layout, table, shape, turned=None, before=None):
    rows, kept, block, dtype = shape
    outputs = rows * kept
    depth = 48
    smem = pl.BlockSpec(memory_space=pltpu.SMEM)
    hbm = pl.BlockSpec(memory_space=pltpu.HBM)
    operands = [table, plane, *arrays]
    aliases = {}
    if before is not None:
        operands.append(before)
        aliases = {len(operands) - 1: 0}
    return pl.pallas_call(
        functools.partial(multiply_kernel, loads, kept, layout, turned),
        out_shape=jax.ShapeDtypeStruct((outputs, block, block), dtype),
        in_specs=[smem] + [hbm] * (len(operands) - 1),
        out_specs=hbm,
        scratch_shapes=[
            pltpu.VMEM((n_entries + 1, PACKED * block, block), dtype),
            pltpu.VMEM((depth + 1, block, block), dtype),
            pltpu.VMEM((BATCH, block, block), jnp.float32),
            pltpu.VMEM((2 * BATCH, block, block), dtype),
            pltpu.SemaphoreType.DMA((len(loads),)),
            pltpu.SemaphoreType.DMA,
            pltpu.SemaphoreType.DMA((depth,)),
            pltpu.SemaphoreType.DMA((2 * BATCH,)),
        ],
        input_output_aliases=aliases,
        compiler_params=pltpu.CompilerParams(vmem_limit_bytes=VMEM_LIMIT),
    )(*operands)


def shift(array, pairs):
    return lax.ppermute(array, "col", pairs)


def gather_line(parts, facts):
    first = [shift(part, [(0, 1), (1, 0), (2, 3), (3, 2)]) for part in parts]
    middle = [shift(part, [(1, 2), (2, 1)]) for part in parts]
    facts = gather_facts(facts)
    first[0], middle[0], facts = lax.optimization_barrier((first[0], middle[0], facts))
    end_two = [shift(part, [(1, 0), (2, 3)]) for part in middle]
    middle_two = [shift(part, [(1, 2), (2, 1)]) for part in first]
    pairs = []
    for row in range(lax.axis_size("row")):
        pairs += [(4 * row + 1, 4 * row)] * (row // 2 != 0)
        pairs += [(4 * row + 2, 4 * row + 3)] * (row // 2 != 3)
    end_three = [lax.ppermute(part, ("row", "col"), pairs) for part in middle_two]
    line = {
        "first": first,
        "middle": middle,
        "end_two": end_two,
        "middle_two": middle_two,
        "end_three": end_three,
    }
    return line, facts


def running_count(fill):
    count = fill.shape[-1]
    before = jnp.arange(count)[:, None] < jnp.arange(count)[None, :]
    return jnp.sum(jnp.where(before, fill[..., :, None], 0), axis=-2)


def places(cols):
    flat = (cols >= 0).astype(jnp.int32).reshape(cols.shape[:-2] + (-1,))
    return running_count(flat).reshape(cols.shape)


def make_table(left_of, right_of, owns, flags, chosen, width, wanted):
    kept = right_of.shape[0] // left_of.shape[0]
    outputs = right_of.shape[0]
    left_of = jnp.repeat(left_of, kept, axis=0)
    live = (left_of > 0) & (right_of > 0) & chosen[:, None]
    counts = jnp.sum(live.astype(jnp.int32), axis=1)
    term = jnp.where(live, running_count(live.astype(jnp.int32)), -1)
    across = jnp.arange(width, dtype=jnp.int32)
    pick = term[:, None, :] == across[:, None]
    lefts = jnp.sum(jnp.where(pick, left_of[:, None, :] - 1, 0), axis=2)
    rights = jnp.sum(jnp.where(pick, right_of[:, None, :] - 1, 0), axis=2)
    flat = jnp.where(across < counts[:, None], running_count(counts)[:, None] + across, -1)
    pick = flat[None] == jnp.arange(PACKED * width, dtype=jnp.int32)[:, None, None]
    lefts = jnp.sum(jnp.where(pick, lefts, 0), axis=(1, 2))
    rights = jnp.sum(jnp.where(pick, rights, 0), axis=(1, 2))
    every = jnp.arange(outputs, dtype=jnp.int32)
    number = jnp.where(chosen, running_count(chosen.astype(jnp.int32)), -1)
    pick = number[None, :] == every[:, None]
    outs = jnp.sum(jnp.where(pick, every, 0), axis=1)
    ordered = jnp.sum(jnp.where(pick, counts, 0), axis=1)
    sizes = jnp.stack([jnp.sum(chosen.astype(jnp.int32)), jnp.sum(counts)])
    spare = jnp.zeros((BATCH,), jnp.int32)
    lists = {
        "sizes": sizes,
        "wanted": wanted,
        "outs": jnp.concatenate([outs, spare]),
        "counts": jnp.concatenate([ordered, spare]),
        "lefts": lefts,
        "rights": rights,
        "owns": owns,
        "flags": flags,
    }
    layout = {}
    first = 0
    for name, values in lists.items():
        layout[name] = first
        first += values.shape[0]
    return jnp.concatenate(list(lists.values())), layout


def gather_facts(facts):
    n_row = lax.axis_size("row")
    n_col = lax.axis_size("col")
    for axis, size in (("row", n_row), ("col", n_col)):
        mask = 1
        while mask < size:
            other = lax.ppermute(facts, axis, [(i, i ^ mask) for i in range(size)])
            facts = jnp.concatenate([facts, other])
            mask *= 2
    step = jnp.arange(n_row * n_col, dtype=jnp.int32)
    row = jnp.bitwise_xor(lax.axis_index("row"), step % n_row)
    col = jnp.bitwise_xor(lax.axis_index("col"), step // n_row)
    hit = (row * n_col + col)[None, :] == step[:, None]
    facts = jnp.sum(jnp.where(hit[..., None], facts, 0.0), axis=1)
    return facts.reshape(n_row, n_col, 128)


def per_device(x_blocks, x_cols, out_cols, branch_flag):
    rows, slots = x_cols.shape
    kept = out_cols.shape[1]
    block = x_blocks.shape[-1]
    dtype = x_blocks.dtype
    n_row = lax.axis_size("row")
    n_col = lax.axis_size("col")
    row = lax.axis_index("row")
    col = lax.axis_index("col")
    n_blocks = n_row * rows
    width = n_col * slots
    shape = (rows, kept, block, dtype)

    part_a, part_b, full, facts = pack(x_blocks, x_cols, branch_flag, row * rows)
    plane = lax.all_gather(full, "row", axis=0)
    tuned = n_col == 4 and n_row == 8
    if tuned:
        line, facts = gather_line((part_a, part_b), facts)
    else:
        line = lax.all_gather(full, "col", axis=0)
        facts = gather_facts(facts)
    trace = jnp.sum(facts[:, :, rows * slots]).reshape(1)
    all_cols = facts[:, :, : rows * slots].astype(jnp.int32).reshape(n_row, n_col, rows, slots)
    all_places = places(all_cols)

    plane_cols = lax.dynamic_index_in_dim(all_cols, col, 1, keepdims=False)
    plane_places = lax.dynamic_index_in_dim(all_places, col, 1, keepdims=False)
    targets = out_cols.reshape(rows * kept)
    right_at = plane_places + STRIDE * jnp.arange(n_row, dtype=jnp.int32)[:, None, None]
    hit = plane_cols.reshape(n_blocks, slots)[None] == targets[:, None, None]
    right_of = jnp.sum(jnp.where(hit, right_at.reshape(n_blocks, slots) + 1, 0), axis=2)
    hit = x_cols[:, None, :] == out_cols[:, :, None]
    owns = jnp.sum(jnp.where(hit, places(x_cols)[:, None, :] + 1, 0), axis=2) - 1
    owns = owns.reshape(rows * kept)

    every = jnp.arange(n_blocks, dtype=jnp.int32)
    line_cols = lax.dynamic_index_in_dim(all_cols, row, 0, keepdims=False)
    line_places = lax.dynamic_index_in_dim(all_places, row, 0, keepdims=False)

    def straight(entries, wanted):
        at = line_places + STRIDE * entries[:, None, None]
        hit = (line_cols[..., None] == every) & wanted[:, None, None, None]
        return jnp.sum(jnp.where(hit, at[..., None] + 1, 0), axis=(0, 2))

    def turned(entry, device, wanted):
        cols = lax.dynamic_slice_in_dim(plane_cols, device, 2, 0)
        at = lax.dynamic_slice_in_dim(plane_places, device, 2, 0)
        at = at + STRIDE * (entry + jnp.arange(2, dtype=jnp.int32)[:, None, None])
        own = row * rows + jnp.arange(rows, dtype=jnp.int32)
        hit = (cols[..., None] == own) & wanted
        found = jnp.sum(jnp.where(hit, at[..., None] + 1, 0), axis=2)
        names = device * rows + jnp.arange(2 * rows, dtype=jnp.int32).reshape(2, rows)
        found = jnp.where(names[:, :, None, None] == every, found[..., None], 0)
        return jnp.sum(found, axis=(0, 1))

    heights = jnp.arange(n_col, dtype=jnp.int32)
    if not tuned:
        left_of = straight(1 + heights, heights >= 0)
        everything = jnp.ones((rows * kept,), bool)
        one = jnp.ones((1,), jnp.int32)
        table, layout = make_table(left_of, right_of, owns, branch_flag, everything, width, one)
        loads = [(0, None, 0, 0, PACKED, 2)]
        loads += [(1, c, 1 + c, 0, PACKED, 2) for c in range(n_col)]
        purified = multiply(plane, [full, line], tuple(loads), 1 + n_col, layout, table, shape)
        return purified.reshape(rows, kept, block, block), trace

    at_end = (col == 0) | (col == n_col - 1)
    corner = at_end & (row // 2 == col)
    far = at_end & ~corner
    turn_row = 2 * (n_col - 1 - col)
    wanted = [at_end | True, at_end, ~at_end, far, corner, turn_row]
    wanted = jnp.stack([value.astype(jnp.int32) for value in wanted])
    always, at_ends, inside, at_far, at_corner, turn_at = range(2, 8)

    second = jnp.where(col < 2, 2, 1)
    entries = jnp.where(heights == second, 2, 3)
    entries = jnp.where(heights == jnp.bitwise_xor(col, 1), 1, entries)
    entries = jnp.where(heights == col, 0, entries)
    early = straight(entries, (entries < 3) | ~at_end) + turned(4, turn_row, corner)
    late = straight(entries, (entries == 3) & far)
    meets = (jnp.repeat(late, kept, axis=0) > 0) & (right_of > 0)
    is_late = jnp.any(meets, axis=1)

    arrays = [full]
    loads = [(0, None, 0, 0, PACKED, always)]

    def add(name, entry, wanted):
        spans = ((0, SPLIT), (SPLIT, PACKED - SPLIT))
        for which in range(2):
            loads.append((len(arrays), None, entry) + spans[which] + (wanted,))
            arrays.append(line[name][which])

    def call(left_of, chosen, before=None):
        table, layout = make_table(left_of, right_of, owns, branch_flag, chosen, width, wanted)
        turn = (at_corner, turn_at, 4) if before is None else None
        return multiply(
            plane, list(arrays), tuple(loads), 6, layout, table, shape, turn, before
        )

    add("first", 1, always)
    add("middle", 2, inside)
    add("end_two", 2, at_ends)
    add("middle_two", 3, inside)
    purified = call(early, ~is_late)
    add("end_three", 3, at_far)
    purified = call(early + late, is_late, purified)
    return purified.reshape(rows, kept, block, block), trace


def solution(mesh):
    in_specs = (P("row", "col", None, None), P("row", "col"), P("row", "col"), P("row"))
    out_specs = (P("row", "col", None, None), P())
    return jax.shard_map(
        per_device, mesh=mesh, in_specs=in_specs, out_specs=out_specs, check_vma=False
    )
```

```python
import functools

import jax
import jax.numpy as jnp
from jax import lax
from jax.experimental import pallas as pl
from jax.experimental.pallas import tpu as pltpu
from jax.sharding import PartitionSpec as P

PACKED = 13
SPLIT = (PACKED + 1) // 2
STRIDE = 1 << (PACKED - 1).bit_length()
VMEM_LIMIT = 58 << 20


def pack_kernel(
    cols_ref, flag_ref, first_ref, x_ref, part_a, part_b, full, facts, held, norm, in_sems, sems
):
    count, block, _ = x_ref.shape
    slots = cols_ref.shape[0]
    loads = []
    place = jnp.int32(0)
    for index in range(count):
        filled = cols_ref[index % slots, index // slots] >= 0
        load = pltpu.make_async_copy(x_ref.at[index], held.at[index], in_sems.at[index])
        pl.when(filled)(load.start)
        loads.append((filled, place, load))
        place = place + filled.astype(jnp.int32)
    sends = []
    for index, (filled, place, load) in enumerate(loads):
        pl.when(filled)(load.wait)
        targets = (
            (full, filled, place),
            (part_a, filled & (place < SPLIT), place),
            (part_b, filled & (place >= SPLIT), place - SPLIT),
        )
        for which, (out, wanted, target) in enumerate(targets):
            target = pl.multiple_of(jnp.where(wanted, target, 0) * block, block)
            copy = pltpu.make_async_copy(
                held.at[index], out.at[pl.ds(target, block)], sems.at[which, index]
            )
            pl.when(wanted)(copy.start)
            sends.append((wanted, copy))

    norm[...] = jnp.zeros_like(norm)
    for index in range(count):
        row = index // slots
        col = cols_ref[index % slots, row]
        flag = flag_ref[row]

        @pl.when(col >= 0)
        def _():
            values = held[index].astype(jnp.float32)
            weight = (1 - 2 * flag).astype(jnp.float32)
            norm[...] += weight * jnp.sum(values * values, axis=0, keepdims=True)

        @pl.when((col == first_ref[0] + row) & (flag != 0))
        def _():
            values = held[index].astype(jnp.float32)
            eye = lax.broadcasted_iota(jnp.int32, (block, block), 0)
            eye = eye == lax.broadcasted_iota(jnp.int32, (block, block), 1)
            norm[...] += 2.0 * jnp.sum(jnp.where(eye, values, 0.0), axis=0, keepdims=True)

    across = lax.broadcasted_iota(jnp.int32, facts.shape, 1)
    values = jnp.where(across == count, jnp.sum(norm[...]), 0.0)
    for index in range(count):
        value = cols_ref[index % slots, index // slots].astype(jnp.float32)
        values = jnp.where(across == index, value, values)
    facts[...] = values
    for wanted, copy in sends:
        pl.when(wanted)(copy.wait)


def pack(x_blocks, x_cols, branch_flag, first_row):
    rows, slots, block, _ = x_blocks.shape
    count = rows * slots
    smem = pl.BlockSpec(memory_space=pltpu.SMEM)
    hbm = pl.BlockSpec(memory_space=pltpu.HBM)
    packed = [
        jax.ShapeDtypeStruct((size * block, block), x_blocks.dtype)
        for size in (SPLIT, PACKED - SPLIT, PACKED)
    ]
    return pl.pallas_call(
        pack_kernel,
        out_shape=packed + [jax.ShapeDtypeStruct((1, 128), jnp.float32)],
        in_specs=[smem, smem, smem, hbm],
        out_specs=[hbm] * 3 + [pl.BlockSpec(memory_space=pltpu.VMEM)],
        scratch_shapes=[
            pltpu.VMEM((count, block, block), x_blocks.dtype),
            pltpu.VMEM((1, block), jnp.float32),
            pltpu.SemaphoreType.DMA((count,)),
            pltpu.SemaphoreType.DMA((3, count)),
        ],
        compiler_params=pltpu.CompilerParams(vmem_limit_bytes=VMEM_LIMIT),
    )(x_cols.T, branch_flag, first_row.reshape(1), x_blocks.reshape(count, block, block))


BATCH = 4


def multiply_kernel(loads, kept, layout, turned, table, plane, *refs):
    arrays = refs[: 1 + max(load[0] for load in loads)]
    out_ref, pool, ring, more, done, in_sem, turn_sem, ring_sem, out_sem = refs[-9:]
    depth = ring.shape[0] - 1
    block = out_ref.shape[-1]
    n_out = table[0]
    n_terms = table[1]
    zero_entry = pool.shape[0] - 1

    copies = []
    for number, (which, at, entry, first, size, wanted) in enumerate(loads):
        source = arrays[which] if at is None else arrays[which].at[at]
        copy = pltpu.make_async_copy(
            source.at[pl.ds(0, size * block)],
            pool.at[entry, pl.ds(first * block, size * block)],
            in_sem.at[number],
        )
        copies.append(((table[wanted] != 0) & (n_out > 0), copy))
    for here, copy in copies:
        pl.when(here)(copy.start)

    def decode(index):
        entry = lax.shift_right_logical(index, STRIDE.bit_length() - 1)
        return entry, pl.multiple_of(jnp.bitwise_and(index, STRIDE - 1) * block, block)

    def fetch(term):
        entry, first = decode(table[layout["rights"] + term])
        slot = lax.rem(term, depth)
        return pltpu.make_async_copy(
            plane.at[entry, pl.ds(first, block)], ring.at[slot], ring_sem.at[slot]
        )

    def begin(term, carry):
        fetch(term).start()
        return carry

    if turned is not None:
        is_wanted, at, target, n_turn = turned
        rows = pltpu.make_async_copy(
            plane.at[pl.ds(table[at], n_turn)], pool.at[pl.ds(target, n_turn)], turn_sem
        )
        pl.when(table[is_wanted] != 0)(rows.start)
    lax.fori_loop(0, jnp.minimum(depth, n_terms), begin, 0)
    ring[depth] = jnp.zeros((block, block), ring.dtype)
    pool[zero_entry, pl.ds(0, block)] = jnp.zeros((block, block), pool.dtype)

    if turned is not None:
        @pl.when(table[is_wanted] != 0)
        def _():
            down = lax.broadcasted_iota(jnp.int32, (block, block), 0)
            eye = down == lax.broadcasted_iota(jnp.int32, (block, block), 1)
            eye = eye.astype(jnp.float32).astype(pool.dtype)
            rows.wait()

            def turn(place, carry):
                first = pl.multiple_of(place * block, block)
                for entry in range(n_turn):
                    @pl.when(table[layout["turn"] + entry * PACKED + place] != 0)
                    def _():
                        pool[target + entry, pl.ds(first, block)] = lax.dot_general(
                            eye,
                            pool[target + entry, pl.ds(first, block)],
                            (((1,), (1,)), ((), ())),
                            preferred_element_type=jnp.float32,
                        ).astype(pool.dtype)

                return carry

            lax.fori_loop(0, PACKED, turn, 0)

    for here, copy in copies:
        pl.when(here)(copy.wait)

    def product(term, live):
        entry, first = decode(
            jnp.where(live, table[layout["lefts"] + term], zero_entry * STRIDE)
        )
        left = pool[entry, pl.ds(first, block)]
        right = ring[jnp.where(live, lax.rem(term, depth), depth)]
        return jnp.dot(left, right, preferred_element_type=jnp.float32)

    def write(number, slot):
        output = table[layout["outs"] + number]
        return pltpu.make_async_copy(done.at[slot], out_ref.at[output], out_sem.at[slot])

    def one_batch(batch, term):
        begins, counts = [], []
        last = term
        for local in range(BATCH):
            begins.append(last)
            counts.append(table[layout["counts"] + batch * BATCH + local])
            last = last + counts[local]

        def arrived(number, carry):
            fetch(number).wait()
            return carry

        lax.fori_loop(term, last, arrived, 0)
        half = lax.rem(batch, 2) * BATCH
        for local in range(BATCH):
            @pl.when(batch >= 2)
            def _():
                write((batch - 2) * BATCH + local, half + local).wait()

            more[local] = jnp.zeros_like(more[local])

            def two_terms(pair, carry):
                number = begins[local] + 2 + 2 * pair
                second = number + 1 < begins[local] + counts[local]
                more[local] += product(number, True) + product(
                    jnp.where(second, number + 1, 0), second
                )
                return carry

            lax.fori_loop(0, (counts[local] - 1) // 2, two_terms, 0)

        for local in range(BATCH):
            output = table[layout["outs"] + batch * BATCH + local]
            square = more[local]
            for place in range(2):
                live = counts[local] > place
                square = square + product(jnp.where(live, begins[local] + place, 0), live)
            flag = table[layout["flags"] + output // kept].astype(jnp.float32)
            own = table[layout["owns"] + output]
            entry, first = decode(jnp.where(own >= 0, own, zero_entry * STRIDE))
            mine = pool[entry, pl.ds(first, block)].astype(jnp.float32)
            result = (2.0 * flag) * mine + (1.0 - 2.0 * flag) * square
            done[half + local] = result.astype(done.dtype)
        for local in range(BATCH):
            @pl.when(batch * BATCH + local < n_out)
            def _():
                write(batch * BATCH + local, half + local).start()

        def refill(number, carry):
            fetch(number + depth).start()
            return carry

        lax.fori_loop(term, jnp.clip(n_terms - depth, term, last), refill, 0)
        return last

    n_batches = (n_out + BATCH - 1) // BATCH
    lax.fori_loop(0, n_batches, one_batch, jnp.int32(0))
    for back in range(2):
        batch = n_batches - 1 - back
        for local in range(BATCH):
            number = jnp.maximum(batch, 0) * BATCH + local

            @pl.when((batch >= 0) & (number < n_out))
            def _():
                write(number, lax.rem(batch, 2) * BATCH + local).wait()


def multiply(plane, arrays, loads, n_entries, layout, table, shape, turned=None, before=None):
    rows, kept, block, dtype = shape
    outputs = rows * kept
    depth = 48
    smem = pl.BlockSpec(memory_space=pltpu.SMEM)
    hbm = pl.BlockSpec(memory_space=pltpu.HBM)
    operands = [table, plane, *arrays]
    aliases = {}
    if before is not None:
        operands.append(before)
        aliases = {len(operands) - 1: 0}
    return pl.pallas_call(
        functools.partial(multiply_kernel, loads, kept, layout, turned),
        out_shape=jax.ShapeDtypeStruct((outputs, block, block), dtype),
        in_specs=[smem] + [hbm] * (len(operands) - 1),
        out_specs=hbm,
        scratch_shapes=[
            pltpu.VMEM((n_entries + 1, PACKED * block, block), dtype),
            pltpu.VMEM((depth + 1, block, block), dtype),
            pltpu.VMEM((BATCH, block, block), jnp.float32),
            pltpu.VMEM((2 * BATCH, block, block), dtype),
            pltpu.SemaphoreType.DMA((len(loads),)),
            pltpu.SemaphoreType.DMA,
            pltpu.SemaphoreType.DMA((depth,)),
            pltpu.SemaphoreType.DMA((2 * BATCH,)),
        ],
        input_output_aliases=aliases,
        compiler_params=pltpu.CompilerParams(vmem_limit_bytes=VMEM_LIMIT),
    )(*operands)


def shift(array, pairs):
    return lax.ppermute(array, "col", pairs)


def send(array, moves):
    pairs = []
    for (q, c), (q_to, c_to) in list(moves):
        for core in range(2):
            pairs.append((4 * (2 * q + core) + c, 4 * (2 * q_to + core) + c_to))
            pairs.append((4 * (7 - 2 * q - core) + 3 - c, 4 * (7 - 2 * q_to - core) + 3 - c_to))
    return lax.ppermute(array, ("row", "col"), sorted(set(pairs)))


def after(array, *others):
    return lax.optimization_barrier((array, *others))[0]


def gather_line(parts, facts):
    part_a, part_b = parts
    lines = range(4)
    down = [((q, 3), (q, 2)) for q in lines]
    inner = [((q, 2), (q, 1)) for q in lines]
    ends = [((q, 1), (q, 0)) for q in lines]
    first_a = send(part_a, down + ends)
    middle_a = send(part_a, inner)
    over = [send(part_b, [((q, 1), (0, 0))]) for q in (1, 2, 3)]
    facts = gather_facts(facts, ("row",))
    first_a, middle_a, part_b, facts = lax.optimization_barrier(
        (first_a, middle_a, part_b, facts)
    )
    middle_b = send(part_b, inner)
    first_b = send(part_b, down + ends[:1])
    end_two_a = send(middle_a, ends[1:])
    middle_two_a = send(after(first_a, middle_b, end_two_a), inner)
    end_two_b = send(middle_b, ends[1:])
    middle_two_b = send(after(first_b, middle_two_a, end_two_b), inner)
    end_three_a = send(middle_two_a, ends[1:])
    end_three_b = send(after(middle_two_b, end_three_a), ends[1:])
    over = [after(array, end_two_b) for array in over]
    line = {
        "first": (first_a, first_b),
        "middle": (middle_a, middle_b),
        "end_two": (end_two_a, end_two_b),
        "middle_two": (middle_two_a, middle_two_b),
        "end_three": (end_three_a, end_three_b),
        "round": [send(over[q - 1], [((0, 0), (q, 0))]) for q in (1, 2, 3)],
    }
    return line, facts


def running_count(fill):
    count = fill.shape[-1]
    before = jnp.arange(count)[:, None] < jnp.arange(count)[None, :]
    return jnp.sum(jnp.where(before, fill[..., :, None], 0), axis=-2)


def places(cols):
    flat = (cols >= 0).astype(jnp.int32).reshape(cols.shape[:-2] + (-1,))
    return running_count(flat).reshape(cols.shape)


def make_table(left_of, right_of, owns, flags, chosen, width, wanted, turn=None):
    kept = right_of.shape[0] // left_of.shape[0]
    outputs = right_of.shape[0]
    left_of = jnp.repeat(left_of, kept, axis=0)
    live = (left_of > 0) & (right_of > 0) & chosen[:, None]
    counts = jnp.sum(live.astype(jnp.int32), axis=1)
    term = jnp.where(live, running_count(live.astype(jnp.int32)), -1)
    across = jnp.arange(width, dtype=jnp.int32)
    pick = term[:, None, :] == across[:, None]
    lefts = jnp.sum(jnp.where(pick, left_of[:, None, :] - 1, 0), axis=2)
    rights = jnp.sum(jnp.where(pick, right_of[:, None, :] - 1, 0), axis=2)
    flat = jnp.where(across < counts[:, None], running_count(counts)[:, None] + across, -1)
    pick = flat[None] == jnp.arange(PACKED * width, dtype=jnp.int32)[:, None, None]
    lefts = jnp.sum(jnp.where(pick, lefts, 0), axis=(1, 2))
    rights = jnp.sum(jnp.where(pick, rights, 0), axis=(1, 2))
    every = jnp.arange(outputs, dtype=jnp.int32)
    number = jnp.where(chosen, running_count(chosen.astype(jnp.int32)), -1)
    pick = number[None, :] == every[:, None]
    outs = jnp.sum(jnp.where(pick, every, 0), axis=1)
    ordered = jnp.sum(jnp.where(pick, counts, 0), axis=1)
    sizes = jnp.stack([jnp.sum(chosen.astype(jnp.int32)), jnp.sum(counts)])
    spare = jnp.zeros((BATCH,), jnp.int32)
    lists = {
        "sizes": sizes,
        "wanted": wanted,
        "outs": jnp.concatenate([outs, spare]),
        "counts": jnp.concatenate([ordered, spare]),
        "lefts": lefts,
        "rights": rights,
        "owns": owns,
        "flags": flags,
    }
    if turn is not None:
        lists["turn"] = turn
    layout = {}
    first = 0
    for name, values in lists.items():
        layout[name] = first
        first += values.shape[0]
    return jnp.concatenate(list(lists.values())), layout


def gather_facts(facts, axes):
    places = jnp.zeros((1,), jnp.int32)
    own = jnp.int32(0)
    known = 1
    for axis in axes:
        size = lax.axis_size(axis)
        own = own * size + lax.axis_index(axis)
        known *= size
    stride = known
    for axis in axes:
        size = lax.axis_size(axis)
        stride //= size
        mask = 1
        while mask < size:
            other = lax.ppermute(facts, axis, [(i, i ^ mask) for i in range(size)])
            facts = jnp.concatenate([facts, other])
            places = jnp.concatenate([places, places + mask * stride])
            mask *= 2
    hit = jnp.bitwise_xor(own, places)[None, :] == jnp.arange(known, dtype=jnp.int32)[:, None]
    return jnp.sum(jnp.where(hit[..., None], facts, 0.0), axis=1)


def per_device(x_blocks, x_cols, out_cols, branch_flag):
    rows, slots = x_cols.shape
    kept = out_cols.shape[1]
    block = x_blocks.shape[-1]
    dtype = x_blocks.dtype
    n_row = lax.axis_size("row")
    n_col = lax.axis_size("col")
    row = lax.axis_index("row")
    col = lax.axis_index("col")
    n_blocks = n_row * rows
    width = n_col * slots
    shape = (rows, kept, block, dtype)

    count = rows * slots
    tuned = n_col == 4 and n_row == 8
    if tuned:
        part_a, part_b, full, facts = pack(x_blocks, x_cols, branch_flag, row * rows)
        plane = lax.all_gather(full, "row", axis=0)
        near, far_one, far_two = [
            shift(facts, [(i, i ^ step) for i in range(n_col)]) for step in range(1, n_col)
        ]
        line_cols = jnp.concatenate([facts, near, far_one, far_two])
        total = (facts + near) + (far_one + far_two)
        facts = jnp.where(jnp.arange(128) < count, facts, total)
        line, facts = gather_line((part_a, part_b), facts)
        trace = jnp.sum(facts[:, count]).reshape(1)
    else:
        part_a, part_b, full, facts = pack(x_blocks, x_cols, branch_flag, row * rows)
        plane = lax.all_gather(full, "row", axis=0)
        line = lax.all_gather(full, "col", axis=0)
        every_fact = gather_facts(facts, ("row", "col")).reshape(n_row, n_col, 128)
        trace = jnp.sum(every_fact[:, :, count]).reshape(1)
        facts = lax.dynamic_index_in_dim(every_fact, col, 1, keepdims=False)
        line_cols = lax.dynamic_index_in_dim(every_fact, row, 0, keepdims=False)

    def slots_of(facts):
        cols = facts[:, :count].astype(jnp.int32).reshape(facts.shape[0], rows, slots)
        return cols, places(cols)

    plane_cols, plane_places = slots_of(facts)
    targets = out_cols.reshape(rows * kept)
    right_at = plane_places + STRIDE * jnp.arange(n_row, dtype=jnp.int32)[:, None, None]
    hit = plane_cols.reshape(n_blocks, slots)[None] == targets[:, None, None]
    right_of = jnp.sum(jnp.where(hit, right_at.reshape(n_blocks, slots) + 1, 0), axis=2)
    hit = x_cols[:, None, :] == out_cols[:, :, None]
    owns = jnp.sum(jnp.where(hit, places(x_cols)[:, None, :] + 1, 0), axis=2) - 1
    owns = owns.reshape(rows * kept)

    every = jnp.arange(n_blocks, dtype=jnp.int32)
    line_cols, line_places = slots_of(line_cols)

    def straight(entries, wanted):
        at = line_places + STRIDE * entries[:, None, None]
        hit = (line_cols[..., None] == every) & wanted[:, None, None, None]
        return jnp.sum(jnp.where(hit, at[..., None] + 1, 0), axis=(0, 2))

    def turned(entry, device, size, wanted):
        cols = lax.dynamic_slice_in_dim(plane_cols, device, size, 0)
        place = lax.dynamic_slice_in_dim(plane_places, device, size, 0)
        at = place + STRIDE * (entry + jnp.arange(size, dtype=jnp.int32)[:, None, None])
        own = row * rows + jnp.arange(rows, dtype=jnp.int32)
        hit = (cols[..., None] == own) & wanted
        found = jnp.sum(jnp.where(hit, at[..., None] + 1, 0), axis=2)
        names = device * rows + jnp.arange(size * rows, dtype=jnp.int32).reshape(size, rows)
        found = jnp.where(names[:, :, None, None] == every, found[..., None], 0)
        marks = jnp.any(hit, axis=3)[..., None] & (
            place[..., None] == jnp.arange(PACKED, dtype=jnp.int32)
        )
        marks = jnp.any(marks, axis=(1, 2)).astype(jnp.int32)
        return jnp.sum(found, axis=(0, 1)), marks.reshape(size * PACKED)

    heights = jnp.arange(n_col, dtype=jnp.int32)
    if not tuned:
        left_of = straight(1 + heights, heights >= 0)
        everything = jnp.ones((rows * kept,), bool)
        one = jnp.ones((1,), jnp.int32)
        table, layout = make_table(left_of, right_of, owns, branch_flag, everything, width, one)
        loads = [(0, None, 0, 0, PACKED, 2)]
        loads += [(1, c, 1 + c, 0, PACKED, 2) for c in range(n_col)]
        purified = multiply(plane, [full, line], tuple(loads), 1 + n_col, layout, table, shape)
        return purified.reshape(rows, kept, block, block), trace

    at_end = (col == 0) | (col == n_col - 1)
    pair = row // 2
    corner = at_end & (pair == col)
    far = at_end & ~corner
    from_corner = jnp.where(col == 0, pair, 3 - pair)
    turn_row = jnp.where(col == 0, 4, 0)
    wanted = [at_end | True, ~far, ~at_end, far, corner, turn_row]
    wanted += [far & (from_corner == q) for q in (1, 2, 3)]
    wanted = jnp.stack([value.astype(jnp.int32) for value in wanted])
    always, not_far, inside, at_far, at_corner, turn_at = range(2, 8)
    rounds = (8, 9, 10)

    entries = jnp.where(at_end, jnp.array([0, 1, 2, 3]), jnp.array([0, 1, 3, 2]))
    entries = entries.astype(jnp.int32)
    early = straight(entries, (entries < 2) | ((entries == 2) & ~corner) | ~at_end)
    from_plane, marks = turned(4, turn_row, 4, corner)
    early = early + from_plane
    late = straight(entries, (entries == 3) & far)
    meets = (jnp.repeat(late, kept, axis=0) > 0) & (right_of > 0)
    is_late = jnp.any(meets, axis=1)

    arrays = [full]
    loads = [(0, None, 0, 0, PACKED, always)]
    spans = ((0, SPLIT), (SPLIT, PACKED - SPLIT))

    def add(array, entry, which, wanted):
        loads.append((len(arrays), None, entry) + spans[which] + (wanted,))
        arrays.append(array)

    def call(left_of, chosen, before=None):
        turn = marks if before is None else None
        table, layout = make_table(
            left_of, right_of, owns, branch_flag, chosen, width, wanted, turn
        )
        turn = (at_corner, turn_at, 4, 4) if before is None else None
        n_entries = 8 if before is None else 4
        return multiply(
            plane, list(arrays), tuple(loads), n_entries, layout, table, shape, turn, before
        )

    add(line["first"][0], 1, 0, always)
    add(line["first"][1], 1, 1, not_far)
    for array, flag in zip(line["round"], rounds):
        add(array, 1, 1, flag)
    for name, entry, flag in (("middle", 2, inside), ("end_two", 2, at_far), ("middle_two", 3, inside)):
        for which in range(2):
            add(line[name][which], entry, which, flag)
    purified = call(early, ~is_late)
    for which in range(2):
        add(line["end_three"][which], 3, which, at_far)
    purified, trace = lax.optimization_barrier((purified, trace))
    purified = call(early + late, is_late, purified)
    return purified.reshape(rows, kept, block, block), trace


def solution(mesh):
    in_specs = (P("row", "col", None, None), P("row", "col"), P("row", "col"), P("row"))
    out_specs = (P("row", "col", None, None), P())
    return jax.shard_map(
        per_device, mesh=mesh, in_specs=in_specs, out_specs=out_specs, check_vma=False
    )
```

```python
import functools

import jax
import jax.numpy as jnp
from jax import lax
from jax.experimental import pallas as pl
from jax.experimental.pallas import tpu as pltpu
from jax.sharding import PartitionSpec as P

PACKED = 13
SPLIT = (PACKED + 1) // 2
STRIDE = 1 << (PACKED - 1).bit_length()
VMEM_LIMIT = 58 << 20


def pack_kernel(
    cols_ref, flag_ref, first_ref, x_ref, part_a, part_b, full, facts, held, norm, in_sems, sems
):
    count, block, _ = x_ref.shape
    slots = cols_ref.shape[0]
    loads = []
    place = jnp.int32(0)
    for index in range(count):
        filled = cols_ref[index % slots, index // slots] >= 0
        load = pltpu.make_async_copy(x_ref.at[index], held.at[index], in_sems.at[index])
        pl.when(filled)(load.start)
        loads.append((filled, place, load))
        place = place + filled.astype(jnp.int32)
    sends = []
    for index, (filled, place, load) in enumerate(loads):
        pl.when(filled)(load.wait)
        targets = (
            (full, filled, place),
            (part_a, filled & (place < SPLIT), place),
            (part_b, filled & (place >= SPLIT), place - SPLIT),
        )
        for which, (out, wanted, target) in enumerate(targets):
            target = pl.multiple_of(jnp.where(wanted, target, 0) * block, block)
            copy = pltpu.make_async_copy(
                held.at[index], out.at[pl.ds(target, block)], sems.at[which, index]
            )
            pl.when(wanted)(copy.start)
            sends.append((wanted, copy))

    norm[...] = jnp.zeros_like(norm)
    for index in range(count):
        row = index // slots
        col = cols_ref[index % slots, row]
        flag = flag_ref[row]

        @pl.when(col >= 0)
        def _():
            values = held[index].astype(jnp.float32)
            weight = (1 - 2 * flag).astype(jnp.float32)
            norm[...] += weight * jnp.sum(values * values, axis=0, keepdims=True)

        @pl.when((col == first_ref[0] + row) & (flag != 0))
        def _():
            values = held[index].astype(jnp.float32)
            eye = lax.broadcasted_iota(jnp.int32, (block, block), 0)
            eye = eye == lax.broadcasted_iota(jnp.int32, (block, block), 1)
            norm[...] += 2.0 * jnp.sum(jnp.where(eye, values, 0.0), axis=0, keepdims=True)

    across = lax.broadcasted_iota(jnp.int32, facts.shape, 1)
    values = jnp.where(across == count, jnp.sum(norm[...]), 0.0)
    for index in range(count):
        value = cols_ref[index % slots, index // slots].astype(jnp.float32)
        values = jnp.where(across == index, value, values)
    facts[...] = values
    for wanted, copy in sends:
        pl.when(wanted)(copy.wait)


def pack(x_blocks, x_cols, branch_flag, first_row):
    rows, slots, block, _ = x_blocks.shape
    count = rows * slots
    smem = pl.BlockSpec(memory_space=pltpu.SMEM)
    hbm = pl.BlockSpec(memory_space=pltpu.HBM)
    packed = [
        jax.ShapeDtypeStruct((size * block, block), x_blocks.dtype)
        for size in (SPLIT, PACKED - SPLIT, PACKED)
    ]
    return pl.pallas_call(
        pack_kernel,
        out_shape=packed + [jax.ShapeDtypeStruct((1, 128), jnp.float32)],
        in_specs=[smem, smem, smem, hbm],
        out_specs=[hbm] * 3 + [pl.BlockSpec(memory_space=pltpu.VMEM)],
        scratch_shapes=[
            pltpu.VMEM((count, block, block), x_blocks.dtype),
            pltpu.VMEM((1, block), jnp.float32),
            pltpu.SemaphoreType.DMA((count,)),
            pltpu.SemaphoreType.DMA((3, count)),
        ],
        compiler_params=pltpu.CompilerParams(vmem_limit_bytes=VMEM_LIMIT),
    )(x_cols.T, branch_flag, first_row.reshape(1), x_blocks.reshape(count, block, block))


BATCH = 4


def multiply_kernel(loads, kept, layout, turned, table, plane, *refs):
    arrays = refs[: 1 + max(load[0] for load in loads)]
    out_ref, pool, ring, more, done, in_sem, turn_sem, ring_sem, out_sem = refs[-9:]
    depth = ring.shape[0] - 1
    block = out_ref.shape[-1]
    n_out = table[0]
    n_terms = table[1]
    zero_entry = pool.shape[0] - 1

    copies = []
    for number, (which, at, entry, first, size, wanted) in enumerate(loads):
        source = arrays[which] if at is None else arrays[which].at[at]
        copy = pltpu.make_async_copy(
            source.at[pl.ds(0, size * block)],
            pool.at[entry, pl.ds(first * block, size * block)],
            in_sem.at[number],
        )
        copies.append(((table[wanted] != 0) & (n_out > 0), copy))
    for here, copy in copies:
        pl.when(here)(copy.start)

    def decode(index):
        entry = lax.shift_right_logical(index, STRIDE.bit_length() - 1)
        return entry, pl.multiple_of(jnp.bitwise_and(index, STRIDE - 1) * block, block)

    def fetch(term):
        entry, first = decode(table[layout["rights"] + term])
        slot = lax.rem(term, depth)
        return pltpu.make_async_copy(
            plane.at[entry, pl.ds(first, block)], ring.at[slot], ring_sem.at[slot]
        )

    def begin(term, carry):
        fetch(term).start()
        return carry

    if turned is not None:
        is_wanted, at, target, n_turn = turned
        rows = pltpu.make_async_copy(
            plane.at[pl.ds(table[at], n_turn)], pool.at[pl.ds(target, n_turn)], turn_sem
        )
        pl.when(table[is_wanted] != 0)(rows.start)
    lax.fori_loop(0, jnp.minimum(depth, n_terms), begin, 0)
    ring[depth] = jnp.zeros((block, block), ring.dtype)
    pool[zero_entry, pl.ds(0, block)] = jnp.zeros((block, block), pool.dtype)

    if turned is not None:
        @pl.when(table[is_wanted] != 0)
        def _():
            down = lax.broadcasted_iota(jnp.int32, (block, block), 0)
            eye = down == lax.broadcasted_iota(jnp.int32, (block, block), 1)
            eye = eye.astype(jnp.float32).astype(pool.dtype)
            rows.wait()

            def turn(place, carry):
                first = pl.multiple_of(place * block, block)
                for entry in range(n_turn):
                    @pl.when(table[layout["turn"] + entry * PACKED + place] != 0)
                    def _():
                        pool[target + entry, pl.ds(first, block)] = lax.dot_general(
                            eye,
                            pool[target + entry, pl.ds(first, block)],
                            (((1,), (1,)), ((), ())),
                            preferred_element_type=jnp.float32,
                        ).astype(pool.dtype)

                return carry

            lax.fori_loop(0, PACKED, turn, 0)

    for here, copy in copies:
        pl.when(here)(copy.wait)

    def product(term, live):
        entry, first = decode(
            jnp.where(live, table[layout["lefts"] + term], zero_entry * STRIDE)
        )
        left = pool[entry, pl.ds(first, block)]
        right = ring[jnp.where(live, lax.rem(term, depth), depth)]
        return jnp.dot(left, right, preferred_element_type=jnp.float32)

    def write(number, slot):
        output = table[layout["outs"] + number]
        return pltpu.make_async_copy(done.at[slot], out_ref.at[output], out_sem.at[slot])

    def one_batch(batch, term):
        begins, counts = [], []
        last = term
        for local in range(BATCH):
            begins.append(last)
            counts.append(table[layout["counts"] + batch * BATCH + local])
            last = last + counts[local]

        def arrived(number, carry):
            fetch(number).wait()
            return carry

        lax.fori_loop(term, last, arrived, 0)
        half = lax.rem(batch, 2) * BATCH
        for local in range(BATCH):
            @pl.when(batch >= 2)
            def _():
                write((batch - 2) * BATCH + local, half + local).wait()

            more[local] = jnp.zeros_like(more[local])

            def two_terms(pair, carry):
                number = begins[local] + 2 + 2 * pair
                second = number + 1 < begins[local] + counts[local]
                more[local] += product(number, True) + product(
                    jnp.where(second, number + 1, 0), second
                )
                return carry

            lax.fori_loop(0, (counts[local] - 1) // 2, two_terms, 0)

        for local in range(BATCH):
            output = table[layout["outs"] + batch * BATCH + local]
            square = more[local]
            for place in range(2):
                live = counts[local] > place
                square = square + product(jnp.where(live, begins[local] + place, 0), live)
            flag = table[layout["flags"] + output // kept].astype(jnp.float32)
            own = table[layout["owns"] + output]
            entry, first = decode(jnp.where(own >= 0, own, zero_entry * STRIDE))
            mine = pool[entry, pl.ds(first, block)].astype(jnp.float32)
            result = (2.0 * flag) * mine + (1.0 - 2.0 * flag) * square
            done[half + local] = result.astype(done.dtype)
        for local in range(BATCH):
            @pl.when(batch * BATCH + local < n_out)
            def _():
                write(batch * BATCH + local, half + local).start()

        def refill(number, carry):
            fetch(number + depth).start()
            return carry

        lax.fori_loop(term, jnp.clip(n_terms - depth, term, last), refill, 0)
        return last

    n_batches = (n_out + BATCH - 1) // BATCH
    lax.fori_loop(0, n_batches, one_batch, jnp.int32(0))
    for back in range(2):
        batch = n_batches - 1 - back
        for local in range(BATCH):
            number = jnp.maximum(batch, 0) * BATCH + local

            @pl.when((batch >= 0) & (number < n_out))
            def _():
                write(number, lax.rem(batch, 2) * BATCH + local).wait()


def multiply(plane, arrays, loads, n_entries, layout, table, shape, turned=None, before=None):
    rows, kept, block, dtype = shape
    outputs = rows * kept
    depth = 48
    smem = pl.BlockSpec(memory_space=pltpu.SMEM)
    hbm = pl.BlockSpec(memory_space=pltpu.HBM)
    operands = [table, plane, *arrays]
    aliases = {}
    if before is not None:
        operands.append(before)
        aliases = {len(operands) - 1: 0}
    return pl.pallas_call(
        functools.partial(multiply_kernel, loads, kept, layout, turned),
        out_shape=jax.ShapeDtypeStruct((outputs, block, block), dtype),
        in_specs=[smem] + [hbm] * (len(operands) - 1),
        out_specs=hbm,
        scratch_shapes=[
            pltpu.VMEM((n_entries + 1, PACKED * block, block), dtype),
            pltpu.VMEM((depth + 1, block, block), dtype),
            pltpu.VMEM((BATCH, block, block), jnp.float32),
            pltpu.VMEM((2 * BATCH, block, block), dtype),
            pltpu.SemaphoreType.DMA((len(loads),)),
            pltpu.SemaphoreType.DMA,
            pltpu.SemaphoreType.DMA((depth,)),
            pltpu.SemaphoreType.DMA((2 * BATCH,)),
        ],
        input_output_aliases=aliases,
        compiler_params=pltpu.CompilerParams(vmem_limit_bytes=VMEM_LIMIT),
    )(*operands)


def shift(array, pairs):
    return lax.ppermute(array, "col", pairs)


def gather_line(parts, facts):
    first = [shift(part, [(0, 1), (1, 0), (2, 3), (3, 2)]) for part in parts]
    middle = [shift(part, [(1, 2), (2, 1)]) for part in parts]
    facts = gather_facts(facts, ("row",))
    first[0], middle[0], facts = lax.optimization_barrier((first[0], middle[0], facts))
    end_two = [shift(part, [(1, 0), (2, 3)]) for part in middle]
    middle_two = [shift(part, [(1, 2), (2, 1)]) for part in first]
    pairs = []
    for row in range(lax.axis_size("row")):
        pairs += [(4 * row + 1, 4 * row)] * (row // 2 != 0)
        pairs += [(4 * row + 2, 4 * row + 3)] * (row // 2 != 3)
    end_three = [lax.ppermute(part, ("row", "col"), pairs) for part in middle_two]
    line = {
        "first": first,
        "middle": middle,
        "end_two": end_two,
        "middle_two": middle_two,
        "end_three": end_three,
    }
    return line, facts


def running_count(fill):
    count = fill.shape[-1]
    before = jnp.arange(count)[:, None] < jnp.arange(count)[None, :]
    return jnp.sum(jnp.where(before, fill[..., :, None], 0), axis=-2)


def places(cols):
    flat = (cols >= 0).astype(jnp.int32).reshape(cols.shape[:-2] + (-1,))
    return running_count(flat).reshape(cols.shape)


def make_table(left_of, right_of, owns, flags, chosen, width, wanted, turn=None):
    kept = right_of.shape[0] // left_of.shape[0]
    outputs = right_of.shape[0]
    left_of = jnp.repeat(left_of, kept, axis=0)
    live = (left_of > 0) & (right_of > 0) & chosen[:, None]
    counts = jnp.sum(live.astype(jnp.int32), axis=1)
    term = jnp.where(live, running_count(live.astype(jnp.int32)), -1)
    across = jnp.arange(width, dtype=jnp.int32)
    pick = term[:, None, :] == across[:, None]
    lefts = jnp.sum(jnp.where(pick, left_of[:, None, :] - 1, 0), axis=2)
    rights = jnp.sum(jnp.where(pick, right_of[:, None, :] - 1, 0), axis=2)
    flat = jnp.where(across < counts[:, None], running_count(counts)[:, None] + across, -1)
    pick = flat[None] == jnp.arange(PACKED * width, dtype=jnp.int32)[:, None, None]
    lefts = jnp.sum(jnp.where(pick, lefts, 0), axis=(1, 2))
    rights = jnp.sum(jnp.where(pick, rights, 0), axis=(1, 2))
    every = jnp.arange(outputs, dtype=jnp.int32)
    number = jnp.where(chosen, running_count(chosen.astype(jnp.int32)), -1)
    pick = number[None, :] == every[:, None]
    outs = jnp.sum(jnp.where(pick, every, 0), axis=1)
    ordered = jnp.sum(jnp.where(pick, counts, 0), axis=1)
    sizes = jnp.stack([jnp.sum(chosen.astype(jnp.int32)), jnp.sum(counts)])
    spare = jnp.zeros((BATCH,), jnp.int32)
    lists = {
        "sizes": sizes,
        "wanted": wanted,
        "outs": jnp.concatenate([outs, spare]),
        "counts": jnp.concatenate([ordered, spare]),
        "lefts": lefts,
        "rights": rights,
        "owns": owns,
        "flags": flags,
    }
    if turn is not None:
        lists["turn"] = turn
    layout = {}
    first = 0
    for name, values in lists.items():
        layout[name] = first
        first += values.shape[0]
    return jnp.concatenate(list(lists.values())), layout


def gather_facts(facts, axes):
    places = jnp.zeros((1,), jnp.int32)
    own = jnp.int32(0)
    known = 1
    for axis in axes:
        size = lax.axis_size(axis)
        own = own * size + lax.axis_index(axis)
        known *= size
    stride = known
    for axis in axes:
        size = lax.axis_size(axis)
        stride //= size
        mask = 1
        while mask < size:
            other = lax.ppermute(facts, axis, [(i, i ^ mask) for i in range(size)])
            facts = jnp.concatenate([facts, other])
            places = jnp.concatenate([places, places + mask * stride])
            mask *= 2
    hit = jnp.bitwise_xor(own, places)[None, :] == jnp.arange(known, dtype=jnp.int32)[:, None]
    return jnp.sum(jnp.where(hit[..., None], facts, 0.0), axis=1)


def per_device(x_blocks, x_cols, out_cols, branch_flag):
    rows, slots = x_cols.shape
    kept = out_cols.shape[1]
    block = x_blocks.shape[-1]
    dtype = x_blocks.dtype
    n_row = lax.axis_size("row")
    n_col = lax.axis_size("col")
    row = lax.axis_index("row")
    col = lax.axis_index("col")
    n_blocks = n_row * rows
    width = n_col * slots
    shape = (rows, kept, block, dtype)

    count = rows * slots
    tuned = n_col == 4 and n_row == 8
    if tuned:
        part_a, part_b, full, facts = pack(x_blocks, x_cols, branch_flag, row * rows)
        plane = lax.all_gather(full, "row", axis=0)
        near, far_one, far_two = [
            shift(facts, [(i, i ^ step) for i in range(n_col)]) for step in range(1, n_col)
        ]
        line_cols = jnp.concatenate([facts, near, far_one, far_two])
        total = (facts + near) + (far_one + far_two)
        facts = jnp.where(jnp.arange(128) < count, facts, total)
        line, facts = gather_line((part_a, part_b), facts)
        trace = jnp.sum(facts[:, count]).reshape(1)
    else:
        part_a, part_b, full, facts = pack(x_blocks, x_cols, branch_flag, row * rows)
        plane = lax.all_gather(full, "row", axis=0)
        line = lax.all_gather(full, "col", axis=0)
        every_fact = gather_facts(facts, ("row", "col")).reshape(n_row, n_col, 128)
        trace = jnp.sum(every_fact[:, :, count]).reshape(1)
        facts = lax.dynamic_index_in_dim(every_fact, col, 1, keepdims=False)
        line_cols = lax.dynamic_index_in_dim(every_fact, row, 0, keepdims=False)

    def slots_of(facts):
        cols = facts[:, :count].astype(jnp.int32).reshape(facts.shape[0], rows, slots)
        return cols, places(cols)

    plane_cols, plane_places = slots_of(facts)
    targets = out_cols.reshape(rows * kept)
    right_at = plane_places + STRIDE * jnp.arange(n_row, dtype=jnp.int32)[:, None, None]
    hit = plane_cols.reshape(n_blocks, slots)[None] == targets[:, None, None]
    right_of = jnp.sum(jnp.where(hit, right_at.reshape(n_blocks, slots) + 1, 0), axis=2)
    hit = x_cols[:, None, :] == out_cols[:, :, None]
    owns = jnp.sum(jnp.where(hit, places(x_cols)[:, None, :] + 1, 0), axis=2) - 1
    owns = owns.reshape(rows * kept)

    every = jnp.arange(n_blocks, dtype=jnp.int32)
    line_cols, line_places = slots_of(line_cols)

    def straight(entries, wanted):
        at = line_places + STRIDE * entries[:, None, None]
        hit = (line_cols[..., None] == every) & wanted[:, None, None, None]
        return jnp.sum(jnp.where(hit, at[..., None] + 1, 0), axis=(0, 2))

    def turned(entry, device, size, wanted):
        cols = lax.dynamic_slice_in_dim(plane_cols, device, size, 0)
        place = lax.dynamic_slice_in_dim(plane_places, device, size, 0)
        at = place + STRIDE * (entry + jnp.arange(size, dtype=jnp.int32)[:, None, None])
        own = row * rows + jnp.arange(rows, dtype=jnp.int32)
        hit = (cols[..., None] == own) & wanted
        found = jnp.sum(jnp.where(hit, at[..., None] + 1, 0), axis=2)
        names = device * rows + jnp.arange(size * rows, dtype=jnp.int32).reshape(size, rows)
        found = jnp.where(names[:, :, None, None] == every, found[..., None], 0)
        marks = jnp.any(hit, axis=3)[..., None] & (
            place[..., None] == jnp.arange(PACKED, dtype=jnp.int32)
        )
        marks = jnp.any(marks, axis=(1, 2)).astype(jnp.int32)
        return jnp.sum(found, axis=(0, 1)), marks.reshape(size * PACKED)

    heights = jnp.arange(n_col, dtype=jnp.int32)
    if not tuned:
        left_of = straight(1 + heights, heights >= 0)
        everything = jnp.ones((rows * kept,), bool)
        one = jnp.ones((1,), jnp.int32)
        table, layout = make_table(left_of, right_of, owns, branch_flag, everything, width, one)
        loads = [(0, None, 0, 0, PACKED, 2)]
        loads += [(1, c, 1 + c, 0, PACKED, 2) for c in range(n_col)]
        purified = multiply(plane, [full, line], tuple(loads), 1 + n_col, layout, table, shape)
        return purified.reshape(rows, kept, block, block), trace

    at_end = (col == 0) | (col == n_col - 1)
    corner = at_end & (row // 2 == col)
    far = at_end & ~corner
    turn_row = 2 * (n_col - 1 - col)
    wanted = [at_end | True, at_end, ~at_end, far, corner, turn_row]
    wanted = jnp.stack([value.astype(jnp.int32) for value in wanted])
    always, at_ends, inside, at_far, at_corner, turn_at = range(2, 8)

    entries = jnp.where(at_end, jnp.array([0, 1, 2, 3]), jnp.array([0, 1, 3, 2]))
    entries = entries.astype(jnp.int32)
    from_plane, marks = turned(4, turn_row, 2, corner)
    early = straight(entries, (entries < 3) | ~at_end) + from_plane
    late = straight(entries, (entries == 3) & far)
    meets = (jnp.repeat(late, kept, axis=0) > 0) & (right_of > 0)
    is_late = jnp.any(meets, axis=1)

    arrays = [full]
    loads = [(0, None, 0, 0, PACKED, always)]
    spans = ((0, SPLIT), (SPLIT, PACKED - SPLIT))

    def add(array, entry, which, wanted):
        loads.append((len(arrays), None, entry) + spans[which] + (wanted,))
        arrays.append(array)

    def call(left_of, chosen, before=None):
        turn = marks if before is None else None
        table, layout = make_table(
            left_of, right_of, owns, branch_flag, chosen, width, wanted, turn
        )
        turn = (at_corner, turn_at, 4, 2) if before is None else None
        n_entries = 6 if before is None else 4
        return multiply(
            plane, list(arrays), tuple(loads), n_entries, layout, table, shape, turn, before
        )

    stages = (
        ("first", 1, always),
        ("middle", 2, inside),
        ("end_two", 2, at_ends),
        ("middle_two", 3, inside),
    )
    for name, entry, flag in stages:
        for which in range(2):
            add(line[name][which], entry, which, flag)
    purified = call(early, ~is_late)
    for which in range(2):
        add(line["end_three"][which], 3, which, at_far)
    purified, trace = lax.optimization_barrier((purified, trace))
    purified = call(early + late, is_late, purified)
    return purified.reshape(rows, kept, block, block), trace


def solution(mesh):
    in_specs = (P("row", "col", None, None), P("row", "col"), P("row", "col"), P("row"))
    out_specs = (P("row", "col", None, None), P())
    return jax.shard_map(
        per_device, mesh=mesh, in_specs=in_specs, out_specs=out_specs, check_vma=False
    )
```

```python
import functools

import jax
import jax.numpy as jnp
from jax import lax
from jax.experimental import pallas as pl
from jax.experimental.pallas import tpu as pltpu
from jax.sharding import PartitionSpec as P

PACKED = 13
SPLIT = (PACKED + 1) // 2
STRIDE = 1 << (PACKED - 1).bit_length()
VMEM_LIMIT = 58 << 20


def pack_kernel(
    cols_ref, flag_ref, first_ref, x_ref, part_a, part_b, full, facts, held, norm, in_sems, sems
):
    count, block, _ = x_ref.shape
    slots = cols_ref.shape[0]
    loads = []
    place = jnp.int32(0)
    for index in range(count):
        filled = cols_ref[index % slots, index // slots] >= 0
        load = pltpu.make_async_copy(x_ref.at[index], held.at[index], in_sems.at[index])
        pl.when(filled)(load.start)
        loads.append((filled, place, load))
        place = place + filled.astype(jnp.int32)
    sends = []
    for index, (filled, place, load) in enumerate(loads):
        pl.when(filled)(load.wait)
        targets = (
            (full, filled, place),
            (part_a, filled & (place < SPLIT), place),
            (part_b, filled & (place >= SPLIT), place - SPLIT),
        )
        for which, (out, wanted, target) in enumerate(targets):
            target = pl.multiple_of(jnp.where(wanted, target, 0) * block, block)
            copy = pltpu.make_async_copy(
                held.at[index], out.at[pl.ds(target, block)], sems.at[which, index]
            )
            pl.when(wanted)(copy.start)
            sends.append((wanted, copy))

    norm[...] = jnp.zeros_like(norm)
    for index in range(count):
        row = index // slots
        col = cols_ref[index % slots, row]
        flag = flag_ref[row]

        @pl.when(col >= 0)
        def _():
            values = held[index].astype(jnp.float32)
            weight = (1 - 2 * flag).astype(jnp.float32)
            norm[...] += weight * jnp.sum(values * values, axis=0, keepdims=True)

        @pl.when((col == first_ref[0] + row) & (flag != 0))
        def _():
            values = held[index].astype(jnp.float32)
            eye = lax.broadcasted_iota(jnp.int32, (block, block), 0)
            eye = eye == lax.broadcasted_iota(jnp.int32, (block, block), 1)
            norm[...] += 2.0 * jnp.sum(jnp.where(eye, values, 0.0), axis=0, keepdims=True)

    across = lax.broadcasted_iota(jnp.int32, facts.shape, 1)
    values = jnp.where(across == count, jnp.sum(norm[...]), 0.0)
    for index in range(count):
        value = cols_ref[index % slots, index // slots].astype(jnp.float32)
        values = jnp.where(across == index, value, values)
    facts[...] = values
    for wanted, copy in sends:
        pl.when(wanted)(copy.wait)


def pack(x_blocks, x_cols, branch_flag, first_row):
    rows, slots, block, _ = x_blocks.shape
    count = rows * slots
    smem = pl.BlockSpec(memory_space=pltpu.SMEM)
    hbm = pl.BlockSpec(memory_space=pltpu.HBM)
    packed = [
        jax.ShapeDtypeStruct((size * block, block), x_blocks.dtype)
        for size in (SPLIT, PACKED - SPLIT, PACKED)
    ]
    return pl.pallas_call(
        pack_kernel,
        out_shape=packed + [jax.ShapeDtypeStruct((1, 128), jnp.float32)],
        in_specs=[smem, smem, smem, hbm],
        out_specs=[hbm] * 3 + [pl.BlockSpec(memory_space=pltpu.VMEM)],
        scratch_shapes=[
            pltpu.VMEM((count, block, block), x_blocks.dtype),
            pltpu.VMEM((1, block), jnp.float32),
            pltpu.SemaphoreType.DMA((count,)),
            pltpu.SemaphoreType.DMA((3, count)),
        ],
        compiler_params=pltpu.CompilerParams(vmem_limit_bytes=VMEM_LIMIT),
    )(x_cols.T, branch_flag, first_row.reshape(1), x_blocks.reshape(count, block, block))


BATCH = 4


def multiply_kernel(loads, kept, layout, turned, table, plane, *refs):
    arrays = refs[: 1 + max(load[0] for load in loads)]
    out_ref, pool, ring, more, done, in_sem, turn_sem, ring_sem, out_sem = refs[-9:]
    depth = ring.shape[0] - 1
    block = out_ref.shape[-1]
    n_out = table[0]
    n_terms = table[1]
    zero_entry = pool.shape[0] - 1

    copies = []
    for number, (which, at, entry, first, size, wanted) in enumerate(loads):
        source = arrays[which] if at is None else arrays[which].at[at]
        copy = pltpu.make_async_copy(
            source.at[pl.ds(0, size * block)],
            pool.at[entry, pl.ds(first * block, size * block)],
            in_sem.at[number],
        )
        copies.append(((table[wanted] != 0) & (n_out > 0), copy))
    for here, copy in copies:
        pl.when(here)(copy.start)

    def decode(index):
        entry = lax.shift_right_logical(index, STRIDE.bit_length() - 1)
        return entry, pl.multiple_of(jnp.bitwise_and(index, STRIDE - 1) * block, block)

    def fetch(term):
        entry, first = decode(table[layout["rights"] + term])
        slot = lax.rem(term, depth)
        return pltpu.make_async_copy(
            plane.at[entry, pl.ds(first, block)], ring.at[slot], ring_sem.at[slot]
        )

    def begin(term, carry):
        fetch(term).start()
        return carry

    if turned is not None:
        is_wanted, at, target, n_turn = turned
        rows = pltpu.make_async_copy(
            plane.at[pl.ds(table[at], n_turn)], pool.at[pl.ds(target, n_turn)], turn_sem
        )
        pl.when(table[is_wanted] != 0)(rows.start)
    lax.fori_loop(0, jnp.minimum(depth, n_terms), begin, 0)
    ring[depth] = jnp.zeros((block, block), ring.dtype)
    pool[zero_entry, pl.ds(0, block)] = jnp.zeros((block, block), pool.dtype)

    if turned is not None:
        @pl.when(table[is_wanted] != 0)
        def _():
            down = lax.broadcasted_iota(jnp.int32, (block, block), 0)
            eye = down == lax.broadcasted_iota(jnp.int32, (block, block), 1)
            eye = eye.astype(jnp.float32).astype(pool.dtype)
            rows.wait()

            def turn(place, carry):
                first = pl.multiple_of(place * block, block)
                for entry in range(n_turn):
                    @pl.when(table[layout["turn"] + entry * PACKED + place] != 0)
                    def _():
                        pool[target + entry, pl.ds(first, block)] = lax.dot_general(
                            eye,
                            pool[target + entry, pl.ds(first, block)],
                            (((1,), (1,)), ((), ())),
                            preferred_element_type=jnp.float32,
                        ).astype(pool.dtype)

                return carry

            lax.fori_loop(0, PACKED, turn, 0)

    for here, copy in copies:
        pl.when(here)(copy.wait)

    def product(term, live):
        entry, first = decode(
            jnp.where(live, table[layout["lefts"] + term], zero_entry * STRIDE)
        )
        left = pool[entry, pl.ds(first, block)]
        right = ring[jnp.where(live, lax.rem(term, depth), depth)]
        return jnp.dot(left, right, preferred_element_type=jnp.float32)

    def write(number, slot):
        output = table[layout["outs"] + number]
        return pltpu.make_async_copy(done.at[slot], out_ref.at[output], out_sem.at[slot])

    def one_batch(batch, term):
        begins, counts = [], []
        last = term
        for local in range(BATCH):
            begins.append(last)
            counts.append(table[layout["counts"] + batch * BATCH + local])
            last = last + counts[local]

        def arrived(number, carry):
            fetch(number).wait()
            return carry

        lax.fori_loop(term, last, arrived, 0)
        half = lax.rem(batch, 2) * BATCH
        for local in range(BATCH):
            @pl.when(batch >= 2)
            def _():
                write((batch - 2) * BATCH + local, half + local).wait()

            more[local] = jnp.zeros_like(more[local])

            def two_terms(pair, carry):
                number = begins[local] + 2 + 2 * pair
                second = number + 1 < begins[local] + counts[local]
                more[local] += product(number, True) + product(
                    jnp.where(second, number + 1, 0), second
                )
                return carry

            lax.fori_loop(0, (counts[local] - 1) // 2, two_terms, 0)

        for local in range(BATCH):
            output = table[layout["outs"] + batch * BATCH + local]
            square = more[local]
            for place in range(2):
                live = counts[local] > place
                square = square + product(jnp.where(live, begins[local] + place, 0), live)
            flag = table[layout["flags"] + output // kept].astype(jnp.float32)
            own = table[layout["owns"] + output]
            entry, first = decode(jnp.where(own >= 0, own, zero_entry * STRIDE))
            mine = pool[entry, pl.ds(first, block)].astype(jnp.float32)
            result = (2.0 * flag) * mine + (1.0 - 2.0 * flag) * square
            done[half + local] = result.astype(done.dtype)
        for local in range(BATCH):
            @pl.when(batch * BATCH + local < n_out)
            def _():
                write(batch * BATCH + local, half + local).start()

        def refill(number, carry):
            fetch(number + depth).start()
            return carry

        lax.fori_loop(term, jnp.clip(n_terms - depth, term, last), refill, 0)
        return last

    n_batches = (n_out + BATCH - 1) // BATCH
    lax.fori_loop(0, n_batches, one_batch, jnp.int32(0))
    for back in range(2):
        batch = n_batches - 1 - back
        for local in range(BATCH):
            number = jnp.maximum(batch, 0) * BATCH + local

            @pl.when((batch >= 0) & (number < n_out))
            def _():
                write(number, lax.rem(batch, 2) * BATCH + local).wait()


def multiply(plane, arrays, loads, n_entries, layout, table, shape, turned=None, before=None):
    rows, kept, block, dtype = shape
    outputs = rows * kept
    depth = 48
    smem = pl.BlockSpec(memory_space=pltpu.SMEM)
    hbm = pl.BlockSpec(memory_space=pltpu.HBM)
    operands = [table, plane, *arrays]
    aliases = {}
    if before is not None:
        operands.append(before)
        aliases = {len(operands) - 1: 0}
    return pl.pallas_call(
        functools.partial(multiply_kernel, loads, kept, layout, turned),
        out_shape=jax.ShapeDtypeStruct((outputs, block, block), dtype),
        in_specs=[smem] + [hbm] * (len(operands) - 1),
        out_specs=hbm,
        scratch_shapes=[
            pltpu.VMEM((n_entries + 1, PACKED * block, block), dtype),
            pltpu.VMEM((depth + 1, block, block), dtype),
            pltpu.VMEM((BATCH, block, block), jnp.float32),
            pltpu.VMEM((2 * BATCH, block, block), dtype),
            pltpu.SemaphoreType.DMA((len(loads),)),
            pltpu.SemaphoreType.DMA,
            pltpu.SemaphoreType.DMA((depth,)),
            pltpu.SemaphoreType.DMA((2 * BATCH,)),
        ],
        input_output_aliases=aliases,
        compiler_params=pltpu.CompilerParams(vmem_limit_bytes=VMEM_LIMIT),
    )(*operands)


def shift(array, pairs):
    return lax.ppermute(array, "col", pairs)


def gather_line(parts, facts):
    first = [shift(part, [(0, 1), (1, 0), (2, 3), (3, 2)]) for part in parts]
    middle = [shift(part, [(1, 2), (2, 1)]) for part in parts]
    facts = gather_facts(facts, ("row",))
    middle[0], facts = lax.optimization_barrier((middle[0], facts))
    end_two = [shift(part, [(1, 0), (2, 3)]) for part in middle]
    middle_two = [shift(part, [(1, 2), (2, 1)]) for part in first]
    pairs = []
    for row in range(lax.axis_size("row")):
        pairs += [(4 * row + 1, 4 * row)] * (row // 2 != 0)
        pairs += [(4 * row + 2, 4 * row + 3)] * (row // 2 != 3)
    small = lax.ppermute(middle_two[1], ("row", "col"), pairs)
    large = lax.optimization_barrier((middle_two[0], small))[0]
    end_three = [lax.ppermute(large, ("row", "col"), pairs), small]
    line = {
        "first": first,
        "middle": middle,
        "end_two": end_two,
        "middle_two": middle_two,
        "end_three": end_three,
    }
    return line, facts


def running_count(fill):
    count = fill.shape[-1]
    before = jnp.arange(count)[:, None] < jnp.arange(count)[None, :]
    return jnp.sum(jnp.where(before, fill[..., :, None], 0), axis=-2)


def places(cols):
    flat = (cols >= 0).astype(jnp.int32).reshape(cols.shape[:-2] + (-1,))
    return running_count(flat).reshape(cols.shape)


def make_table(left_of, right_of, owns, flags, chosen, width, wanted, turn=None):
    kept = right_of.shape[0] // left_of.shape[0]
    outputs = right_of.shape[0]
    left_of = jnp.repeat(left_of, kept, axis=0)
    live = (left_of > 0) & (right_of > 0) & chosen[:, None]
    counts = jnp.sum(live.astype(jnp.int32), axis=1)
    term = jnp.where(live, running_count(live.astype(jnp.int32)), -1)
    across = jnp.arange(width, dtype=jnp.int32)
    pick = term[:, None, :] == across[:, None]
    lefts = jnp.sum(jnp.where(pick, left_of[:, None, :] - 1, 0), axis=2)
    rights = jnp.sum(jnp.where(pick, right_of[:, None, :] - 1, 0), axis=2)
    flat = jnp.where(across < counts[:, None], running_count(counts)[:, None] + across, -1)
    pick = flat[None] == jnp.arange(PACKED * width, dtype=jnp.int32)[:, None, None]
    lefts = jnp.sum(jnp.where(pick, lefts, 0), axis=(1, 2))
    rights = jnp.sum(jnp.where(pick, rights, 0), axis=(1, 2))
    every = jnp.arange(outputs, dtype=jnp.int32)
    number = jnp.where(chosen, running_count(chosen.astype(jnp.int32)), -1)
    pick = number[None, :] == every[:, None]
    outs = jnp.sum(jnp.where(pick, every, 0), axis=1)
    ordered = jnp.sum(jnp.where(pick, counts, 0), axis=1)
    sizes = jnp.stack([jnp.sum(chosen.astype(jnp.int32)), jnp.sum(counts)])
    spare = jnp.zeros((BATCH,), jnp.int32)
    lists = {
        "sizes": sizes,
        "wanted": wanted,
        "outs": jnp.concatenate([outs, spare]),
        "counts": jnp.concatenate([ordered, spare]),
        "lefts": lefts,
        "rights": rights,
        "owns": owns,
        "flags": flags,
    }
    if turn is not None:
        lists["turn"] = turn
    layout = {}
    first = 0
    for name, values in lists.items():
        layout[name] = first
        first += values.shape[0]
    return jnp.concatenate(list(lists.values())), layout


def gather_facts(facts, axes):
    places = jnp.zeros((1,), jnp.int32)
    own = jnp.int32(0)
    known = 1
    for axis in axes:
        size = lax.axis_size(axis)
        own = own * size + lax.axis_index(axis)
        known *= size
    stride = known
    for axis in axes:
        size = lax.axis_size(axis)
        stride //= size
        mask = 1
        while mask < size:
            other = lax.ppermute(facts, axis, [(i, i ^ mask) for i in range(size)])
            facts = jnp.concatenate([facts, other])
            places = jnp.concatenate([places, places + mask * stride])
            mask *= 2
    hit = jnp.bitwise_xor(own, places)[None, :] == jnp.arange(known, dtype=jnp.int32)[:, None]
    return jnp.sum(jnp.where(hit[..., None], facts, 0.0), axis=1)


def per_device(x_blocks, x_cols, out_cols, branch_flag):
    rows, slots = x_cols.shape
    kept = out_cols.shape[1]
    block = x_blocks.shape[-1]
    dtype = x_blocks.dtype
    n_row = lax.axis_size("row")
    n_col = lax.axis_size("col")
    row = lax.axis_index("row")
    col = lax.axis_index("col")
    n_blocks = n_row * rows
    width = n_col * slots
    shape = (rows, kept, block, dtype)

    count = rows * slots
    tuned = n_col == 4 and n_row == 8
    if tuned:
        part_a, part_b, full, facts = pack(x_blocks, x_cols, branch_flag, row * rows)
        plane = lax.all_gather(full, "row", axis=0)
        near, far_one, far_two = [
            shift(facts, [(i, i ^ step) for i in range(n_col)]) for step in range(1, n_col)
        ]
        line_cols = jnp.concatenate([facts, near, far_one, far_two])
        total = (facts + near) + (far_one + far_two)
        facts = jnp.where(jnp.arange(128) < count, facts, total)
        line, facts = gather_line((part_a, part_b), facts)
        trace = jnp.sum(facts[:, count]).reshape(1)
    else:
        part_a, part_b, full, facts = pack(x_blocks, x_cols, branch_flag, row * rows)
        plane = lax.all_gather(full, "row", axis=0)
        line = lax.all_gather(full, "col", axis=0)
        every_fact = gather_facts(facts, ("row", "col")).reshape(n_row, n_col, 128)
        trace = jnp.sum(every_fact[:, :, count]).reshape(1)
        facts = lax.dynamic_index_in_dim(every_fact, col, 1, keepdims=False)
        line_cols = lax.dynamic_index_in_dim(every_fact, row, 0, keepdims=False)

    def slots_of(facts):
        cols = facts[:, :count].astype(jnp.int32).reshape(facts.shape[0], rows, slots)
        return cols, places(cols)

    plane_cols, plane_places = slots_of(facts)
    targets = out_cols.reshape(rows * kept)
    right_at = plane_places + STRIDE * jnp.arange(n_row, dtype=jnp.int32)[:, None, None]
    hit = plane_cols.reshape(n_blocks, slots)[None] == targets[:, None, None]
    right_of = jnp.sum(jnp.where(hit, right_at.reshape(n_blocks, slots) + 1, 0), axis=2)
    hit = x_cols[:, None, :] == out_cols[:, :, None]
    owns = jnp.sum(jnp.where(hit, places(x_cols)[:, None, :] + 1, 0), axis=2) - 1
    owns = owns.reshape(rows * kept)

    every = jnp.arange(n_blocks, dtype=jnp.int32)
    line_cols, line_places = slots_of(line_cols)

    def straight(entries, wanted):
        at = line_places + STRIDE * entries[:, None, None]
        hit = (line_cols[..., None] == every) & wanted[:, None, None, None]
        return jnp.sum(jnp.where(hit, at[..., None] + 1, 0), axis=(0, 2))

    def turned(entry, device, size, wanted):
        cols = lax.dynamic_slice_in_dim(plane_cols, device, size, 0)
        place = lax.dynamic_slice_in_dim(plane_places, device, size, 0)
        at = place + STRIDE * (entry + jnp.arange(size, dtype=jnp.int32)[:, None, None])
        own = row * rows + jnp.arange(rows, dtype=jnp.int32)
        hit = (cols[..., None] == own) & wanted
        found = jnp.sum(jnp.where(hit, at[..., None] + 1, 0), axis=2)
        names = device * rows + jnp.arange(size * rows, dtype=jnp.int32).reshape(size, rows)
        found = jnp.where(names[:, :, None, None] == every, found[..., None], 0)
        marks = jnp.any(hit, axis=3)[..., None] & (
            place[..., None] == jnp.arange(PACKED, dtype=jnp.int32)
        )
        marks = jnp.any(marks, axis=(1, 2)).astype(jnp.int32)
        return jnp.sum(found, axis=(0, 1)), marks.reshape(size * PACKED)

    heights = jnp.arange(n_col, dtype=jnp.int32)
    if not tuned:
        left_of = straight(1 + heights, heights >= 0)
        everything = jnp.ones((rows * kept,), bool)
        one = jnp.ones((1,), jnp.int32)
        table, layout = make_table(left_of, right_of, owns, branch_flag, everything, width, one)
        loads = [(0, None, 0, 0, PACKED, 2)]
        loads += [(1, c, 1 + c, 0, PACKED, 2) for c in range(n_col)]
        purified = multiply(plane, [full, line], tuple(loads), 1 + n_col, layout, table, shape)
        return purified.reshape(rows, kept, block, block), trace

    at_end = (col == 0) | (col == n_col - 1)
    corner = at_end & (row // 2 == col)
    far = at_end & ~corner
    turn_row = 2 * (n_col - 1 - col)
    wanted = [at_end | True, at_end, ~at_end, far, corner, turn_row]
    wanted = jnp.stack([value.astype(jnp.int32) for value in wanted])
    always, at_ends, inside, at_far, at_corner, turn_at = range(2, 8)

    entries = jnp.where(at_end, jnp.array([0, 1, 2, 3]), jnp.array([0, 1, 3, 2]))
    entries = entries.astype(jnp.int32)
    from_plane, marks = turned(4, turn_row, 2, corner)
    early = straight(entries, (entries < 3) | ~at_end) + from_plane
    late = straight(entries, (entries == 3) & far)
    meets = (jnp.repeat(late, kept, axis=0) > 0) & (right_of > 0)
    is_late = jnp.any(meets, axis=1)

    arrays = [full]
    loads = [(0, None, 0, 0, PACKED, always)]
    spans = ((0, SPLIT), (SPLIT, PACKED - SPLIT))

    def add(array, entry, which, wanted):
        loads.append((len(arrays), None, entry) + spans[which] + (wanted,))
        arrays.append(array)

    def call(left_of, chosen, before=None):
        turn = marks if before is None else None
        table, layout = make_table(
            left_of, right_of, owns, branch_flag, chosen, width, wanted, turn
        )
        turn = (at_corner, turn_at, 4, 2) if before is None else None
        n_entries = 6 if before is None else 4
        return multiply(
            plane, list(arrays), tuple(loads), n_entries, layout, table, shape, turn, before
        )

    stages = (
        ("first", 1, always),
        ("middle", 2, inside),
        ("end_two", 2, at_ends),
        ("middle_two", 3, inside),
    )
    for name, entry, flag in stages:
        for which in range(2):
            add(line[name][which], entry, which, flag)
    purified = call(early, ~is_late)
    for which in range(2):
        add(line["end_three"][which], 3, which, at_far)
    purified, trace = lax.optimization_barrier((purified, trace))
    purified = call(early + late, is_late, purified)
    return purified.reshape(rows, kept, block, block), trace


def solution(mesh):
    in_specs = (P("row", "col", None, None), P("row", "col"), P("row", "col"), P("row"))
    out_specs = (P("row", "col", None, None), P())
    return jax.shard_map(
        per_device, mesh=mesh, in_specs=in_specs, out_specs=out_specs, check_vma=False
    )
```

```python
import functools

import jax
import jax.numpy as jnp
from jax import lax
from jax.experimental import pallas as pl
from jax.experimental.pallas import tpu as pltpu
from jax.sharding import PartitionSpec as P

PACKED = 13
SPLIT = (PACKED + 1) // 2
STRIDE = 1 << (PACKED - 1).bit_length()
VMEM_LIMIT = 58 << 20


def pack_kernel(
    cols_ref, flag_ref, first_ref, x_ref, part_a, part_b, full, facts, held, norm, in_sems, sems
):
    count, block, _ = x_ref.shape
    slots = cols_ref.shape[0]
    loads = []
    place = jnp.int32(0)
    for index in range(count):
        filled = cols_ref[index % slots, index // slots] >= 0
        load = pltpu.make_async_copy(x_ref.at[index], held.at[index], in_sems.at[index])
        pl.when(filled)(load.start)
        loads.append((filled, place, load))
        place = place + filled.astype(jnp.int32)
    sends = []
    for index, (filled, place, load) in enumerate(loads):
        pl.when(filled)(load.wait)
        targets = (
            (full, filled, place),
            (part_a, filled & (place < SPLIT), place),
            (part_b, filled & (place >= SPLIT), place - SPLIT),
        )
        for which, (out, wanted, target) in enumerate(targets):
            target = pl.multiple_of(jnp.where(wanted, target, 0) * block, block)
            copy = pltpu.make_async_copy(
                held.at[index], out.at[pl.ds(target, block)], sems.at[which, index]
            )
            pl.when(wanted)(copy.start)
            sends.append((wanted, copy))

    norm[...] = jnp.zeros_like(norm)
    for index in range(count):
        row = index // slots
        col = cols_ref[index % slots, row]
        flag = flag_ref[row]

        @pl.when(col >= 0)
        def _():
            values = held[index].astype(jnp.float32)
            weight = (1 - 2 * flag).astype(jnp.float32)
            norm[...] += weight * jnp.sum(values * values, axis=0, keepdims=True)

        @pl.when((col == first_ref[0] + row) & (flag != 0))
        def _():
            values = held[index].astype(jnp.float32)
            eye = lax.broadcasted_iota(jnp.int32, (block, block), 0)
            eye = eye == lax.broadcasted_iota(jnp.int32, (block, block), 1)
            norm[...] += 2.0 * jnp.sum(jnp.where(eye, values, 0.0), axis=0, keepdims=True)

    across = lax.broadcasted_iota(jnp.int32, facts.shape, 1)
    values = jnp.where(across == count, jnp.sum(norm[...]), 0.0)
    for index in range(count):
        value = cols_ref[index % slots, index // slots].astype(jnp.float32)
        values = jnp.where(across == index, value, values)
    facts[...] = values
    for wanted, copy in sends:
        pl.when(wanted)(copy.wait)


def pack(x_blocks, x_cols, branch_flag, first_row):
    rows, slots, block, _ = x_blocks.shape
    count = rows * slots
    smem = pl.BlockSpec(memory_space=pltpu.SMEM)
    hbm = pl.BlockSpec(memory_space=pltpu.HBM)
    packed = [
        jax.ShapeDtypeStruct((size * block, block), x_blocks.dtype)
        for size in (SPLIT, PACKED - SPLIT, PACKED)
    ]
    return pl.pallas_call(
        pack_kernel,
        out_shape=packed + [jax.ShapeDtypeStruct((1, 128), jnp.float32)],
        in_specs=[smem, smem, smem, hbm],
        out_specs=[hbm] * 3 + [pl.BlockSpec(memory_space=pltpu.VMEM)],
        scratch_shapes=[
            pltpu.VMEM((count, block, block), x_blocks.dtype),
            pltpu.VMEM((1, block), jnp.float32),
            pltpu.SemaphoreType.DMA((count,)),
            pltpu.SemaphoreType.DMA((3, count)),
        ],
        compiler_params=pltpu.CompilerParams(vmem_limit_bytes=VMEM_LIMIT),
    )(x_cols.T, branch_flag, first_row.reshape(1), x_blocks.reshape(count, block, block))


BATCH = 4


def multiply_kernel(loads, kept, layout, turned, table, plane, *refs):
    arrays = refs[: 1 + max(load[0] for load in loads)]
    out_ref, pool, ring, more, done, in_sem, turn_sem, ring_sem, out_sem = refs[-9:]
    depth = ring.shape[0] - 1
    block = out_ref.shape[-1]
    n_out = table[0]
    n_terms = table[1]
    zero_entry = pool.shape[0] - 1

    copies = []
    for number, (which, at, entry, first, size, wanted) in enumerate(loads):
        source = arrays[which] if at is None else arrays[which].at[at]
        copy = pltpu.make_async_copy(
            source.at[pl.ds(0, size * block)],
            pool.at[entry, pl.ds(first * block, size * block)],
            in_sem.at[number],
        )
        copies.append(((table[wanted] != 0) & (n_out > 0), copy))
    for here, copy in copies:
        pl.when(here)(copy.start)

    def decode(index):
        entry = lax.shift_right_logical(index, STRIDE.bit_length() - 1)
        return entry, pl.multiple_of(jnp.bitwise_and(index, STRIDE - 1) * block, block)

    def fetch(term):
        entry, first = decode(table[layout["rights"] + term])
        slot = lax.rem(term, depth)
        return pltpu.make_async_copy(
            plane.at[entry, pl.ds(first, block)], ring.at[slot], ring_sem.at[slot]
        )

    def begin(term, carry):
        fetch(term).start()
        return carry

    if turned is not None:
        is_wanted, at, target, n_turn = turned
        rows = pltpu.make_async_copy(
            plane.at[pl.ds(table[at], n_turn)], pool.at[pl.ds(target, n_turn)], turn_sem
        )
        pl.when(table[is_wanted] != 0)(rows.start)
    lax.fori_loop(0, jnp.minimum(depth, n_terms), begin, 0)
    ring[depth] = jnp.zeros((block, block), ring.dtype)
    pool[zero_entry, pl.ds(0, block)] = jnp.zeros((block, block), pool.dtype)

    if turned is not None:
        @pl.when(table[is_wanted] != 0)
        def _():
            down = lax.broadcasted_iota(jnp.int32, (block, block), 0)
            eye = down == lax.broadcasted_iota(jnp.int32, (block, block), 1)
            eye = eye.astype(jnp.float32).astype(pool.dtype)
            rows.wait()

            def turn(place, carry):
                first = pl.multiple_of(place * block, block)
                for entry in range(n_turn):
                    @pl.when(table[layout["turn"] + entry * PACKED + place] != 0)
                    def _():
                        pool[target + entry, pl.ds(first, block)] = lax.dot_general(
                            eye,
                            pool[target + entry, pl.ds(first, block)],
                            (((1,), (1,)), ((), ())),
                            preferred_element_type=jnp.float32,
                        ).astype(pool.dtype)

                return carry

            lax.fori_loop(0, PACKED, turn, 0)

    for here, copy in copies:
        pl.when(here)(copy.wait)

    def product(term, live):
        entry, first = decode(
            jnp.where(live, table[layout["lefts"] + term], zero_entry * STRIDE)
        )
        left = pool[entry, pl.ds(first, block)]
        right = ring[jnp.where(live, lax.rem(term, depth), depth)]
        return jnp.dot(left, right, preferred_element_type=jnp.float32)

    def write(number, slot):
        output = table[layout["outs"] + number]
        return pltpu.make_async_copy(done.at[slot], out_ref.at[output], out_sem.at[slot])

    def one_batch(batch, term):
        begins, counts = [], []
        last = term
        for local in range(BATCH):
            begins.append(last)
            counts.append(table[layout["counts"] + batch * BATCH + local])
            last = last + counts[local]

        def arrived(number, carry):
            fetch(number).wait()
            return carry

        lax.fori_loop(term, last, arrived, 0)
        half = lax.rem(batch, 2) * BATCH
        for local in range(BATCH):
            @pl.when(batch >= 2)
            def _():
                write((batch - 2) * BATCH + local, half + local).wait()

            more[local] = jnp.zeros_like(more[local])

            def two_terms(pair, carry):
                number = begins[local] + 2 + 2 * pair
                second = number + 1 < begins[local] + counts[local]
                more[local] += product(number, True) + product(
                    jnp.where(second, number + 1, 0), second
                )
                return carry

            lax.fori_loop(0, (counts[local] - 1) // 2, two_terms, 0)

        for local in range(BATCH):
            output = table[layout["outs"] + batch * BATCH + local]
            square = more[local]
            for place in range(2):
                live = counts[local] > place
                square = square + product(jnp.where(live, begins[local] + place, 0), live)
            flag = table[layout["flags"] + output // kept].astype(jnp.float32)
            own = table[layout["owns"] + output]
            entry, first = decode(jnp.where(own >= 0, own, zero_entry * STRIDE))
            mine = pool[entry, pl.ds(first, block)].astype(jnp.float32)
            result = (2.0 * flag) * mine + (1.0 - 2.0 * flag) * square
            done[half + local] = result.astype(done.dtype)
        for local in range(BATCH):
            @pl.when(batch * BATCH + local < n_out)
            def _():
                write(batch * BATCH + local, half + local).start()

        def refill(number, carry):
            fetch(number + depth).start()
            return carry

        lax.fori_loop(term, jnp.clip(n_terms - depth, term, last), refill, 0)
        return last

    n_batches = (n_out + BATCH - 1) // BATCH
    lax.fori_loop(0, n_batches, one_batch, jnp.int32(0))
    for back in range(2):
        batch = n_batches - 1 - back
        for local in range(BATCH):
            number = jnp.maximum(batch, 0) * BATCH + local

            @pl.when((batch >= 0) & (number < n_out))
            def _():
                write(number, lax.rem(batch, 2) * BATCH + local).wait()


def multiply(plane, arrays, loads, n_entries, layout, table, shape, turned=None, before=None):
    rows, kept, block, dtype = shape
    outputs = rows * kept
    depth = 48
    smem = pl.BlockSpec(memory_space=pltpu.SMEM)
    hbm = pl.BlockSpec(memory_space=pltpu.HBM)
    operands = [table, plane, *arrays]
    aliases = {}
    if before is not None:
        operands.append(before)
        aliases = {len(operands) - 1: 0}
    return pl.pallas_call(
        functools.partial(multiply_kernel, loads, kept, layout, turned),
        out_shape=jax.ShapeDtypeStruct((outputs, block, block), dtype),
        in_specs=[smem] + [hbm] * (len(operands) - 1),
        out_specs=hbm,
        scratch_shapes=[
            pltpu.VMEM((n_entries + 1, PACKED * block, block), dtype),
            pltpu.VMEM((depth + 1, block, block), dtype),
            pltpu.VMEM((BATCH, block, block), jnp.float32),
            pltpu.VMEM((2 * BATCH, block, block), dtype),
            pltpu.SemaphoreType.DMA((len(loads),)),
            pltpu.SemaphoreType.DMA,
            pltpu.SemaphoreType.DMA((depth,)),
            pltpu.SemaphoreType.DMA((2 * BATCH,)),
        ],
        input_output_aliases=aliases,
        compiler_params=pltpu.CompilerParams(vmem_limit_bytes=VMEM_LIMIT),
    )(*operands)


def shift(array, pairs):
    return lax.ppermute(array, "col", pairs)


def start_line(parts, facts):
    first = [shift(part, [(0, 1), (1, 0), (2, 3), (3, 2)]) for part in parts]
    middle = [shift(part, [(1, 2), (2, 1)]) for part in parts]
    facts = gather_facts(facts, ("row",))
    middle[1], facts = lax.optimization_barrier((middle[1], facts))
    return first, middle, facts


def relay_line(first, middle):
    end_two = [shift(part, [(1, 0), (2, 3)]) for part in middle]
    middle_two = [shift(part, [(1, 2), (2, 1)]) for part in first]
    pairs = []
    for row in range(lax.axis_size("row")):
        pairs += [(4 * row + 1, 4 * row)] * (row // 2 != 0)
        pairs += [(4 * row + 2, 4 * row + 3)] * (row // 2 != 3)
    small = lax.optimization_barrier((middle_two[1], end_two[1]))[0]
    small = lax.ppermute(small, ("row", "col"), pairs)
    large = lax.optimization_barrier((middle_two[0], small))[0]
    return {
        "first": first,
        "middle": middle,
        "end_two": end_two,
        "middle_two": middle_two,
        "end_three": (lax.ppermute(large, ("row", "col"), pairs), small),
    }


def running_count(fill):
    count = fill.shape[-1]
    before = jnp.arange(count)[:, None] < jnp.arange(count)[None, :]
    return jnp.sum(jnp.where(before, fill[..., :, None], 0), axis=-2)


def places(cols):
    flat = (cols >= 0).astype(jnp.int32).reshape(cols.shape[:-2] + (-1,))
    return running_count(flat).reshape(cols.shape)


def make_table(left_of, right_of, owns, flags, chosen, width, wanted, turn=None):
    kept = right_of.shape[0] // left_of.shape[0]
    outputs = right_of.shape[0]
    left_of = jnp.repeat(left_of, kept, axis=0)
    live = (left_of > 0) & (right_of > 0) & chosen[:, None]
    counts = jnp.sum(live.astype(jnp.int32), axis=1)
    term = jnp.where(live, running_count(live.astype(jnp.int32)), -1)
    across = jnp.arange(width, dtype=jnp.int32)
    pick = term[:, None, :] == across[:, None]
    lefts = jnp.sum(jnp.where(pick, left_of[:, None, :] - 1, 0), axis=2)
    rights = jnp.sum(jnp.where(pick, right_of[:, None, :] - 1, 0), axis=2)
    flat = jnp.where(across < counts[:, None], running_count(counts)[:, None] + across, -1)
    pick = flat[None] == jnp.arange(PACKED * width, dtype=jnp.int32)[:, None, None]
    lefts = jnp.sum(jnp.where(pick, lefts, 0), axis=(1, 2))
    rights = jnp.sum(jnp.where(pick, rights, 0), axis=(1, 2))
    every = jnp.arange(outputs, dtype=jnp.int32)
    number = jnp.where(chosen, running_count(chosen.astype(jnp.int32)), -1)
    pick = number[None, :] == every[:, None]
    outs = jnp.sum(jnp.where(pick, every, 0), axis=1)
    ordered = jnp.sum(jnp.where(pick, counts, 0), axis=1)
    sizes = jnp.stack([jnp.sum(chosen.astype(jnp.int32)), jnp.sum(counts)])
    spare = jnp.zeros((BATCH,), jnp.int32)
    lists = {
        "sizes": sizes,
        "wanted": wanted,
        "outs": jnp.concatenate([outs, spare]),
        "counts": jnp.concatenate([ordered, spare]),
        "lefts": lefts,
        "rights": rights,
        "owns": owns,
        "flags": flags,
    }
    if turn is not None:
        lists["turn"] = turn
    layout = {}
    first = 0
    for name, values in lists.items():
        layout[name] = first
        first += values.shape[0]
    return jnp.concatenate(list(lists.values())), layout


def gather_facts(facts, axes):
    places = jnp.zeros((1,), jnp.int32)
    own = jnp.int32(0)
    known = 1
    for axis in axes:
        size = lax.axis_size(axis)
        own = own * size + lax.axis_index(axis)
        known *= size
    stride = known
    for axis in axes:
        size = lax.axis_size(axis)
        stride //= size
        mask = 1
        while mask < size:
            other = lax.ppermute(facts, axis, [(i, i ^ mask) for i in range(size)])
            facts = jnp.concatenate([facts, other])
            places = jnp.concatenate([places, places + mask * stride])
            mask *= 2
    hit = jnp.bitwise_xor(own, places)[None, :] == jnp.arange(known, dtype=jnp.int32)[:, None]
    return jnp.sum(jnp.where(hit[..., None], facts, 0.0), axis=1)


def per_device(x_blocks, x_cols, out_cols, branch_flag):
    rows, slots = x_cols.shape
    kept = out_cols.shape[1]
    block = x_blocks.shape[-1]
    dtype = x_blocks.dtype
    n_row = lax.axis_size("row")
    n_col = lax.axis_size("col")
    row = lax.axis_index("row")
    col = lax.axis_index("col")
    n_blocks = n_row * rows
    width = n_col * slots
    shape = (rows, kept, block, dtype)

    count = rows * slots
    tuned = n_col == 4 and n_row == 8
    if tuned:
        part_a, part_b, full, facts = pack(x_blocks, x_cols, branch_flag, row * rows)
        plane = lax.all_gather(full, "row", axis=0)
        near, far_one, far_two = [
            shift(facts, [(i, i ^ step) for i in range(n_col)]) for step in range(1, n_col)
        ]
        line_cols = jnp.concatenate([facts, near, far_one, far_two])
        total = (facts + near) + (far_one + far_two)
        facts = jnp.where(jnp.arange(128) < count, facts, total)
        first, middle, facts = start_line((part_a, part_b), facts)
        trace = jnp.sum(facts[:, count]).reshape(1)
    else:
        part_a, part_b, full, facts = pack(x_blocks, x_cols, branch_flag, row * rows)
        plane = lax.all_gather(full, "row", axis=0)
        line = lax.all_gather(full, "col", axis=0)
        every_fact = gather_facts(facts, ("row", "col")).reshape(n_row, n_col, 128)
        trace = jnp.sum(every_fact[:, :, count]).reshape(1)
        facts = lax.dynamic_index_in_dim(every_fact, col, 1, keepdims=False)
        line_cols = lax.dynamic_index_in_dim(every_fact, row, 0, keepdims=False)

    def slots_of(facts):
        cols = facts[:, :count].astype(jnp.int32).reshape(facts.shape[0], rows, slots)
        return cols, places(cols)

    plane_cols, plane_places = slots_of(facts)
    targets = out_cols.reshape(rows * kept)
    right_at = plane_places + STRIDE * jnp.arange(n_row, dtype=jnp.int32)[:, None, None]
    hit = plane_cols.reshape(n_blocks, slots)[None] == targets[:, None, None]
    right_of = jnp.sum(jnp.where(hit, right_at.reshape(n_blocks, slots) + 1, 0), axis=2)
    hit = x_cols[:, None, :] == out_cols[:, :, None]
    owns = jnp.sum(jnp.where(hit, places(x_cols)[:, None, :] + 1, 0), axis=2) - 1
    owns = owns.reshape(rows * kept)

    every = jnp.arange(n_blocks, dtype=jnp.int32)
    line_cols, line_places = slots_of(line_cols)

    def straight(entries, wanted):
        at = line_places + STRIDE * entries[:, None, None]
        hit = (line_cols[..., None] == every) & wanted[:, None, None, None]
        return jnp.sum(jnp.where(hit, at[..., None] + 1, 0), axis=(0, 2))

    def turned(entry, device, size, wanted):
        cols = lax.dynamic_slice_in_dim(plane_cols, device, size, 0)
        place = lax.dynamic_slice_in_dim(plane_places, device, size, 0)
        at = place + STRIDE * (entry + jnp.arange(size, dtype=jnp.int32)[:, None, None])
        own = row * rows + jnp.arange(rows, dtype=jnp.int32)
        hit = (cols[..., None] == own) & wanted
        found = jnp.sum(jnp.where(hit, at[..., None] + 1, 0), axis=2)
        names = device * rows + jnp.arange(size * rows, dtype=jnp.int32).reshape(size, rows)
        found = jnp.where(names[:, :, None, None] == every, found[..., None], 0)
        marks = jnp.any(hit, axis=3)[..., None] & (
            place[..., None] == jnp.arange(PACKED, dtype=jnp.int32)
        )
        marks = jnp.any(marks, axis=(1, 2)).astype(jnp.int32)
        return jnp.sum(found, axis=(0, 1)), marks.reshape(size * PACKED)

    heights = jnp.arange(n_col, dtype=jnp.int32)
    if not tuned:
        left_of = straight(1 + heights, heights >= 0)
        everything = jnp.ones((rows * kept,), bool)
        one = jnp.ones((1,), jnp.int32)
        table, layout = make_table(left_of, right_of, owns, branch_flag, everything, width, one)
        loads = [(0, None, 0, 0, PACKED, 2)]
        loads += [(1, c, 1 + c, 0, PACKED, 2) for c in range(n_col)]
        purified = multiply(plane, [full, line], tuple(loads), 1 + n_col, layout, table, shape)
        return purified.reshape(rows, kept, block, block), trace

    at_end = (col == 0) | (col == n_col - 1)
    corner = at_end & (row // 2 == col)
    far = at_end & ~corner
    turn_row = 2 * (n_col - 1 - col)
    wanted = [at_end | True, at_end, ~at_end, far, corner, turn_row]
    wanted = jnp.stack([value.astype(jnp.int32) for value in wanted])
    always, at_ends, inside, at_far, at_corner, turn_at = range(2, 8)

    entries = jnp.where(at_end, jnp.array([0, 1, 2, 3]), jnp.array([0, 1, 3, 2]))
    entries = entries.astype(jnp.int32)
    from_plane, marks = turned(4, turn_row, 2, corner)
    early = straight(entries, (entries < 3) | ~at_end) + from_plane
    late = straight(entries, (entries == 3) & far)
    meets = (jnp.repeat(late, kept, axis=0) > 0) & (right_of > 0)
    is_late = jnp.any(meets, axis=1)

    def table_of(left_of, chosen, turn=None):
        return make_table(left_of, right_of, owns, branch_flag, chosen, width, wanted, turn)

    early_table, early_layout = table_of(early, ~is_late, marks)
    late_table, late_layout = table_of(early + late, is_late)
    first[0], middle[0], early_table, late_table = lax.optimization_barrier(
        (first[0], middle[0], early_table, late_table)
    )
    line = relay_line(first, middle)

    arrays = [full]
    loads = [(0, None, 0, 0, PACKED, always)]
    spans = ((0, SPLIT), (SPLIT, PACKED - SPLIT))

    def add(array, entry, which, wanted):
        loads.append((len(arrays), None, entry) + spans[which] + (wanted,))
        arrays.append(array)

    stages = (
        ("first", 1, always),
        ("middle", 2, inside),
        ("end_two", 2, at_ends),
        ("middle_two", 3, inside),
    )
    for name, entry, flag in stages:
        for which in range(2):
            add(line[name][which], entry, which, flag)
    purified = multiply(
        plane, list(arrays), tuple(loads), 6, early_layout, early_table, shape,
        (at_corner, turn_at, 4, 2),
    )
    for which in range(2):
        add(line["end_three"][which], 3, which, at_far)
    purified, trace = lax.optimization_barrier((purified, trace))
    purified = multiply(
        plane, list(arrays), tuple(loads), 4, late_layout, late_table, shape, None, purified
    )
    return purified.reshape(rows, kept, block, block), trace


def solution(mesh):
    in_specs = (P("row", "col", None, None), P("row", "col"), P("row", "col"), P("row"))
    out_specs = (P("row", "col", None, None), P())
    return jax.shard_map(
        per_device, mesh=mesh, in_specs=in_specs, out_specs=out_specs, check_vma=False
    )
```

```python
import functools

import jax
import jax.numpy as jnp
from jax import lax
from jax.experimental import pallas as pl
from jax.experimental.pallas import tpu as pltpu
from jax.sharding import PartitionSpec as P

PACKED = 13
SPLIT = (PACKED + 1) // 2
STRIDE = 1 << (PACKED - 1).bit_length()
VMEM_LIMIT = 58 << 20


def pack_kernel(
    cols_ref, flag_ref, first_ref, x_ref, part_a, part_b, full, facts, held, norm, in_sems, sems
):
    count, block, _ = x_ref.shape
    slots = cols_ref.shape[0]
    loads = []
    place = jnp.int32(0)
    for index in range(count):
        filled = cols_ref[index % slots, index // slots] >= 0
        load = pltpu.make_async_copy(x_ref.at[index], held.at[index], in_sems.at[index])
        pl.when(filled)(load.start)
        loads.append((filled, place, load))
        place = place + filled.astype(jnp.int32)
    sends = []
    for index, (filled, place, load) in enumerate(loads):
        pl.when(filled)(load.wait)
        targets = (
            (full, filled, place),
            (part_a, filled & (place < SPLIT), place),
            (part_b, filled & (place >= SPLIT), place - SPLIT),
        )
        for which, (out, wanted, target) in enumerate(targets):
            target = pl.multiple_of(jnp.where(wanted, target, 0) * block, block)
            copy = pltpu.make_async_copy(
                held.at[index], out.at[pl.ds(target, block)], sems.at[which, index]
            )
            pl.when(wanted)(copy.start)
            sends.append((wanted, copy))

    norm[...] = jnp.zeros_like(norm)
    for index in range(count):
        row = index // slots
        col = cols_ref[index % slots, row]
        flag = flag_ref[row]

        @pl.when(col >= 0)
        def _():
            values = held[index].astype(jnp.float32)
            weight = (1 - 2 * flag).astype(jnp.float32)
            norm[...] += weight * jnp.sum(values * values, axis=0, keepdims=True)

        @pl.when((col == first_ref[0] + row) & (flag != 0))
        def _():
            values = held[index].astype(jnp.float32)
            eye = lax.broadcasted_iota(jnp.int32, (block, block), 0)
            eye = eye == lax.broadcasted_iota(jnp.int32, (block, block), 1)
            norm[...] += 2.0 * jnp.sum(jnp.where(eye, values, 0.0), axis=0, keepdims=True)

    across = lax.broadcasted_iota(jnp.int32, facts.shape, 1)
    values = jnp.where(across == count, jnp.sum(norm[...]), 0.0)
    for index in range(count):
        value = cols_ref[index % slots, index // slots].astype(jnp.float32)
        values = jnp.where(across == index, value, values)
    facts[...] = values
    for wanted, copy in sends:
        pl.when(wanted)(copy.wait)


def pack(x_blocks, x_cols, branch_flag, first_row):
    rows, slots, block, _ = x_blocks.shape
    count = rows * slots
    smem = pl.BlockSpec(memory_space=pltpu.SMEM)
    hbm = pl.BlockSpec(memory_space=pltpu.HBM)
    packed = [
        jax.ShapeDtypeStruct((size * block, block), x_blocks.dtype)
        for size in (SPLIT, PACKED - SPLIT, PACKED)
    ]
    return pl.pallas_call(
        pack_kernel,
        out_shape=packed + [jax.ShapeDtypeStruct((1, 128), jnp.float32)],
        in_specs=[smem, smem, smem, hbm],
        out_specs=[hbm] * 3 + [pl.BlockSpec(memory_space=pltpu.VMEM)],
        scratch_shapes=[
            pltpu.VMEM((count, block, block), x_blocks.dtype),
            pltpu.VMEM((1, block), jnp.float32),
            pltpu.SemaphoreType.DMA((count,)),
            pltpu.SemaphoreType.DMA((3, count)),
        ],
        compiler_params=pltpu.CompilerParams(vmem_limit_bytes=VMEM_LIMIT),
    )(x_cols.T, branch_flag, first_row.reshape(1), x_blocks.reshape(count, block, block))


BATCH = 4


def multiply_kernel(loads, kept, layout, turned, table, plane, *refs):
    arrays = refs[: 1 + max(load[0] for load in loads)]
    out_ref, pool, ring, more, done, in_sem, turn_sem, ring_sem, out_sem = refs[-9:]
    depth = ring.shape[0] - 1
    block = out_ref.shape[-1]
    n_out = table[0]
    n_terms = table[1]
    zero_entry = pool.shape[0] - 1

    copies = []
    for number, (which, at, entry, first, size, wanted) in enumerate(loads):
        source = arrays[which] if at is None else arrays[which].at[at]
        copy = pltpu.make_async_copy(
            source.at[pl.ds(0, size * block)],
            pool.at[entry, pl.ds(first * block, size * block)],
            in_sem.at[number],
        )
        copies.append(((table[wanted] != 0) & (n_out > 0), copy))
    for here, copy in copies:
        pl.when(here)(copy.start)

    def decode(index):
        entry = lax.shift_right_logical(index, STRIDE.bit_length() - 1)
        return entry, pl.multiple_of(jnp.bitwise_and(index, STRIDE - 1) * block, block)

    def fetch(term):
        entry, first = decode(table[layout["rights"] + term])
        slot = lax.rem(term, depth)
        return pltpu.make_async_copy(
            plane.at[entry, pl.ds(first, block)], ring.at[slot], ring_sem.at[slot]
        )

    def begin(term, carry):
        fetch(term).start()
        return carry

    if turned is not None:
        is_wanted, at, target, n_turn = turned
        rows = pltpu.make_async_copy(
            plane.at[pl.ds(table[at], n_turn)], pool.at[pl.ds(target, n_turn)], turn_sem
        )
        pl.when(table[is_wanted] != 0)(rows.start)
    lax.fori_loop(0, jnp.minimum(depth, n_terms), begin, 0)
    ring[depth] = jnp.zeros((block, block), ring.dtype)
    pool[zero_entry, pl.ds(0, block)] = jnp.zeros((block, block), pool.dtype)

    if turned is not None:
        @pl.when(table[is_wanted] != 0)
        def _():
            down = lax.broadcasted_iota(jnp.int32, (block, block), 0)
            eye = down == lax.broadcasted_iota(jnp.int32, (block, block), 1)
            eye = eye.astype(jnp.float32).astype(pool.dtype)
            rows.wait()

            def turn(place, carry):
                first = pl.multiple_of(place * block, block)
                for entry in range(n_turn):
                    @pl.when(table[layout["turn"] + entry * PACKED + place] != 0)
                    def _():
                        pool[target + entry, pl.ds(first, block)] = lax.dot_general(
                            eye,
                            pool[target + entry, pl.ds(first, block)],
                            (((1,), (1,)), ((), ())),
                            preferred_element_type=jnp.float32,
                        ).astype(pool.dtype)

                return carry

            lax.fori_loop(0, PACKED, turn, 0)

    for here, copy in copies:
        pl.when(here)(copy.wait)

    def product(term, live):
        entry, first = decode(
            jnp.where(live, table[layout["lefts"] + term], zero_entry * STRIDE)
        )
        left = pool[entry, pl.ds(first, block)]
        right = ring[jnp.where(live, lax.rem(term, depth), depth)]
        return jnp.dot(left, right, preferred_element_type=jnp.float32)

    def write(number, slot):
        output = table[layout["outs"] + number]
        return pltpu.make_async_copy(done.at[slot], out_ref.at[output], out_sem.at[slot])

    def one_batch(batch, term):
        begins, counts = [], []
        last = term
        for local in range(BATCH):
            begins.append(last)
            counts.append(table[layout["counts"] + batch * BATCH + local])
            last = last + counts[local]

        def arrived(number, carry):
            fetch(number).wait()
            return carry

        lax.fori_loop(term, last, arrived, 0)
        half = lax.rem(batch, 2) * BATCH
        for local in range(BATCH):
            @pl.when(batch >= 2)
            def _():
                write((batch - 2) * BATCH + local, half + local).wait()

            more[local] = jnp.zeros_like(more[local])

            def two_terms(pair, carry):
                number = begins[local] + 2 + 2 * pair
                second = number + 1 < begins[local] + counts[local]
                more[local] += product(number, True) + product(
                    jnp.where(second, number + 1, 0), second
                )
                return carry

            lax.fori_loop(0, (counts[local] - 1) // 2, two_terms, 0)

        for local in range(BATCH):
            output = table[layout["outs"] + batch * BATCH + local]
            square = more[local]
            for place in range(2):
                live = counts[local] > place
                square = square + product(jnp.where(live, begins[local] + place, 0), live)
            flag = table[layout["flags"] + output // kept].astype(jnp.float32)
            own = table[layout["owns"] + output]
            entry, first = decode(jnp.where(own >= 0, own, zero_entry * STRIDE))
            mine = pool[entry, pl.ds(first, block)].astype(jnp.float32)
            result = (2.0 * flag) * mine + (1.0 - 2.0 * flag) * square
            done[half + local] = result.astype(done.dtype)
        for local in range(BATCH):
            @pl.when(batch * BATCH + local < n_out)
            def _():
                write(batch * BATCH + local, half + local).start()

        def refill(number, carry):
            fetch(number + depth).start()
            return carry

        lax.fori_loop(term, jnp.clip(n_terms - depth, term, last), refill, 0)
        return last

    n_batches = (n_out + BATCH - 1) // BATCH
    lax.fori_loop(0, n_batches, one_batch, jnp.int32(0))
    for back in range(2):
        batch = n_batches - 1 - back
        for local in range(BATCH):
            number = jnp.maximum(batch, 0) * BATCH + local

            @pl.when((batch >= 0) & (number < n_out))
            def _():
                write(number, lax.rem(batch, 2) * BATCH + local).wait()


def multiply(plane, arrays, loads, n_entries, layout, table, shape, turned=None, before=None):
    rows, kept, block, dtype = shape
    outputs = rows * kept
    depth = 48
    smem = pl.BlockSpec(memory_space=pltpu.SMEM)
    hbm = pl.BlockSpec(memory_space=pltpu.HBM)
    operands = [table, plane, *arrays]
    aliases = {}
    if before is not None:
        operands.append(before)
        aliases = {len(operands) - 1: 0}
    return pl.pallas_call(
        functools.partial(multiply_kernel, loads, kept, layout, turned),
        out_shape=jax.ShapeDtypeStruct((outputs, block, block), dtype),
        in_specs=[smem] + [hbm] * (len(operands) - 1),
        out_specs=hbm,
        scratch_shapes=[
            pltpu.VMEM((n_entries + 1, PACKED * block, block), dtype),
            pltpu.VMEM((depth + 1, block, block), dtype),
            pltpu.VMEM((BATCH, block, block), jnp.float32),
            pltpu.VMEM((2 * BATCH, block, block), dtype),
            pltpu.SemaphoreType.DMA((len(loads),)),
            pltpu.SemaphoreType.DMA,
            pltpu.SemaphoreType.DMA((depth,)),
            pltpu.SemaphoreType.DMA((2 * BATCH,)),
        ],
        input_output_aliases=aliases,
        compiler_params=pltpu.CompilerParams(vmem_limit_bytes=VMEM_LIMIT),
    )(*operands)


def shift(array, pairs):
    return lax.ppermute(array, "col", pairs)


def start_line(parts, facts):
    first = [shift(part, [(0, 1), (1, 0), (2, 3), (3, 2)]) for part in parts]
    middle = [shift(part, [(1, 2), (2, 1)]) for part in parts]
    facts = gather_facts(facts, ("row",))
    middle[0], facts = lax.optimization_barrier((middle[0], facts))
    return first, middle, facts


def relay_line(first, middle):
    end_two = [shift(part, [(1, 0), (2, 3)]) for part in middle]
    middle_two = [shift(part, [(1, 2), (2, 1)]) for part in first]
    pairs = []
    for row in range(lax.axis_size("row")):
        pairs += [(4 * row + 1, 4 * row)] * (row // 2 != 0)
        pairs += [(4 * row + 2, 4 * row + 3)] * (row // 2 != 3)
    small = lax.optimization_barrier((middle_two[1], end_two[1]))[0]
    small = lax.ppermute(small, ("row", "col"), pairs)
    large = lax.optimization_barrier((middle_two[0], small, end_two[0]))[0]
    return {
        "first": first,
        "middle": middle,
        "end_two": end_two,
        "middle_two": middle_two,
        "end_three": (lax.ppermute(large, ("row", "col"), pairs), small),
    }


def running_count(fill):
    count = fill.shape[-1]
    before = jnp.arange(count)[:, None] < jnp.arange(count)[None, :]
    return jnp.sum(jnp.where(before, fill[..., :, None], 0), axis=-2)


def places(cols):
    flat = (cols >= 0).astype(jnp.int32).reshape(cols.shape[:-2] + (-1,))
    return running_count(flat).reshape(cols.shape)


def make_table(left_of, right_of, owns, flags, chosen, width, wanted, turn=None):
    kept = right_of.shape[0] // left_of.shape[0]
    outputs = right_of.shape[0]
    left_of = jnp.repeat(left_of, kept, axis=0)
    live = (left_of > 0) & (right_of > 0) & chosen[:, None]
    counts = jnp.sum(live.astype(jnp.int32), axis=1)
    term = jnp.where(live, running_count(live.astype(jnp.int32)), -1)
    across = jnp.arange(width, dtype=jnp.int32)
    pick = term[:, None, :] == across[:, None]
    lefts = jnp.sum(jnp.where(pick, left_of[:, None, :] - 1, 0), axis=2)
    rights = jnp.sum(jnp.where(pick, right_of[:, None, :] - 1, 0), axis=2)
    flat = jnp.where(across < counts[:, None], running_count(counts)[:, None] + across, -1)
    pick = flat[None] == jnp.arange(PACKED * width, dtype=jnp.int32)[:, None, None]
    lefts = jnp.sum(jnp.where(pick, lefts, 0), axis=(1, 2))
    rights = jnp.sum(jnp.where(pick, rights, 0), axis=(1, 2))
    every = jnp.arange(outputs, dtype=jnp.int32)
    number = jnp.where(chosen, running_count(chosen.astype(jnp.int32)), -1)
    pick = number[None, :] == every[:, None]
    outs = jnp.sum(jnp.where(pick, every, 0), axis=1)
    ordered = jnp.sum(jnp.where(pick, counts, 0), axis=1)
    sizes = jnp.stack([jnp.sum(chosen.astype(jnp.int32)), jnp.sum(counts)])
    spare = jnp.zeros((BATCH,), jnp.int32)
    lists = {
        "sizes": sizes,
        "wanted": wanted,
        "outs": jnp.concatenate([outs, spare]),
        "counts": jnp.concatenate([ordered, spare]),
        "lefts": lefts,
        "rights": rights,
        "owns": owns,
        "flags": flags,
    }
    if turn is not None:
        lists["turn"] = turn
    layout = {}
    first = 0
    for name, values in lists.items():
        layout[name] = first
        first += values.shape[0]
    return jnp.concatenate(list(lists.values())), layout


def gather_facts(facts, axes):
    places = jnp.zeros((1,), jnp.int32)
    own = jnp.int32(0)
    known = 1
    for axis in axes:
        size = lax.axis_size(axis)
        own = own * size + lax.axis_index(axis)
        known *= size
    stride = known
    for axis in axes:
        size = lax.axis_size(axis)
        stride //= size
        mask = 1
        while mask < size:
            other = lax.ppermute(facts, axis, [(i, i ^ mask) for i in range(size)])
            facts = jnp.concatenate([facts, other])
            places = jnp.concatenate([places, places + mask * stride])
            mask *= 2
    hit = jnp.bitwise_xor(own, places)[None, :] == jnp.arange(known, dtype=jnp.int32)[:, None]
    return jnp.sum(jnp.where(hit[..., None], facts, 0.0), axis=1)


def per_device(x_blocks, x_cols, out_cols, branch_flag):
    rows, slots = x_cols.shape
    kept = out_cols.shape[1]
    block = x_blocks.shape[-1]
    dtype = x_blocks.dtype
    n_row = lax.axis_size("row")
    n_col = lax.axis_size("col")
    row = lax.axis_index("row")
    col = lax.axis_index("col")
    n_blocks = n_row * rows
    width = n_col * slots
    shape = (rows, kept, block, dtype)

    count = rows * slots
    tuned = n_col == 4 and n_row == 8
    if tuned:
        part_a, part_b, full, facts = pack(x_blocks, x_cols, branch_flag, row * rows)
        plane = lax.all_gather(full, "row", axis=0)
        near, far_one, far_two = [
            shift(facts, [(i, i ^ step) for i in range(n_col)]) for step in range(1, n_col)
        ]
        line_cols = jnp.concatenate([facts, near, far_one, far_two])
        total = (facts + near) + (far_one + far_two)
        facts = jnp.where(jnp.arange(128) < count, facts, total)
        first, middle, facts = start_line((part_a, part_b), facts)
        trace = jnp.sum(facts[:, count]).reshape(1)
    else:
        part_a, part_b, full, facts = pack(x_blocks, x_cols, branch_flag, row * rows)
        plane = lax.all_gather(full, "row", axis=0)
        line = lax.all_gather(full, "col", axis=0)
        every_fact = gather_facts(facts, ("row", "col")).reshape(n_row, n_col, 128)
        trace = jnp.sum(every_fact[:, :, count]).reshape(1)
        facts = lax.dynamic_index_in_dim(every_fact, col, 1, keepdims=False)
        line_cols = lax.dynamic_index_in_dim(every_fact, row, 0, keepdims=False)

    def slots_of(facts):
        cols = facts[:, :count].astype(jnp.int32).reshape(facts.shape[0], rows, slots)
        return cols, places(cols)

    plane_cols, plane_places = slots_of(facts)
    targets = out_cols.reshape(rows * kept)
    right_at = plane_places + STRIDE * jnp.arange(n_row, dtype=jnp.int32)[:, None, None]
    hit = plane_cols.reshape(n_blocks, slots)[None] == targets[:, None, None]
    right_of = jnp.sum(jnp.where(hit, right_at.reshape(n_blocks, slots) + 1, 0), axis=2)
    hit = x_cols[:, None, :] == out_cols[:, :, None]
    owns = jnp.sum(jnp.where(hit, places(x_cols)[:, None, :] + 1, 0), axis=2) - 1
    owns = owns.reshape(rows * kept)

    every = jnp.arange(n_blocks, dtype=jnp.int32)
    line_cols, line_places = slots_of(line_cols)

    def straight(entries, wanted):
        at = line_places + STRIDE * entries[:, None, None]
        hit = (line_cols[..., None] == every) & wanted[:, None, None, None]
        return jnp.sum(jnp.where(hit, at[..., None] + 1, 0), axis=(0, 2))

    def turned(entry, device, size, wanted):
        cols = lax.dynamic_slice_in_dim(plane_cols, device, size, 0)
        place = lax.dynamic_slice_in_dim(plane_places, device, size, 0)
        at = place + STRIDE * (entry + jnp.arange(size, dtype=jnp.int32)[:, None, None])
        own = row * rows + jnp.arange(rows, dtype=jnp.int32)
        hit = (cols[..., None] == own) & wanted
        found = jnp.sum(jnp.where(hit, at[..., None] + 1, 0), axis=2)
        names = device * rows + jnp.arange(size * rows, dtype=jnp.int32).reshape(size, rows)
        found = jnp.where(names[:, :, None, None] == every, found[..., None], 0)
        marks = jnp.any(hit, axis=3)[..., None] & (
            place[..., None] == jnp.arange(PACKED, dtype=jnp.int32)
        )
        marks = jnp.any(marks, axis=(1, 2)).astype(jnp.int32)
        return jnp.sum(found, axis=(0, 1)), marks.reshape(size * PACKED)

    heights = jnp.arange(n_col, dtype=jnp.int32)
    if not tuned:
        left_of = straight(1 + heights, heights >= 0)
        everything = jnp.ones((rows * kept,), bool)
        one = jnp.ones((1,), jnp.int32)
        table, layout = make_table(left_of, right_of, owns, branch_flag, everything, width, one)
        loads = [(0, None, 0, 0, PACKED, 2)]
        loads += [(1, c, 1 + c, 0, PACKED, 2) for c in range(n_col)]
        purified = multiply(plane, [full, line], tuple(loads), 1 + n_col, layout, table, shape)
        return purified.reshape(rows, kept, block, block), trace

    at_end = (col == 0) | (col == n_col - 1)
    corner = at_end & (row // 2 == col)
    far = at_end & ~corner
    turn_row = 2 * (n_col - 1 - col)
    wanted = [at_end | True, at_end, ~at_end, far, corner, turn_row]
    wanted = jnp.stack([value.astype(jnp.int32) for value in wanted])
    always, at_ends, inside, at_far, at_corner, turn_at = range(2, 8)

    entries = jnp.where(at_end, jnp.array([0, 1, 2, 3]), jnp.array([0, 1, 3, 2]))
    entries = entries.astype(jnp.int32)
    from_plane, marks = turned(4, turn_row, 2, corner)
    early = straight(entries, (entries < 3) | ~at_end) + from_plane
    late = straight(entries, (entries == 3) & far)
    meets = (jnp.repeat(late, kept, axis=0) > 0) & (right_of > 0)
    is_late = jnp.any(meets, axis=1)

    def table_of(left_of, chosen, turn=None):
        return make_table(left_of, right_of, owns, branch_flag, chosen, width, wanted, turn)

    early_table, early_layout = table_of(early, ~is_late, marks)
    late_table, late_layout = table_of(early + late, is_late)
    first[0], early_table, late_table = lax.optimization_barrier(
        (first[0], early_table, late_table)
    )
    line = relay_line(first, middle)

    arrays = [full]
    loads = [(0, None, 0, 0, PACKED, always)]
    spans = ((0, SPLIT), (SPLIT, PACKED - SPLIT))

    def add(array, entry, which, wanted):
        loads.append((len(arrays), None, entry) + spans[which] + (wanted,))
        arrays.append(array)

    stages = (
        ("first", 1, always),
        ("middle", 2, inside),
        ("end_two", 2, at_ends),
        ("middle_two", 3, inside),
    )
    for name, entry, flag in stages:
        for which in range(2):
            add(line[name][which], entry, which, flag)
    purified = multiply(
        plane, list(arrays), tuple(loads), 6, early_layout, early_table, shape,
        (at_corner, turn_at, 4, 2),
    )
    for which in range(2):
        add(line["end_three"][which], 3, which, at_far)
    purified, trace = lax.optimization_barrier((purified, trace))
    purified = multiply(
        plane, list(arrays), tuple(loads), 4, late_layout, late_table, shape, None, purified
    )
    return purified.reshape(rows, kept, block, block), trace


def solution(mesh):
    in_specs = (P("row", "col", None, None), P("row", "col"), P("row", "col"), P("row"))
    out_specs = (P("row", "col", None, None), P())
    return jax.shard_map(
        per_device, mesh=mesh, in_specs=in_specs, out_specs=out_specs, check_vma=False
    )
```
